32 devices in a mesh: pole: 4 (over y, x), row: 4 (over z), col: 2 (over core).
Axes of the slice: x: 2, y: 2, z: 4, core: 2. Of those that a mesh axis runs over, the one named last changes fastest.
Arguments:
- found_inverse: bfloat16 [4, 2, 1024, 4, 2, 128], P('pole', None, 'row', None, 'col'), may hold values from -0.375 to 0.375
- l_panel: bfloat16 [4, 2, 1024, 512], P('pole', None, ('row', 'col')), may hold values from -1.5 to 1.5
- block_pattern: int32 [8, 4], P(('row', 'col')), may hold values 0 or 1
- sup_widths: int32 [4], replicated, may hold values from 1 to 128, 320 in all
- diag_inverse: bfloat16 [4, 2, 512, 128], P('pole'), may hold values from -6 to 6
- pole_weights: float32 [4, 2], P('pole'), may hold values from -4 to 4
Outputs:
- density: float32 [512, 1024], P('col', 'row')
- diagonal: float32 [512, 128], replicated
The draws below stay inside these ranges and needn't reach their ends.
Inputs may be any that keep to these rules, and one draw needn't show every extreme that they name: `sup_widths`: one supernode has exactly 128 columns.
All inputs are finite; a program needn't handle non-finite values. No bound on the sum of `block_pattern` on one device may be relied on, other than what follows from the above.
Results may differ from the reference program's by a relative error of at most 0.0003.
Values may be sent and summed in bfloat16 or wider, within the bound.
No kernel may reach another device: no remote copies, remote signals or barrier semaphores. Data moves between devices by JAX's collectives and lax.ppermute only.
A program may use at most 128 MiB of HBM per device.

```python
import math
import jax
import jax.numpy as jnp
import numpy as np
from jax import lax

S = 128
NSUP = 4
POLES = 4
NB = 8
N = 1024
W = 512
N_ROW = 4
N_COL = 2


def with_ends(drawn, own_key, least, high):
    shape = drawn.shape
    index_at = [jax.random.randint(jax.random.fold_in(own_key, axis), (), 0, shape[axis]) for axis in range(len(shape))]
    drawn = drawn.at[tuple(index_at)].set(least)
    longest = shape.index(max(shape))
    index_at[longest] = (index_at[longest] + 1) % shape[longest]
    return drawn.at[tuple(index_at)].set(high)


def block_scale(stream_key, shape, shards, smallest, largest):
    gain = 1.0
    for position, parts in shards:
        steps = jax.random.uniform(jax.random.fold_in(jax.random.fold_in(stream_key, 6), position), (parts,), jnp.float32, smallest / len(shards), largest / len(shards))
        gain = gain * jnp.repeat(jnp.exp(steps), shape[position] // parts).reshape((-1,) + (1,) * (len(shape) - 1 - position))
    return gain


def profile(count, total, most, skew):
    portions = [(1 << 20) // math.isqrt(standing ** skew) + 1 for standing in range(2, count + 1)]
    surplus, given = total - most - (count - 1), [1] * (count - 1)
    while surplus > 0:
        movable = [i for i in range(count - 1) if given[i] < most]
        mass, budget = sum([portions[i] for i in movable]), surplus
        for i in movable:
            extra = min(most - given[i], max(1, budget * portions[i] // mass), surplus)
            given[i] = given[i] + extra
            surplus = surplus - extra
    return np.array([most] + given)


def uneven_parts(key, count, total, most, skew):
    if count == 2:
        one = jax.random.randint(key, (), max(1, total - most), min(most, total - 1) + 1)
        return jnp.stack([one, total - one])
    sizes = jnp.asarray(profile(count, total, most, skew), jnp.int32)
    couples = (count - 1) // 2
    donor, sink = sizes[1:1 + 2 * couples:2], sizes[2:2 + 2 * couples:2]
    room = jnp.minimum(donor - 1, most - sink)
    passed = jax.random.randint(jax.random.fold_in(key, 1), (couples,), 0, 1 << 20) % (room + 1)
    sizes = sizes.at[1:1 + 2 * couples:2].set(donor - passed).at[2:2 + 2 * couples:2].set(sink + passed)
    return sizes[jax.random.permutation(jax.random.fold_in(key, 2), count)]


def normal_values(rng, dims, scale, reach, cuts=(), held_as=jnp.bfloat16):
    gain = block_scale(rng, dims, cuts, -0.22, 0.18) if cuts else 1.0
    entries = jax.random.normal(rng, dims, jnp.float32) * scale * gain
    return jnp.minimum(jnp.maximum(entries, -reach), reach).astype(held_as)


def setup_inputs(seed: int = 0) -> dict:
    seeds = jax.random.split(jax.random.key(seed), 7)
    return {
        "found_inverse": normal_values(seeds[0], (POLES, 2, N, N_ROW, N_COL, S), (N // 4) ** -0.5, 0.375, ((0, 4), (2, 4), (4, 2))),
        "l_panel": normal_values(seeds[1], (POLES, 2, N, W), 0.25, 1.5, ((0, 4), (2, 8))),
        "block_pattern": with_ends((jax.random.randint(seeds[2], (NB, NSUP), 0, 2) < 1).astype(jnp.int32), jax.random.fold_in(seeds[2], 1), 0, 1),
        "sup_widths": uneven_parts(seeds[3], NSUP, S + (NSUP - 1) * (S // 2), S, 0).astype(jnp.int32),
        "diag_inverse": normal_values(seeds[4], (POLES, 2, W, S), 1.0, 6.0, ((0, 4),)),
        "pole_weights": normal_values(seeds[5], (POLES, 2), 1.0, 4.0, ((0, 4),), jnp.float32),
    }


def product(left, right):
    return jnp.dot(left, right, preferred_element_type=jnp.float32)


def pair_product(left, right):
    return jnp.einsum('ika,ikb->kab', left, right, precision=lax.Precision.HIGHEST)


def reference(found_inverse, l_panel, block_pattern, sup_widths, diag_inverse, pole_weights):
    slot_width = diag_inverse.shape[-1]
    supernodes = sup_widths.shape[0]
    total_cols = supernodes * slot_width
    order = l_panel.shape[2]
    columns = jnp.arange(total_cols, dtype=jnp.int32)
    column_ok = (columns % slot_width) < jnp.repeat(sup_widths, slot_width)
    row_valid = jnp.repeat(jnp.repeat(block_pattern, slot_width, axis=0), slot_width, axis=1) == 1
    keep_mask = row_valid & column_ok[None, :]
    density = jnp.zeros((order, total_cols), jnp.float32)
    diagonal = jnp.zeros((total_cols, slot_width), jnp.float32)
    for pole in range(POLES):
        masked = jnp.where(keep_mask[None], l_panel[pole], jnp.zeros((), jnp.bfloat16))
        inverse = found_inverse[pole].reshape(2, order, order)
        block_real = -(product(inverse[0], masked[0]) - product(inverse[1], masked[1]))
        block_imag = -(product(inverse[0], masked[1]) + product(inverse[1], masked[0]))
        w_real = pole_weights[pole, 0]
        w_imag = pole_weights[pole, 1]
        density = density + (w_real * block_real - w_imag * block_imag)
        lifted = masked.astype(jnp.float32).reshape(2, order, supernodes, slot_width)
        upper_real = block_real.reshape(order, supernodes, slot_width)
        upper_imag = block_imag.reshape(order, supernodes, slot_width)
        t_real = pair_product(lifted[0], upper_real) - pair_product(lifted[1], upper_imag)
        t_imag = pair_product(lifted[0], upper_imag) + pair_product(lifted[1], upper_real)
        d_real = diag_inverse[pole, 0].astype(jnp.float32).reshape(supernodes, slot_width, slot_width)
        d_imag = diag_inverse[pole, 1].astype(jnp.float32).reshape(supernodes, slot_width, slot_width)
        update = w_real * (d_real - t_real) - w_imag * (d_imag - t_imag)
        diagonal = diagonal + update.reshape(total_cols, slot_width)
    return density.T, diagonal
```

```python
import jax
import jax.numpy as jnp
from jax import lax
from jax.sharding import PartitionSpec as P


def is_power_of_two(count):
    return count & (count - 1) == 0


def swap_sum(value, axis, bits):
    count = lax.axis_size(axis)
    for bit in bits:
        value = value + lax.ppermute(value, axis, [(i, i ^ bit) for i in range(count)])
    return value


def bits_of(count):
    return [1 << k for k in range(count.bit_length() - 1)]


def sum_over(value, axis):
    count = lax.axis_size(axis)
    if not is_power_of_two(count):
        return lax.psum(value, axis)
    bits = bits_of(count)
    half = value.shape[0] // 2
    first = swap_sum(value[:half], axis, bits)
    second = swap_sum(value[half:], axis, bits[::-1])
    return jnp.concatenate([first, second], axis=0)


def scatter_sum(value, axis):
    count = lax.axis_size(axis)
    if not is_power_of_two(count):
        return lax.psum_scatter(value, axis, scatter_dimension=0, tiled=True)
    index = lax.axis_index(axis)
    for bit in bits_of(count)[::-1]:
        half = value.shape[0] // 2
        upper = (index & bit) != 0
        keep = jnp.where(upper, value[half:], value[:half])
        send = jnp.where(upper, value[:half], value[half:])
        value = keep + lax.ppermute(send, axis, [(i, i ^ bit) for i in range(count)])
    return value


def gather_pieces(value, axis):
    count = lax.axis_size(axis)
    if not is_power_of_two(count):
        return lax.all_gather(value, axis, axis=0, tiled=True)
    index = lax.axis_index(axis)
    for bit in bits_of(count):
        other = lax.ppermute(value, axis, [(i, i ^ bit) for i in range(count)])
        upper = (index & bit) != 0
        value = jnp.concatenate(
            [jnp.where(upper, other, value), jnp.where(upper, value, other)], axis=0
        )
    return value


def gather_blocks(value, axis):
    count = lax.axis_size(axis)
    index = lax.axis_index(axis)
    pieces = [(index, value)]
    near = max(1, count // 2)
    up, down = {}, {}
    for distance in range(1, count):
        ahead = [(i, i + distance) for i in range(count - distance)]
        back = [(i + distance, i) for i in range(count - distance)]
        if distance <= near:
            up[distance] = lax.ppermute(value, axis, ahead)
            down[distance] = lax.ppermute(value, axis, back)
        else:
            hop = distance - near
            ahead = [(i + near, i + distance) for i in range(count - distance)]
            back = [(i + hop, i) for i in range(count - distance)]
            up[distance] = lax.ppermute(up[near], axis, ahead)
            down[distance] = lax.ppermute(down[near], axis, back)
        pieces.append((index - distance, up[distance]))
        pieces.append((index + distance, down[distance]))
    return pieces


def contract(left, right):
    return jnp.einsum("jk,ij->ki", left, right, preferred_element_type=jnp.float32)


def pair_product(left, right):
    return jnp.einsum("ika,kbi->kab", left, right, preferred_element_type=jnp.float32)


def per_device(found_inverse, l_panel, block_pattern, sup_widths, diag_inverse, pole_weights):
    slot_width = diag_inverse.shape[-1]
    total_cols = l_panel.shape[-1]
    supernodes = total_cols // slot_width
    row_count = lax.axis_size("row")
    lead_flag = ((lax.axis_index("row") == 0) & (lax.axis_index("col") == 0)).astype(jnp.float32)
    columns = jnp.arange(total_cols, dtype=jnp.int32)
    column_ok = columns % slot_width < jnp.repeat(sup_widths, slot_width)
    block_ok = jnp.repeat(block_pattern[0], slot_width) == 1
    masked = jnp.where(
        (column_ok & block_ok)[None, None, :], l_panel[0], jnp.zeros((), jnp.bfloat16)
    )
    own_rows = lax.all_gather(masked, "col", axis=1, tiled=True)
    local_rows = found_inverse.shape[2]
    inverse = found_inverse[0].reshape(2, local_rows, row_count, slot_width)
    part_real = jnp.zeros((total_cols, local_rows), jnp.float32)
    part_imag = jnp.zeros((total_cols, local_rows), jnp.float32)
    for owner, block in gather_blocks(masked, "row"):
        facing = lax.dynamic_index_in_dim(
            inverse, jnp.clip(owner, 0, row_count - 1), axis=2, keepdims=False
        )
        part_real += contract(block[1], facing[1]) - contract(block[0], facing[0])
        part_imag -= contract(block[1], facing[0]) + contract(block[0], facing[1])
    w_real = pole_weights[0, 0]
    w_imag = pole_weights[0, 1]
    weighted = w_real * part_real - w_imag * part_imag
    turned = w_real * part_imag + w_imag * part_real
    density = sum_over(scatter_sum(weighted, "col"), "pole")

    lifted = own_rows.reshape(2, local_rows, supernodes, slot_width)

    def fine_product(left, right):
        right = right.reshape(supernodes, slot_width, local_rows)
        high = lax.reduce_precision(right, 8, 7)
        low = (right - high).astype(jnp.bfloat16)
        return pair_product(left, high.astype(jnp.bfloat16)) + pair_product(left, low)

    update = fine_product(lifted[0], weighted) - fine_product(lifted[1], turned)
    d_real = diag_inverse[0, 0].astype(jnp.float32)
    d_imag = diag_inverse[0, 1].astype(jnp.float32)
    local_term = lead_flag * (w_real * d_real - w_imag * d_imag) - update.reshape(
        total_cols, slot_width
    )
    diagonal = scatter_sum(local_term, "col")
    diagonal = sum_over(diagonal, "pole")
    diagonal = sum_over(diagonal, "row")
    diagonal = gather_pieces(diagonal, "col")
    return (density, diagonal)


def solution(mesh):
    in_specs = (
        P("pole", None, "row", None, "col", None),
        P("pole", None, ("row", "col"), None),
        P(("row", "col"), None),
        P(),
        P("pole", None, None, None),
        P("pole", None),
    )
    out_specs = (P("col", "row"), P())
    return jax.shard_map(
        per_device, mesh=mesh, in_specs=in_specs, out_specs=out_specs, check_vma=False
    )
```

```python
import functools

import jax
import jax.numpy as jnp
from jax import lax
from jax.experimental import pallas as pl
from jax.experimental.pallas import tpu as pltpu
from jax.sharding import PartitionSpec as P

F32 = jnp.float32
BF16 = jnp.bfloat16
VMEM_SPEC = pl.BlockSpec(memory_space=pltpu.VMEM)
SMEM_SPEC = pl.BlockSpec(memory_space=pltpu.SMEM)


def rows_by_rows(left, right):
    return lax.dot_general(left, right, (((1,), (1,)), ((), ())), preferred_element_type=F32)


def offsets_of(widths_ref, supernodes):
    offsets = [0]
    for k in range(supernodes):
        offsets.append(offsets[-1] + widths_ref[k])
    return offsets


def pack_kernel(supernodes, slot, pattern_ref, widths_ref, panel_ref, packed_ref, wide_ref):
    copies, double_width, _ = packed_ref.shape
    packed_width = double_width // 2
    offsets = offsets_of(widths_ref, supernodes)
    place, keep = [], []
    lane = lax.broadcasted_iota(jnp.int32, (1, slot), 1)
    for k in range(supernodes):
        valid = (lane < widths_ref[k]) & (pattern_ref[0, k] == 1)
        place.append(jnp.where(valid, offsets[k] + lane, -1))
    place = jnp.concatenate(place, axis=1)
    target = lax.broadcasted_iota(jnp.int32, (packed_width, supernodes * slot), 0)
    select = jnp.where(target == place, 1.0, 0.0).astype(BF16)
    for part in range(2):
        packed = rows_by_rows(select, panel_ref[part]).astype(BF16)
        for copy in range(copies):
            packed_ref[copy, part * packed_width:(part + 1) * packed_width, :] = packed
        for k in range(supernodes):
            valid = (lane < widths_ref[k]) & (pattern_ref[0, k] == 1)
            row_id = lax.broadcasted_iota(jnp.int32, (slot, slot), 0)
            col_id = lax.broadcasted_iota(jnp.int32, (slot, slot), 1)
            chosen = jnp.where((row_id == col_id) & valid, 1.0, 0.0).astype(BF16)
            piece = panel_ref[part, :, k * slot:(k + 1) * slot]
            wide_ref[part, k * slot:(k + 1) * slot, :] = rows_by_rows(chosen, piece).astype(BF16)


def compute_kernel(
    pieces, widths_ref, weights_ref, lead_ref, inverse_ref, packed_ref, own_ref, diag_ref,
    payload_ref, straight_ref, x_ref, y_ref, diagonal_ref,
):
    pole_count, col_count = pieces
    row_count, double_width, block = packed_ref.shape
    packed_width = double_width // 2
    local_rows = inverse_ref.shape[0] // (2 * row_count)
    slot = diag_ref.shape[2]
    total_cols = diag_ref.shape[1]
    supernodes = total_cols // slot
    w_real = weights_ref[0, 0]
    w_imag = weights_ref[0, 1]
    lead = lead_ref[0].astype(F32)

    group = 256 // row_count
    span = group * row_count
    row_id = lax.broadcasted_iota(jnp.int32, (span, span), 0)
    col_id = lax.broadcasted_iota(jnp.int32, (span, span), 1)
    source = (row_id % group) * row_count + row_id // group
    order = jnp.where(col_id == source, 1.0, 0.0).astype(BF16)
    for part in range(2):
        for chunk in range(local_rows // group):
            base = (part * local_rows + chunk * group) * row_count
            mixed = inverse_ref[base:base + span, :]
            sorted_rows = jnp.dot(order, mixed, preferred_element_type=F32).astype(BF16)
            for owner in range(row_count):
                straight_ref[
                    part, chunk * group:(chunk + 1) * group, owner * block:(owner + 1) * block
                ] = sorted_rows[owner * group:(owner + 1) * group]

    panel = jnp.concatenate([packed_ref[owner] for owner in range(row_count)], axis=1)
    with_real = rows_by_rows(panel, straight_ref[0])
    with_imag = rows_by_rows(panel, straight_ref[1])
    u_real = with_imag[packed_width:] - with_real[:packed_width]
    u_imag = -(with_real[packed_width:] + with_imag[:packed_width])
    weighted = w_real * u_real - w_imag * u_imag
    turned = w_real * u_imag + w_imag * u_real
    strips = local_rows // slot
    for ref, value in ((x_ref, weighted), (y_ref, turned)):
        for s in range(strips):
            ref[s, :packed_width] = value[:, s * slot:(s + 1) * slot]
            ref[s, packed_width:] = jnp.zeros((slot, slot), F32)

    per_col = total_cols // col_count
    per_piece = per_col // pole_count
    offsets = offsets_of(widths_ref, supernodes)
    row_in_slot = lax.broadcasted_iota(jnp.int32, (slot, 1), 0)
    own = [
        jnp.concatenate([own_ref[c, part] for c in range(col_count)], axis=1) for part in range(2)
    ]
    for k in range(supernodes):
        valid = row_in_slot < widths_ref[k]
        x, y = (
            jnp.concatenate(
                [jnp.where(valid, ref[s, pl.ds(offsets[k], slot), :], 0.0) for s in range(strips)],
                axis=1,
            )
            for ref in (x_ref, y_ref)
        )
        x_high, y_high = x.astype(BF16), y.astype(BF16)
        x_low = (x - x_high.astype(F32)).astype(BF16)
        y_low = (y - y_high.astype(F32)).astype(BF16)
        l_real = own[0][k * slot:(k + 1) * slot]
        l_imag = own[1][k * slot:(k + 1) * slot]
        product = (rows_by_rows(l_real, x_high) - rows_by_rows(l_imag, y_high)) + (
            rows_by_rows(l_real, x_low) - rows_by_rows(l_imag, y_low)
        )
        d_real = diag_ref[0, k * slot:(k + 1) * slot].astype(F32)
        d_imag = diag_ref[1, k * slot:(k + 1) * slot].astype(F32)
        diagonal_ref[k * slot:(k + 1) * slot] = lead * (w_real * d_real - w_imag * d_imag) - product
        size = min(per_piece, slot)
        for begin in range(k * slot, (k + 1) * slot, size):
            c, within = divmod(begin, per_col)
            p, inside = divmod(within, per_piece)
            piece = p * col_count + c
            payload_ref[piece, inside:inside + size, :local_rows] = x[begin - k * slot:begin - k * slot + size]
    for piece in range(pole_count * col_count):
        p, c = divmod(piece, col_count)
        begin = c * per_col + p * per_piece
        payload_ref[piece, :, local_rows:] = diagonal_ref[begin:begin + per_piece]


def exchange(value, axis):
    return lax.all_to_all(value, axis, 0, 0, tiled=True)


def spread(value, axis, count):
    return exchange(jnp.broadcast_to(value[None], (count,) + value.shape), axis)


def per_device(found_inverse, l_panel, block_pattern, sup_widths, diag_inverse, pole_weights):
    slot = diag_inverse.shape[-1]
    total_cols = l_panel.shape[-1]
    supernodes = total_cols // slot
    packed_width = slot + (supernodes - 1) * (slot // 2)
    local_rows = found_inverse.shape[2]
    block = l_panel.shape[2]
    pole_count = lax.axis_size("pole")
    row_count = lax.axis_size("row")
    col_count = lax.axis_size("col")
    pieces = pole_count * col_count
    per_piece = total_cols // pieces

    packed, wide = pl.pallas_call(
        functools.partial(pack_kernel, supernodes, slot),
        in_specs=[SMEM_SPEC, SMEM_SPEC, VMEM_SPEC],
        out_specs=[VMEM_SPEC, VMEM_SPEC],
        out_shape=[
            jax.ShapeDtypeStruct((row_count, 2 * packed_width, block), BF16),
            jax.ShapeDtypeStruct((2, total_cols, block), BF16),
        ],
        name="pack",
    )(block_pattern, sup_widths, l_panel[0])

    own = lax.all_gather(wide, "col", axis=0)
    gathered = exchange(packed, "row")

    lead = ((lax.axis_index("row") == 0) & (lax.axis_index("col") == 0)).astype(jnp.int32)
    payload = pl.pallas_call(
        functools.partial(compute_kernel, (pole_count, col_count)),
        in_specs=[SMEM_SPEC] * 3 + [VMEM_SPEC] * 4,
        out_specs=VMEM_SPEC,
        out_shape=jax.ShapeDtypeStruct((pieces, per_piece, local_rows + slot), F32),
        scratch_shapes=[
            pltpu.VMEM((2, local_rows, row_count * block), BF16),
            pltpu.VMEM((local_rows // slot, packed_width + slot, slot), F32),
            pltpu.VMEM((local_rows // slot, packed_width + slot, slot), F32),
            pltpu.VMEM((total_cols, slot), F32),
        ],
        compiler_params=pltpu.CompilerParams(vmem_limit_bytes=48 * 1024 * 1024),
        name="compute",
    )(
        sup_widths, pole_weights, lead.reshape(1),
        found_inverse.reshape(2 * local_rows * row_count, block), gathered, own, diag_inverse[0],
    )

    summed = jnp.sum(exchange(payload, ("pole", "col")), axis=0)
    density = spread(summed[:, :local_rows], "pole", pole_count)
    density = density.reshape(pole_count * per_piece, local_rows)
    diagonal = jnp.sum(spread(summed[:, local_rows:], "row", row_count), axis=0)
    diagonal = spread(diagonal, ("pole", "col"), pieces)
    diagonal = diagonal.reshape(pole_count, col_count, per_piece, slot).transpose(1, 0, 2, 3)
    return (density, diagonal.reshape(total_cols, slot))


def solution(mesh):
    in_specs = (
        P("pole", None, "row", None, "col", None),
        P("pole", None, ("row", "col"), None),
        P(("row", "col"), None),
        P(),
        P("pole", None, None, None),
        P("pole", None),
    )
    out_specs = (P("col", "row"), P())
    return jax.shard_map(
        per_device, mesh=mesh, in_specs=in_specs, out_specs=out_specs, check_vma=False
    )
```

```python
import functools

import jax
import jax.numpy as jnp
from jax import lax
from jax.experimental import pallas as pl
from jax.experimental.pallas import tpu as pltpu
from jax.sharding import PartitionSpec as P

F32 = jnp.float32
BF16 = jnp.bfloat16
VMEM_SPEC = pl.BlockSpec(memory_space=pltpu.VMEM)
SMEM_SPEC = pl.BlockSpec(memory_space=pltpu.SMEM)
PARAMS = pltpu.CompilerParams(vmem_limit_bytes=48 * 1024 * 1024)


def rows_by_rows(left, right):
    return lax.dot_general(left, right, (((1,), (1,)), ((), ())), preferred_element_type=F32)


def offsets_of(widths_ref, supernodes):
    offsets = [0]
    for k in range(supernodes):
        offsets.append(offsets[-1] + widths_ref[k])
    return offsets


def pack_kernel(supernodes, slot, pattern_ref, widths_ref, panel_ref, packed_ref):
    packed_width = packed_ref.shape[0] // 2
    offsets = offsets_of(widths_ref, supernodes)
    lane = lax.broadcasted_iota(jnp.int32, (1, slot), 1)
    place = []
    for k in range(supernodes):
        valid = (lane < widths_ref[k]) & (pattern_ref[0, k] == 1)
        place.append(jnp.where(valid, offsets[k] + lane, -1))
    place = jnp.concatenate(place, axis=1)
    target = lax.broadcasted_iota(jnp.int32, (packed_width, supernodes * slot), 0)
    select = jnp.where(target == place, 1.0, 0.0).astype(BF16)
    for part in range(2):
        packed_ref[part * packed_width:(part + 1) * packed_width, :] = rows_by_rows(
            select, panel_ref[part]
        ).astype(BF16)


def prepare_kernel(row_count, place_ref, inverse_ref, straight_ref):
    block = inverse_ref.shape[1]
    local_rows = straight_ref.shape[1]
    row_index = place_ref[0]
    group = max(8, 256 // row_count)
    span = group * row_count
    row_id = lax.broadcasted_iota(jnp.int32, (span, span), 0)
    col_id = lax.broadcasted_iota(jnp.int32, (span, span), 1)
    source = (row_id % group) * row_count + (row_id // group + row_index) % row_count
    order = jnp.where(col_id == source, 1.0, 0.0).astype(BF16)
    for part in range(2):
        for chunk in range(local_rows // group):
            base = (part * local_rows + chunk * group) * row_count
            mixed = inverse_ref[base:base + span, :]
            sorted_rows = jnp.dot(order, mixed, preferred_element_type=F32).astype(BF16)
            for owner in range(row_count):
                straight_ref[
                    part, chunk * group:(chunk + 1) * group, owner * block:(owner + 1) * block
                ] = sorted_rows[owner * group:(owner + 1) * group]


def compute_kernel(
    counts, supernodes, slot, widths_ref, weights_ref, place_ref, straight_ref, diag_ref, *refs
):
    row_count, col_count = counts
    block_refs, refs = refs[:row_count], refs[row_count:]
    own_refs, refs = refs[:col_count], refs[col_count:]
    keep_d_ref, send_d_ref, keep_t_ref, send_t_ref, term_ref, x_ref, y_ref = refs
    packed_width = block_refs[0].shape[0] // 2
    local_rows = straight_ref.shape[1]
    strips = local_rows // slot
    w_real = weights_ref[0, 0]
    w_imag = weights_ref[0, 1]
    col_index = place_ref[1]

    panel = jnp.concatenate([ref[...] for ref in block_refs], axis=1)
    with_real = rows_by_rows(panel, straight_ref[0])
    with_imag = rows_by_rows(panel, straight_ref[1])
    u_real = with_imag[packed_width:] - with_real[:packed_width]
    u_imag = -(with_real[packed_width:] + with_imag[:packed_width])
    weighted = w_real * u_real - w_imag * u_imag
    turned = w_real * u_imag + w_imag * u_real

    half = packed_width // 2
    upper = (col_index & (col_count // 2)) != 0
    keep_d_ref[...] = jnp.where(upper, weighted[half:], weighted[:half])
    send_d_ref[...] = jnp.where(upper, weighted[:half], weighted[half:])

    for ref, value in ((x_ref, weighted), (y_ref, turned)):
        for s in range(strips):
            ref[s, :packed_width] = value[:, s * slot:(s + 1) * slot]
            ref[s, packed_width:] = jnp.zeros((slot, slot), F32)

    own = [jnp.zeros((), BF16)] * col_count
    for c in range(col_count):
        block_of = own_refs[0][...]
        for other in range(1, col_count):
            block_of = jnp.where((col_index ^ c) == other, own_refs[other][...], block_of)
        own[c] = block_of
    own = jnp.concatenate(own, axis=1)
    offsets = offsets_of(widths_ref, supernodes)
    row_in_slot = lax.broadcasted_iota(jnp.int32, (slot, 1), 0)
    row_packed = lax.broadcasted_iota(jnp.int32, (packed_width, 1), 0)
    total = jnp.zeros((packed_width, slot), F32)
    for k in range(supernodes):
        valid = row_in_slot < widths_ref[k]
        x, y = (
            jnp.concatenate(
                [jnp.where(valid, ref[s, pl.ds(offsets[k], slot), :], 0.0) for s in range(strips)],
                axis=1,
            )
            for ref in (x_ref, y_ref)
        )
        x_high, y_high = x.astype(BF16), y.astype(BF16)
        x_low = (x - x_high.astype(F32)).astype(BF16)
        y_low = (y - y_high.astype(F32)).astype(BF16)
        product = (
            rows_by_rows(own[:packed_width], x_high) - rows_by_rows(own[packed_width:], y_high)
        ) + (rows_by_rows(own[:packed_width], x_low) - rows_by_rows(own[packed_width:], y_low))
        inside = (row_packed >= offsets[k]) & (row_packed < offsets[k + 1])
        total = jnp.where(inside, product, total)
    keep_t_ref[...] = jnp.where(upper, total[half:], total[:half])
    send_t_ref[...] = jnp.where(upper, total[:half], total[half:])

    folded = term_ref.shape[0]
    for s in range(strips):
        first = pl.multiple_of((col_index * strips + s) * folded, folded)
        term_ref[:, s * slot:(s + 1) * slot] = w_real * diag_ref[
            0, pl.ds(first, folded), :
        ].astype(F32) - w_imag * diag_ref[1, pl.ds(first, folded), :].astype(F32)


def expand_kernel(
    col_count, slot, widths_ref, place_ref, mine_d_ref, other_d_ref, mine_t_ref, other_t_ref,
    density_ref, diagonal_ref, strip_ref,
):
    supernodes = diagonal_ref.shape[0] // slot
    per_col, local_rows = density_ref.shape
    strips = local_rows // slot
    folded = per_col // strips
    share = col_count // 2
    tall = mine_d_ref.shape[0] // share
    part = tall - folded
    col_index = place_ref[1]
    upper = (col_index & share) != 0
    for side in range(2):
        own_side = upper if side else jnp.logical_not(upper)
        d_value = jnp.where(own_side, mine_d_ref[...], other_d_ref[...])
        t_value = jnp.where(own_side, mine_t_ref[...], other_t_ref[...])
        for q in range(share):
            owner = side * share + q
            base = owner * part
            for s in range(strips):
                lanes = slice(s * slot, (s + 1) * slot)
                strip_ref[s, base:base + part] = d_value[q * tall:q * tall + part, lanes]
                first = (owner * strips + s) * folded
                diagonal_ref[first:first + folded] = d_value[q * tall + part:(q + 1) * tall, lanes]
            rows = slice(q * part // 2, (q + 1) * part // 2)
            strip_ref[strips, base:base + part // 2] = t_value[rows, :slot]
            strip_ref[strips, base + part // 2:base + part] = t_value[rows, slot:]
    for s in range(strips + 1):
        strip_ref[s, col_count * part:] = jnp.zeros((slot, slot), F32)
    offsets = offsets_of(widths_ref, supernodes)
    row_in_slot = lax.broadcasted_iota(jnp.int32, (slot, 1), 0)
    for k in range(supernodes):
        product = strip_ref[strips, pl.ds(offsets[k], slot), :]
        product = jnp.where(row_in_slot < widths_ref[k], product, 0.0)
        diagonal_ref[k * slot:(k + 1) * slot] = diagonal_ref[k * slot:(k + 1) * slot] - product
    size = min(per_col, slot)
    row_in_part = lax.broadcasted_iota(jnp.int32, (size, 1), 0)
    for part in range(per_col // size):
        first = col_index * per_col + part * size
        owner = first // slot
        within = first % slot
        start, count = 0, 0
        for k in range(supernodes):
            start = start + jnp.where(k < owner, widths_ref[k], 0)
            count = count + jnp.where(k == owner, widths_ref[k], 0)
        for s in range(strips):
            piece = strip_ref[s, pl.ds(start + within, size), :]
            density_ref[part * size:(part + 1) * size, s * slot:(s + 1) * slot] = jnp.where(
                row_in_part < count - within, piece, 0.0
            )


def bits_of(count):
    return [1 << k for k in range(count.bit_length() - 1)]


def swap(value, axis, bit):
    return lax.ppermute(value, axis, [(i, i ^ bit) for i in range(lax.axis_size(axis))])


def pole_sum(value):
    bits = bits_of(lax.axis_size("pole"))
    half = value.shape[0] // 2
    first, second = value[:half], value[half:]
    for bit, mirrored in zip(bits, bits[::-1]):
        first, second = first + swap(first, "pole", bit), second + swap(second, "pole", mirrored)
    return first, second


def scatter_rest(value, axis):
    index = lax.axis_index(axis)
    for bit in bits_of(lax.axis_size(axis))[:-1][::-1]:
        half = value.shape[0] // 2
        upper = (index & bit) != 0
        keep = jnp.where(upper, value[half:], value[:half])
        value = keep + swap(jnp.where(upper, value[:half], value[half:]), axis, bit)
    return value


def gather_but_last(value, axis):
    index = lax.axis_index(axis)
    for bit in bits_of(lax.axis_size(axis))[:-1]:
        other = swap(value, axis, bit)
        upper = (index & bit) != 0
        value = jnp.concatenate(
            [jnp.where(upper, other, value), jnp.where(upper, value, other)], axis=0
        )
    return value


def per_device(found_inverse, l_panel, block_pattern, sup_widths, diag_inverse, pole_weights):
    slot = diag_inverse.shape[-1]
    total_cols = l_panel.shape[-1]
    supernodes = total_cols // slot
    packed_width = slot + (supernodes - 1) * (slot // 2)
    half = packed_width // 2
    local_rows = found_inverse.shape[2]
    block = l_panel.shape[2]
    row_count = lax.axis_size("row")
    col_count = lax.axis_size("col")
    top = col_count // 2
    place = jnp.stack([lax.axis_index("row"), lax.axis_index("col")]).astype(jnp.int32)

    packed = pl.pallas_call(
        functools.partial(pack_kernel, supernodes, slot),
        in_specs=[SMEM_SPEC, SMEM_SPEC, VMEM_SPEC],
        out_specs=VMEM_SPEC,
        out_shape=jax.ShapeDtypeStruct((2 * packed_width, block), BF16),
        compiler_params=PARAMS,
        name="pack",
    )(block_pattern, sup_widths, l_panel[0])

    blocks = {0: packed}
    for shift in sorted(range(1, row_count), key=lambda s: -min(s, row_count - s)):
        pairs = [((i + shift) % row_count, i) for i in range(row_count)]
        blocks[shift] = lax.ppermute(packed, "row", pairs)
    own = [packed] + [swap(packed, "col", other) for other in range(1, col_count)]

    straight = pl.pallas_call(
        functools.partial(prepare_kernel, row_count),
        in_specs=[SMEM_SPEC, VMEM_SPEC],
        out_specs=VMEM_SPEC,
        out_shape=jax.ShapeDtypeStruct((2, local_rows, row_count * block), BF16),
        compiler_params=PARAMS,
        cost_estimate=pl.CostEstimate(
            flops=4 * 256 * local_rows * row_count * block,
            bytes_accessed=8 * local_rows * row_count * block,
            transcendentals=0,
        ),
        name="prepare",
    )(place, found_inverse.reshape(2 * local_rows * row_count, block))

    keep_d, send_d, keep_t, send_t, term = pl.pallas_call(
        functools.partial(compute_kernel, (row_count, col_count), supernodes, slot),
        in_specs=[SMEM_SPEC] * 3 + [VMEM_SPEC] * (2 + row_count + col_count),
        out_specs=[VMEM_SPEC] * 5,
        out_shape=[jax.ShapeDtypeStruct((half, local_rows), F32)] * 2
        + [jax.ShapeDtypeStruct((half, slot), F32)] * 2
        + [jax.ShapeDtypeStruct((total_cols * slot // (col_count * local_rows), local_rows), F32)],
        scratch_shapes=[
            pltpu.VMEM((local_rows // slot, packed_width + slot, slot), F32),
            pltpu.VMEM((local_rows // slot, packed_width + slot, slot), F32),
        ],
        compiler_params=PARAMS,
        name="compute",
    )(
        sup_widths, pole_weights, place, straight, diag_inverse[0],
        *[blocks[shift] for shift in range(row_count)], *own,
    )

    products = scatter_rest(keep_t + swap(send_t, "col", top), "col")
    density = scatter_rest(keep_d + swap(send_d, "col", top), "col")
    products = jnp.concatenate(pole_sum(products), axis=1)
    for bit in bits_of(row_count):
        products = products + swap(products, "row", bit)
    density = jnp.concatenate(pole_sum(jnp.concatenate([density, term], axis=0)), axis=0)
    density = gather_but_last(density, "col")
    products = gather_but_last(products, "col")

    return pl.pallas_call(
        functools.partial(expand_kernel, col_count, slot),
        in_specs=[SMEM_SPEC] * 2 + [VMEM_SPEC] * 4,
        out_specs=[VMEM_SPEC] * 2,
        out_shape=[
            jax.ShapeDtypeStruct((total_cols // col_count, local_rows), F32),
            jax.ShapeDtypeStruct((total_cols, slot), F32),
        ],
        scratch_shapes=[pltpu.VMEM((local_rows // slot + 1, packed_width + slot, slot), F32)],
        compiler_params=PARAMS,
        name="expand",
    )(
        sup_widths, place, density, swap(density, "col", top),
        products, swap(products, "col", top),
    )


def solution(mesh):
    in_specs = (
        P("pole", None, "row", None, "col", None),
        P("pole", None, ("row", "col"), None),
        P(("row", "col"), None),
        P(),
        P("pole", None, None, None),
        P("pole", None),
    )
    out_specs = (P("col", "row"), P())
    return jax.shard_map(
        per_device, mesh=mesh, in_specs=in_specs, out_specs=out_specs, check_vma=False
    )
```

```python
import functools

import jax
import jax.numpy as jnp
from jax import lax
from jax.experimental import pallas as pl
from jax.experimental.pallas import tpu as pltpu
from jax.sharding import PartitionSpec as P

F32 = jnp.float32
BF16 = jnp.bfloat16
VMEM_SPEC = pl.BlockSpec(memory_space=pltpu.VMEM)
SMEM_SPEC = pl.BlockSpec(memory_space=pltpu.SMEM)
PARAMS = pltpu.CompilerParams(vmem_limit_bytes=48 * 1024 * 1024)


def rows_by_rows(left, right):
    return lax.dot_general(left, right, (((1,), (1,)), ((), ())), preferred_element_type=F32)


def offsets_of(widths_ref, supernodes):
    offsets = [0]
    for k in range(supernodes):
        offsets.append(offsets[-1] + widths_ref[k])
    return offsets


def pack_kernel(supernodes, slot, pattern_ref, widths_ref, panel_ref, packed_ref):
    packed_width = packed_ref.shape[0] // 2
    offsets = offsets_of(widths_ref, supernodes)
    lane = lax.broadcasted_iota(jnp.int32, (1, slot), 1)
    place = []
    for k in range(supernodes):
        valid = (lane < widths_ref[k]) & (pattern_ref[0, k] == 1)
        place.append(jnp.where(valid, offsets[k] + lane, -1))
    place = jnp.concatenate(place, axis=1)
    target = lax.broadcasted_iota(jnp.int32, (packed_width, supernodes * slot), 0)
    select = jnp.where(target == place, 1.0, 0.0).astype(BF16)
    for part in range(2):
        packed_ref[part * packed_width:(part + 1) * packed_width, :] = rows_by_rows(
            select, panel_ref[part]
        ).astype(BF16)


def prepare_kernel(row_count, place_ref, inverse_ref, straight_ref):
    block = inverse_ref.shape[1]
    local_rows = straight_ref.shape[1]
    row_index = place_ref[0]
    group = max(8, 256 // row_count)
    span = group * row_count
    row_id = lax.broadcasted_iota(jnp.int32, (span, span), 0)
    col_id = lax.broadcasted_iota(jnp.int32, (span, span), 1)
    source = (row_id % group) * row_count + (row_id // group + row_index) % row_count
    order = jnp.where(col_id == source, 1.0, 0.0).astype(BF16)
    for part in range(2):
        for chunk in range(local_rows // group):
            base = (part * local_rows + chunk * group) * row_count
            mixed = inverse_ref[base:base + span, :]
            sorted_rows = jnp.dot(order, mixed, preferred_element_type=F32).astype(BF16)
            for owner in range(row_count):
                straight_ref[
                    part, chunk * group:(chunk + 1) * group, owner * block:(owner + 1) * block
                ] = sorted_rows[owner * group:(owner + 1) * group]


def compute_kernel(
    counts, supernodes, slot, widths_ref, weights_ref, place_ref, straight_ref, diag_ref, *refs
):
    row_count, col_count = counts
    block_refs, refs = refs[:row_count], refs[row_count:]
    own_refs, refs = refs[:col_count], refs[col_count:]
    keep_d_ref, send_d_ref, keep_t_ref, send_t_ref, term_ref, x_ref, y_ref = refs
    packed_width = block_refs[0].shape[0] // 2
    local_rows = straight_ref.shape[1]
    strips = local_rows // slot
    w_real = weights_ref[0, 0]
    w_imag = weights_ref[0, 1]
    col_index = place_ref[1]

    panel = jnp.concatenate([ref[...] for ref in block_refs], axis=1)
    with_real = rows_by_rows(panel, straight_ref[0])
    with_imag = rows_by_rows(panel, straight_ref[1])
    u_real = with_imag[packed_width:] - with_real[:packed_width]
    u_imag = -(with_real[packed_width:] + with_imag[:packed_width])
    weighted = w_real * u_real - w_imag * u_imag
    turned = w_real * u_imag + w_imag * u_real

    half = packed_width // 2
    upper = (col_index & (col_count // 2)) != 0
    keep_d_ref[...] = jnp.where(upper, weighted[half:], weighted[:half])
    send_d_ref[...] = jnp.where(upper, weighted[:half], weighted[half:])

    for ref, value in ((x_ref, weighted), (y_ref, turned)):
        for s in range(strips):
            ref[s, :packed_width] = value[:, s * slot:(s + 1) * slot]
            ref[s, packed_width:] = jnp.zeros((slot, slot), F32)

    own = [jnp.zeros((), BF16)] * col_count
    for c in range(col_count):
        block_of = own_refs[0][...]
        for other in range(1, col_count):
            block_of = jnp.where((col_index ^ c) == other, own_refs[other][...], block_of)
        own[c] = block_of
    own = jnp.concatenate(own, axis=1)
    offsets = offsets_of(widths_ref, supernodes)
    row_in_slot = lax.broadcasted_iota(jnp.int32, (slot, 1), 0)
    row_packed = lax.broadcasted_iota(jnp.int32, (packed_width, 1), 0)
    total = jnp.zeros((packed_width, slot), F32)
    for k in range(supernodes):
        valid = row_in_slot < widths_ref[k]
        x, y = (
            jnp.concatenate(
                [jnp.where(valid, ref[s, pl.ds(offsets[k], slot), :], 0.0) for s in range(strips)],
                axis=1,
            )
            for ref in (x_ref, y_ref)
        )
        x_high, y_high = x.astype(BF16), y.astype(BF16)
        x_low = (x - x_high.astype(F32)).astype(BF16)
        y_low = (y - y_high.astype(F32)).astype(BF16)
        product = (
            rows_by_rows(own[:packed_width], x_high) - rows_by_rows(own[packed_width:], y_high)
        ) + (rows_by_rows(own[:packed_width], x_low) - rows_by_rows(own[packed_width:], y_low))
        inside = (row_packed >= offsets[k]) & (row_packed < offsets[k + 1])
        total = jnp.where(inside, product, total)
    keep_t_ref[...] = jnp.where(upper, total[half:], total[:half])
    send_t_ref[...] = jnp.where(upper, total[:half], total[half:])

    folded = term_ref.shape[0]
    for s in range(strips):
        first = pl.multiple_of((col_index * strips + s) * folded, folded)
        term_ref[:, s * slot:(s + 1) * slot] = w_real * diag_ref[
            0, pl.ds(first, folded), :
        ].astype(F32) - w_imag * diag_ref[1, pl.ds(first, folded), :].astype(F32)


def expand_kernel(
    col_count, slot, widths_ref, place_ref, mine_d_ref, other_d_ref, mine_t_ref, other_t_ref,
    density_ref, diagonal_ref, strip_ref,
):
    supernodes = diagonal_ref.shape[0] // slot
    per_col, local_rows = density_ref.shape
    strips = local_rows // slot
    folded = per_col // strips
    share = col_count // 2
    tall = mine_d_ref.shape[0] // share
    part = tall - folded
    col_index = place_ref[1]
    upper = (col_index & share) != 0
    for side in range(2):
        own_side = upper if side else jnp.logical_not(upper)
        d_value = jnp.where(own_side, mine_d_ref[...], other_d_ref[...])
        t_value = jnp.where(own_side, mine_t_ref[...], other_t_ref[...])
        for q in range(share):
            owner = side * share + q
            base = owner * part
            for s in range(strips):
                lanes = slice(s * slot, (s + 1) * slot)
                strip_ref[s, base:base + part] = d_value[q * tall:q * tall + part, lanes]
                first = (owner * strips + s) * folded
                diagonal_ref[first:first + folded] = d_value[q * tall + part:(q + 1) * tall, lanes]
            rows = slice(q * part // 2, (q + 1) * part // 2)
            strip_ref[strips, base:base + part // 2] = t_value[rows, :slot]
            strip_ref[strips, base + part // 2:base + part] = t_value[rows, slot:]
    for s in range(strips + 1):
        strip_ref[s, col_count * part:] = jnp.zeros((slot, slot), F32)
    offsets = offsets_of(widths_ref, supernodes)
    row_in_slot = lax.broadcasted_iota(jnp.int32, (slot, 1), 0)
    for k in range(supernodes):
        product = strip_ref[strips, pl.ds(offsets[k], slot), :]
        product = jnp.where(row_in_slot < widths_ref[k], product, 0.0)
        diagonal_ref[k * slot:(k + 1) * slot] = diagonal_ref[k * slot:(k + 1) * slot] - product
    size = min(per_col, slot)
    row_in_part = lax.broadcasted_iota(jnp.int32, (size, 1), 0)
    for part in range(per_col // size):
        first = col_index * per_col + part * size
        owner = first // slot
        within = first % slot
        start, count = 0, 0
        for k in range(supernodes):
            start = start + jnp.where(k < owner, widths_ref[k], 0)
            count = count + jnp.where(k == owner, widths_ref[k], 0)
        for s in range(strips):
            piece = strip_ref[s, pl.ds(start + within, size), :]
            density_ref[part * size:(part + 1) * size, s * slot:(s + 1) * slot] = jnp.where(
                row_in_part < count - within, piece, 0.0
            )


def bits_of(count):
    return [1 << k for k in range(count.bit_length() - 1)]


def swap(value, axis, bit):
    return lax.ppermute(value, axis, [(i, i ^ bit) for i in range(lax.axis_size(axis))])


def halves_of(value):
    half = value.shape[0] // 2
    return value[:half], value[half:]


def scatter_rest(value, axis):
    index = lax.axis_index(axis)
    for bit in bits_of(lax.axis_size(axis))[:-1][::-1]:
        half = value.shape[0] // 2
        upper = (index & bit) != 0
        keep = jnp.where(upper, value[half:], value[:half])
        value = keep + swap(jnp.where(upper, value[:half], value[half:]), axis, bit)
    return value


def gather_but_last(value, axis):
    index = lax.axis_index(axis)
    for bit in bits_of(lax.axis_size(axis))[:-1]:
        other = swap(value, axis, bit)
        upper = (index & bit) != 0
        value = jnp.concatenate(
            [jnp.where(upper, other, value), jnp.where(upper, value, other)], axis=0
        )
    return value


def per_device(found_inverse, l_panel, block_pattern, sup_widths, diag_inverse, pole_weights):
    slot = diag_inverse.shape[-1]
    total_cols = l_panel.shape[-1]
    supernodes = total_cols // slot
    packed_width = slot + (supernodes - 1) * (slot // 2)
    half = packed_width // 2
    local_rows = found_inverse.shape[2]
    block = l_panel.shape[2]
    row_count = lax.axis_size("row")
    col_count = lax.axis_size("col")
    top = col_count // 2
    place = jnp.stack([lax.axis_index("row"), lax.axis_index("col")]).astype(jnp.int32)

    packed = pl.pallas_call(
        functools.partial(pack_kernel, supernodes, slot),
        in_specs=[SMEM_SPEC, SMEM_SPEC, VMEM_SPEC],
        out_specs=VMEM_SPEC,
        out_shape=jax.ShapeDtypeStruct((2 * packed_width, block), BF16),
        compiler_params=PARAMS,
        name="pack",
    )(block_pattern, sup_widths, l_panel[0])

    blocks = {0: packed}
    for shift in sorted(range(1, row_count), key=lambda s: -min(s, row_count - s)):
        pairs = [((i + shift) % row_count, i) for i in range(row_count)]
        blocks[shift] = lax.ppermute(packed, "row", pairs)
    own = [packed] + [swap(packed, "col", other) for other in range(1, col_count)]

    straight = pl.pallas_call(
        functools.partial(prepare_kernel, row_count),
        in_specs=[SMEM_SPEC, VMEM_SPEC],
        out_specs=VMEM_SPEC,
        out_shape=jax.ShapeDtypeStruct((2, local_rows, row_count * block), BF16),
        compiler_params=PARAMS,
        cost_estimate=pl.CostEstimate(
            flops=4 * 256 * local_rows * row_count * block,
            bytes_accessed=8 * local_rows * row_count * block,
            transcendentals=0,
        ),
        name="prepare",
    )(place, found_inverse.reshape(2 * local_rows * row_count, block))

    keep_d, send_d, keep_t, send_t, term = pl.pallas_call(
        functools.partial(compute_kernel, (row_count, col_count), supernodes, slot),
        in_specs=[SMEM_SPEC] * 3 + [VMEM_SPEC] * (2 + row_count + col_count),
        out_specs=[VMEM_SPEC] * 5,
        out_shape=[jax.ShapeDtypeStruct((half, local_rows), F32)] * 2
        + [jax.ShapeDtypeStruct((half, slot), F32)] * 2
        + [jax.ShapeDtypeStruct((total_cols * slot // (col_count * local_rows), local_rows), F32)],
        scratch_shapes=[
            pltpu.VMEM((local_rows // slot, packed_width + slot, slot), F32),
            pltpu.VMEM((local_rows // slot, packed_width + slot, slot), F32),
        ],
        compiler_params=PARAMS,
        name="compute",
    )(
        sup_widths, pole_weights, place, straight, diag_inverse[0],
        *[blocks[shift] for shift in range(row_count)], *own,
    )

    tie = lax.optimization_barrier
    products = keep_t + swap(send_t, "col", top)
    products, send_d = tie((scatter_rest(products, "col"), send_d))
    first, second = halves_of(products)
    bits = bits_of(lax.axis_size("pole"))
    for bit, mirrored in zip(bits, bits[::-1]):
        first, second = tie((
            first + swap(first, "pole", bit), second + swap(second, "pole", mirrored)
        ))
    products = jnp.concatenate([first, second], axis=1)
    density = scatter_rest(keep_d + swap(send_d, "col", top), "col")
    low, high = halves_of(jnp.concatenate([density, term], axis=0))
    products, low, high = tie((products, low, high))
    row_bits = bits_of(row_count)
    for step in range(max(len(bits), len(row_bits))):
        if step < len(row_bits):
            products = products + swap(products, "row", row_bits[step])
        if step < len(bits):
            low, high = (
                low + swap(low, "pole", bits[step]), high + swap(high, "pole", bits[-1 - step])
            )
        products, low, high = tie((products, low, high))
    density = jnp.concatenate([low, high], axis=0)
    density = gather_but_last(density, "col")
    products = gather_but_last(products, "col")

    return pl.pallas_call(
        functools.partial(expand_kernel, col_count, slot),
        in_specs=[SMEM_SPEC] * 2 + [VMEM_SPEC] * 4,
        out_specs=[VMEM_SPEC] * 2,
        out_shape=[
            jax.ShapeDtypeStruct((total_cols // col_count, local_rows), F32),
            jax.ShapeDtypeStruct((total_cols, slot), F32),
        ],
        scratch_shapes=[pltpu.VMEM((local_rows // slot + 1, packed_width + slot, slot), F32)],
        compiler_params=PARAMS,
        name="expand",
    )(
        sup_widths, place, density, swap(density, "col", top),
        products, swap(products, "col", top),
    )


def solution(mesh):
    in_specs = (
        P("pole", None, "row", None, "col", None),
        P("pole", None, ("row", "col"), None),
        P(("row", "col"), None),
        P(),
        P("pole", None, None, None),
        P("pole", None),
    )
    out_specs = (P("col", "row"), P())
    return jax.shard_map(
        per_device, mesh=mesh, in_specs=in_specs, out_specs=out_specs, check_vma=False
    )
```

```python
import functools

import jax
import jax.numpy as jnp
from jax import lax
from jax.experimental import pallas as pl
from jax.experimental.pallas import tpu as pltpu
from jax.sharding import PartitionSpec as P

F32 = jnp.float32
BF16 = jnp.bfloat16
VMEM_SPEC = pl.BlockSpec(memory_space=pltpu.VMEM)
SMEM_SPEC = pl.BlockSpec(memory_space=pltpu.SMEM)
PARAMS = pltpu.CompilerParams(vmem_limit_bytes=48 * 1024 * 1024)


def rows_by_rows(left, right):
    return lax.dot_general(left, right, (((1,), (1,)), ((), ())), preferred_element_type=F32)


def offsets_of(widths_ref, supernodes):
    offsets = [0]
    for k in range(supernodes):
        offsets.append(offsets[-1] + widths_ref[k])
    return offsets


def pack_kernel(supernodes, slot, pattern_ref, widths_ref, panel_ref, packed_ref):
    packed_width = packed_ref.shape[0] // 2
    offsets = offsets_of(widths_ref, supernodes)
    lane = lax.broadcasted_iota(jnp.int32, (1, slot), 1)
    place = []
    for k in range(supernodes):
        valid = (lane < widths_ref[k]) & (pattern_ref[0, k] == 1)
        place.append(jnp.where(valid, offsets[k] + lane, -1))
    place = jnp.concatenate(place, axis=1)
    target = lax.broadcasted_iota(jnp.int32, (packed_width, supernodes * slot), 0)
    select = jnp.where(target == place, 1.0, 0.0).astype(BF16)
    for part in range(2):
        packed_ref[part * packed_width:(part + 1) * packed_width, :] = rows_by_rows(
            select, panel_ref[part]
        ).astype(BF16)


def prepare_kernel(row_count, place_ref, inverse_ref, straight_ref):
    block = inverse_ref.shape[1]
    local_rows = straight_ref.shape[1]
    row_index = place_ref[0]
    group = max(8, 256 // row_count)
    span = group * row_count
    row_id = lax.broadcasted_iota(jnp.int32, (span, span), 0)
    col_id = lax.broadcasted_iota(jnp.int32, (span, span), 1)
    source = (row_id % group) * row_count + (row_id // group + row_index) % row_count
    order = jnp.where(col_id == source, 1.0, 0.0).astype(BF16)
    for part in range(2):
        for chunk in range(local_rows // group):
            base = (part * local_rows + chunk * group) * row_count
            mixed = inverse_ref[base:base + span, :]
            sorted_rows = jnp.dot(order, mixed, preferred_element_type=F32).astype(BF16)
            for owner in range(row_count):
                straight_ref[
                    part, chunk * group:(chunk + 1) * group, owner * block:(owner + 1) * block
                ] = sorted_rows[owner * group:(owner + 1) * group]


def compute_kernel(
    counts, supernodes, slot, widths_ref, weights_ref, place_ref, straight_ref, diag_ref, *refs
):
    row_count, col_count = counts
    block_refs, refs = refs[:row_count], refs[row_count:]
    own_refs, refs = refs[:col_count], refs[col_count:]
    density_ref, product_ref, term_ref, x_ref, y_ref = refs
    packed_width = block_refs[0].shape[0] // 2
    local_rows = straight_ref.shape[1]
    strips = local_rows // slot
    w_real = weights_ref[0, 0]
    w_imag = weights_ref[0, 1]
    col_index = place_ref[1]

    panel = jnp.concatenate([ref[...] for ref in block_refs], axis=1)
    with_real = rows_by_rows(panel, straight_ref[0])
    with_imag = rows_by_rows(panel, straight_ref[1])
    u_real = with_imag[packed_width:] - with_real[:packed_width]
    u_imag = -(with_real[packed_width:] + with_imag[:packed_width])
    weighted = w_real * u_real - w_imag * u_imag
    turned = w_real * u_imag + w_imag * u_real

    density_ref[...] = weighted
    for ref, value in ((x_ref, weighted), (y_ref, turned)):
        for s in range(strips):
            ref[s, :packed_width] = value[:, s * slot:(s + 1) * slot]
            ref[s, packed_width:] = jnp.zeros((slot, slot), F32)

    own = [jnp.zeros((), BF16)] * col_count
    for c in range(col_count):
        block_of = own_refs[0][...]
        for other in range(1, col_count):
            block_of = jnp.where((col_index ^ c) == other, own_refs[other][...], block_of)
        own[c] = block_of
    own = jnp.concatenate(own, axis=1)
    offsets = offsets_of(widths_ref, supernodes)
    row_in_slot = lax.broadcasted_iota(jnp.int32, (slot, 1), 0)
    row_packed = lax.broadcasted_iota(jnp.int32, (packed_width, 1), 0)
    total = jnp.zeros((packed_width, slot), F32)
    for k in range(supernodes):
        valid = row_in_slot < widths_ref[k]
        x, y = (
            jnp.concatenate(
                [jnp.where(valid, ref[s, pl.ds(offsets[k], slot), :], 0.0) for s in range(strips)],
                axis=1,
            )
            for ref in (x_ref, y_ref)
        )
        x_high, y_high = x.astype(BF16), y.astype(BF16)
        x_low = (x - x_high.astype(F32)).astype(BF16)
        y_low = (y - y_high.astype(F32)).astype(BF16)
        product = (
            rows_by_rows(own[:packed_width], x_high) - rows_by_rows(own[packed_width:], y_high)
        ) + (rows_by_rows(own[:packed_width], x_low) - rows_by_rows(own[packed_width:], y_low))
        inside = (row_packed >= offsets[k]) & (row_packed < offsets[k + 1])
        total = jnp.where(inside, product, total)
    product_ref[...] = total

    folded = term_ref.shape[0]
    flag = (col_index == density_root(col_count)).astype(F32)
    for s in range(strips):
        rows = slice(s * folded, (s + 1) * folded)
        term_ref[:, s * slot:(s + 1) * slot] = flag * (
            w_real * diag_ref[0, rows].astype(F32) - w_imag * diag_ref[1, rows].astype(F32)
        )


def expand_kernel(
    slot, widths_ref, place_ref, mine_d_ref, other_d_ref, mine_t_ref, other_t_ref,
    density_ref, diagonal_ref, strip_ref,
):
    total_cols = diagonal_ref.shape[0]
    supernodes = total_cols // slot
    per_col, local_rows = density_ref.shape
    strips = local_rows // slot
    folded = total_cols // strips
    packed_width = mine_t_ref.shape[0]
    col_index = place_ref[1]
    has_d = place_ref[2] != 0
    has_t = place_ref[3] != 0
    d_value = jnp.where(has_d, mine_d_ref[...], other_d_ref[...])
    for s in range(strips):
        lanes = slice(s * slot, (s + 1) * slot)
        strip_ref[s, :packed_width] = d_value[:packed_width, lanes]
        diagonal_ref[s * folded:(s + 1) * folded] = d_value[packed_width:, lanes]
    strip_ref[strips, :packed_width] = jnp.where(has_t, mine_t_ref[...], other_t_ref[...])
    for s in range(strips + 1):
        strip_ref[s, packed_width:] = jnp.zeros((slot, slot), F32)
    offsets = offsets_of(widths_ref, supernodes)
    row_in_slot = lax.broadcasted_iota(jnp.int32, (slot, 1), 0)
    for k in range(supernodes):
        product = strip_ref[strips, pl.ds(offsets[k], slot), :]
        product = jnp.where(row_in_slot < widths_ref[k], product, 0.0)
        diagonal_ref[k * slot:(k + 1) * slot] = diagonal_ref[k * slot:(k + 1) * slot] - product
    size = min(per_col, slot)
    row_in_part = lax.broadcasted_iota(jnp.int32, (size, 1), 0)
    for part in range(per_col // size):
        first = col_index * per_col + part * size
        owner = first // slot
        within = first % slot
        start, count = 0, 0
        for k in range(supernodes):
            start = start + jnp.where(k < owner, widths_ref[k], 0)
            count = count + jnp.where(k == owner, widths_ref[k], 0)
        for s in range(strips):
            piece = strip_ref[s, pl.ds(start + within, size), :]
            density_ref[part * size:(part + 1) * size, s * slot:(s + 1) * slot] = jnp.where(
                row_in_part < count - within, piece, 0.0
            )


def bits_of(count):
    return [1 << k for k in range(count.bit_length() - 1)]


def product_root(col_count):
    return 0


def density_root(col_count):
    return min(1, col_count - 1)


def swap(value, axis, bit):
    return lax.ppermute(value, axis, [(i, i ^ bit) for i in range(lax.axis_size(axis))])


def swap_at(value, axis, bit, col):
    col_count = lax.axis_size("col")
    return lax.ppermute(
        value, (axis, "col"),
        [(i * col_count + col, (i ^ bit) * col_count + col) for i in range(lax.axis_size(axis))],
    )


def sum_onto(value, root):
    count = lax.axis_size("col")
    for bit in bits_of(count):
        pairs = [(i ^ root, i ^ bit ^ root) for i in range(bit, count, 2 * bit)]
        value = value + lax.ppermute(value, "col", pairs)
    return value


def spread_from(value, root):
    count = lax.axis_size("col")
    relative = lax.axis_index("col") ^ root
    received = value
    for bit in bits_of(count)[::-1]:
        pairs = [(i ^ root, i ^ bit ^ root) for i in range(0, count, 2 * bit)]
        received = lax.ppermute(value, "col", pairs)
        if bit > 1:
            value = jnp.where(relative % (2 * bit) == bit, received, value)
    return value, received


def per_device(found_inverse, l_panel, block_pattern, sup_widths, diag_inverse, pole_weights):
    slot = diag_inverse.shape[-1]
    total_cols = l_panel.shape[-1]
    supernodes = total_cols // slot
    packed_width = slot + (supernodes - 1) * (slot // 2)
    local_rows = found_inverse.shape[2]
    block = l_panel.shape[2]
    row_count = lax.axis_size("row")
    col_count = lax.axis_size("col")
    t_root, d_root = product_root(col_count), density_root(col_count)
    col_index = lax.axis_index("col")
    has_d, has_t = (col_index ^ d_root) % 2 == 0, (col_index ^ t_root) % 2 == 0
    place = jnp.stack([lax.axis_index("row"), col_index, has_d, has_t]).astype(jnp.int32)

    packed = pl.pallas_call(
        functools.partial(pack_kernel, supernodes, slot),
        in_specs=[SMEM_SPEC, SMEM_SPEC, VMEM_SPEC],
        out_specs=VMEM_SPEC,
        out_shape=jax.ShapeDtypeStruct((2 * packed_width, block), BF16),
        name="pack",
    )(block_pattern, sup_widths, l_panel[0])

    blocks = {0: packed}
    for shift in sorted(range(1, row_count), key=lambda s: -min(s, row_count - s)):
        pairs = [((i + shift) % row_count, i) for i in range(row_count)]
        blocks[shift] = lax.ppermute(packed, "row", pairs)
    own = [packed] + [swap(packed, "col", other) for other in range(1, col_count)]

    straight = pl.pallas_call(
        functools.partial(prepare_kernel, row_count),
        in_specs=[SMEM_SPEC, VMEM_SPEC],
        out_specs=VMEM_SPEC,
        out_shape=jax.ShapeDtypeStruct((2, local_rows, row_count * block), BF16),
        compiler_params=PARAMS,
        cost_estimate=pl.CostEstimate(
            flops=4 * 256 * local_rows * row_count * block,
            bytes_accessed=8 * local_rows * row_count * block,
            transcendentals=0,
        ),
        name="prepare",
    )(place, found_inverse.reshape(2 * local_rows * row_count, block))

    density, products, term = pl.pallas_call(
        functools.partial(compute_kernel, (row_count, col_count), supernodes, slot),
        in_specs=[SMEM_SPEC] * 3 + [VMEM_SPEC] * (2 + row_count + col_count),
        out_specs=[VMEM_SPEC] * 3,
        out_shape=[
            jax.ShapeDtypeStruct((packed_width, local_rows), F32),
            jax.ShapeDtypeStruct((packed_width, slot), F32),
            jax.ShapeDtypeStruct((total_cols * slot // local_rows, local_rows), F32),
        ],
        scratch_shapes=[
            pltpu.VMEM((local_rows // slot, packed_width + slot, slot), F32),
            pltpu.VMEM((local_rows // slot, packed_width + slot, slot), F32),
        ],
        compiler_params=PARAMS,
        name="compute",
    )(
        sup_widths, pole_weights, place, straight, diag_inverse[0],
        *[blocks[shift] for shift in range(row_count)], *own,
    )

    products, density = lax.optimization_barrier((sum_onto(products, t_root), density))
    density = jnp.concatenate([sum_onto(density, d_root), term], axis=0)
    for bit in bits_of(lax.axis_size("pole")):
        products = products + swap_at(products, "pole", bit, t_root)
        density = density + swap_at(density, "pole", bit, d_root)
    for bit in bits_of(row_count):
        products = products + swap_at(products, "row", bit, t_root)

    return pl.pallas_call(
        functools.partial(expand_kernel, slot),
        in_specs=[SMEM_SPEC] * 2 + [VMEM_SPEC] * 4,
        out_specs=[VMEM_SPEC] * 2,
        out_shape=[
            jax.ShapeDtypeStruct((total_cols // col_count, local_rows), F32),
            jax.ShapeDtypeStruct((total_cols, slot), F32),
        ],
        scratch_shapes=[pltpu.VMEM((local_rows // slot + 1, packed_width + slot, slot), F32)],
        compiler_params=PARAMS,
        name="expand",
    )(sup_widths, place, *spread_from(density, d_root), *spread_from(products, t_root))


def solution(mesh):
    in_specs = (
        P("pole", None, "row", None, "col", None),
        P("pole", None, ("row", "col"), None),
        P(("row", "col"), None),
        P(),
        P("pole", None, None, None),
        P("pole", None),
    )
    out_specs = (P("col", "row"), P())
    return jax.shard_map(
        per_device, mesh=mesh, in_specs=in_specs, out_specs=out_specs, check_vma=False
    )
```

```python
import functools

import jax
import jax.numpy as jnp
from jax import lax
from jax.experimental import pallas as pl
from jax.experimental.pallas import tpu as pltpu
from jax.sharding import PartitionSpec as P

F32 = jnp.float32
BF16 = jnp.bfloat16
VMEM_SPEC = pl.BlockSpec(memory_space=pltpu.VMEM)
SMEM_SPEC = pl.BlockSpec(memory_space=pltpu.SMEM)
PARAMS = pltpu.CompilerParams(vmem_limit_bytes=48 * 1024 * 1024)


def rows_by_rows(left, right):
    return lax.dot_general(left, right, (((1,), (1,)), ((), ())), preferred_element_type=F32)


def offsets_of(widths_ref, supernodes):
    offsets = [0]
    for k in range(supernodes):
        offsets.append(offsets[-1] + widths_ref[k])
    return offsets


def pack_kernel(supernodes, slot, pattern_ref, widths_ref, panel_ref, packed_ref):
    packed_width = packed_ref.shape[0] // 2
    offsets = offsets_of(widths_ref, supernodes)
    lane = lax.broadcasted_iota(jnp.int32, (1, slot), 1)
    place = []
    for k in range(supernodes):
        valid = (lane < widths_ref[k]) & (pattern_ref[0, k] == 1)
        place.append(jnp.where(valid, offsets[k] + lane, -1))
    place = jnp.concatenate(place, axis=1)
    target = lax.broadcasted_iota(jnp.int32, (packed_width, supernodes * slot), 0)
    select = jnp.where(target == place, 1.0, 0.0).astype(BF16)
    for part in range(2):
        packed_ref[part * packed_width:(part + 1) * packed_width, :] = rows_by_rows(
            select, panel_ref[part]
        ).astype(BF16)


def prepare_kernel(row_count, place_ref, inverse_ref, straight_ref):
    block = inverse_ref.shape[1]
    local_rows = straight_ref.shape[1]
    row_index = place_ref[0]
    group = max(8, 256 // row_count)
    span = group * row_count
    row_id = lax.broadcasted_iota(jnp.int32, (span, span), 0)
    col_id = lax.broadcasted_iota(jnp.int32, (span, span), 1)
    source = (row_id % group) * row_count + (row_id // group + row_index) % row_count
    order = jnp.where(col_id == source, 1.0, 0.0).astype(BF16)
    for part in range(2):
        for chunk in range(local_rows // group):
            base = (part * local_rows + chunk * group) * row_count
            mixed = inverse_ref[base:base + span, :]
            sorted_rows = jnp.dot(order, mixed, preferred_element_type=F32).astype(BF16)
            for owner in range(row_count):
                straight_ref[
                    part, chunk * group:(chunk + 1) * group, owner * block:(owner + 1) * block
                ] = sorted_rows[owner * group:(owner + 1) * group]


def weigh_kernel(weights_ref, diag_ref, packed_ref, term_ref):
    del packed_ref
    term_ref[...] = weights_ref[0, 0] * diag_ref[0].astype(F32) - weights_ref[
        0, 1
    ] * diag_ref[1].astype(F32)


def compute_kernel(
    counts, supernodes, slot, widths_ref, weights_ref, place_ref, straight_ref, *refs
):
    row_count, col_count = counts
    block_refs, refs = refs[:row_count], refs[row_count:]
    own_refs, refs = refs[:col_count], refs[col_count:]
    keep_d_ref, send_d_ref, keep_t_ref, send_t_ref, x_ref, y_ref = refs
    packed_width = block_refs[0].shape[0] // 2
    local_rows = straight_ref.shape[1]
    strips = local_rows // slot
    w_real = weights_ref[0, 0]
    w_imag = weights_ref[0, 1]
    col_index = place_ref[1]

    panel = jnp.concatenate([ref[...] for ref in block_refs], axis=1)
    with_real = rows_by_rows(panel, straight_ref[0])
    with_imag = rows_by_rows(panel, straight_ref[1])
    u_real = with_imag[packed_width:] - with_real[:packed_width]
    u_imag = -(with_real[packed_width:] + with_imag[:packed_width])
    weighted = w_real * u_real - w_imag * u_imag
    turned = w_real * u_imag + w_imag * u_real

    half = packed_width // 2
    upper = (col_index & (col_count // 2)) != 0
    keep_d_ref[...] = jnp.where(upper, weighted[half:], weighted[:half])
    send_d_ref[...] = jnp.where(upper, weighted[:half], weighted[half:])

    for ref, value in ((x_ref, weighted), (y_ref, turned)):
        for s in range(strips):
            ref[s, :packed_width] = value[:, s * slot:(s + 1) * slot]
            ref[s, packed_width:] = jnp.zeros((slot, slot), F32)

    own = [jnp.zeros((), BF16)] * col_count
    for c in range(col_count):
        block_of = own_refs[0][...]
        for other in range(1, col_count):
            block_of = jnp.where((col_index ^ c) == other, own_refs[other][...], block_of)
        own[c] = block_of
    own = jnp.concatenate(own, axis=1)
    offsets = offsets_of(widths_ref, supernodes)
    row_in_slot = lax.broadcasted_iota(jnp.int32, (slot, 1), 0)
    row_packed = lax.broadcasted_iota(jnp.int32, (packed_width, 1), 0)
    total = jnp.zeros((packed_width, slot), F32)
    for k in range(supernodes):
        valid = row_in_slot < widths_ref[k]
        x, y = (
            jnp.concatenate(
                [jnp.where(valid, ref[s, pl.ds(offsets[k], slot), :], 0.0) for s in range(strips)],
                axis=1,
            )
            for ref in (x_ref, y_ref)
        )
        x_high, y_high = x.astype(BF16), y.astype(BF16)
        x_low = (x - x_high.astype(F32)).astype(BF16)
        y_low = (y - y_high.astype(F32)).astype(BF16)
        product = (
            rows_by_rows(own[:packed_width], x_high) - rows_by_rows(own[packed_width:], y_high)
        ) + (rows_by_rows(own[:packed_width], x_low) - rows_by_rows(own[packed_width:], y_low))
        inside = (row_packed >= offsets[k]) & (row_packed < offsets[k + 1])
        total = jnp.where(inside, product, total)
    keep_t_ref[...] = jnp.where(upper, total[half:], total[:half])
    send_t_ref[...] = jnp.where(upper, total[:half], total[half:])


def expand_kernel(
    col_count, slot, widths_ref, place_ref, mine_d_ref, other_d_ref, mine_t_ref, other_t_ref,
    term_ref, density_ref, diagonal_ref, strip_ref,
):
    supernodes = diagonal_ref.shape[0] // slot
    per_col, local_rows = density_ref.shape
    strips = local_rows // slot
    share = col_count // 2
    part = mine_d_ref.shape[0] // share
    col_index = place_ref[1]
    upper = (col_index & share) != 0
    for side in range(2):
        own_side = upper if side else jnp.logical_not(upper)
        d_value = jnp.where(own_side, mine_d_ref[...], other_d_ref[...])
        t_value = jnp.where(own_side, mine_t_ref[...], other_t_ref[...])
        for q in range(share):
            owner = side * share + q
            base = owner * part
            for s in range(strips):
                lanes = slice(s * slot, (s + 1) * slot)
                strip_ref[s, base:base + part] = d_value[q * part:(q + 1) * part, lanes]
            strip_ref[strips, base:base + part] = t_value[q * part:(q + 1) * part]
    for s in range(strips + 1):
        strip_ref[s, col_count * part:] = jnp.zeros((slot, slot), F32)
    offsets = offsets_of(widths_ref, supernodes)
    row_in_slot = lax.broadcasted_iota(jnp.int32, (slot, 1), 0)
    for k in range(supernodes):
        product = strip_ref[strips, pl.ds(offsets[k], slot), :]
        product = jnp.where(row_in_slot < widths_ref[k], product, 0.0)
        diagonal_ref[k * slot:(k + 1) * slot] = (
            tree_sum([term_ref[p, k * slot:(k + 1) * slot] for p in range(term_ref.shape[0])])
            - product
        )
    size = min(per_col, slot)
    row_in_part = lax.broadcasted_iota(jnp.int32, (size, 1), 0)
    for part in range(per_col // size):
        first = col_index * per_col + part * size
        owner = first // slot
        within = first % slot
        start, count = 0, 0
        for k in range(supernodes):
            start = start + jnp.where(k < owner, widths_ref[k], 0)
            count = count + jnp.where(k == owner, widths_ref[k], 0)
        for s in range(strips):
            piece = strip_ref[s, pl.ds(start + within, size), :]
            density_ref[part * size:(part + 1) * size, s * slot:(s + 1) * slot] = jnp.where(
                row_in_part < count - within, piece, 0.0
            )


def bits_of(count):
    return [1 << k for k in range(count.bit_length() - 1)]


def swap(value, axis, bit):
    return lax.ppermute(value, axis, [(i, i ^ bit) for i in range(lax.axis_size(axis))])


def tree_sum(terms):
    while len(terms) > 1:
        terms = [terms[j] + terms[j + 1] for j in range(0, len(terms), 2)]
    return terms[0]


def sum_direct(value, axis):
    return tree_sum([value] + [swap(value, axis, j) for j in range(1, lax.axis_size(axis))])


def scatter_rest(value, axis):
    index = lax.axis_index(axis)
    for bit in bits_of(lax.axis_size(axis))[:-1][::-1]:
        half = value.shape[0] // 2
        upper = (index & bit) != 0
        keep = jnp.where(upper, value[half:], value[:half])
        value = keep + swap(jnp.where(upper, value[:half], value[half:]), axis, bit)
    return value


def gather_but_last(value, axis):
    index = lax.axis_index(axis)
    for bit in bits_of(lax.axis_size(axis))[:-1]:
        other = swap(value, axis, bit)
        upper = (index & bit) != 0
        value = jnp.concatenate(
            [jnp.where(upper, other, value), jnp.where(upper, value, other)], axis=0
        )
    return value


def per_device(found_inverse, l_panel, block_pattern, sup_widths, diag_inverse, pole_weights):
    slot = diag_inverse.shape[-1]
    total_cols = l_panel.shape[-1]
    supernodes = total_cols // slot
    packed_width = slot + (supernodes - 1) * (slot // 2)
    half = packed_width // 2
    local_rows = found_inverse.shape[2]
    block = l_panel.shape[2]
    row_count = lax.axis_size("row")
    col_count = lax.axis_size("col")
    top = col_count // 2
    place = jnp.stack([lax.axis_index("row"), lax.axis_index("col")]).astype(jnp.int32)

    packed = pl.pallas_call(
        functools.partial(pack_kernel, supernodes, slot),
        in_specs=[SMEM_SPEC, SMEM_SPEC, VMEM_SPEC],
        out_specs=VMEM_SPEC,
        out_shape=jax.ShapeDtypeStruct((2 * packed_width, block), BF16),
        name="pack",
    )(block_pattern, sup_widths, l_panel[0])

    blocks = {0: packed}
    for shift in sorted(range(1, row_count), key=lambda s: -min(s, row_count - s)):
        pairs = [((i + shift) % row_count, i) for i in range(row_count)]
        blocks[shift] = lax.ppermute(packed, "row", pairs)
    own = [packed] + [swap(packed, "col", other) for other in range(1, col_count)]

    straight = pl.pallas_call(
        functools.partial(prepare_kernel, row_count),
        in_specs=[SMEM_SPEC, VMEM_SPEC],
        out_specs=VMEM_SPEC,
        out_shape=jax.ShapeDtypeStruct((2, local_rows, row_count * block), BF16),
        compiler_params=PARAMS,
        cost_estimate=pl.CostEstimate(
            flops=4 * 256 * local_rows * row_count * block,
            bytes_accessed=8 * local_rows * row_count * block,
            transcendentals=0,
        ),
        name="prepare",
    )(place, found_inverse.reshape(2 * local_rows * row_count, block))
    term = pl.pallas_call(
        weigh_kernel,
        in_specs=[SMEM_SPEC, VMEM_SPEC, pl.BlockSpec(memory_space=pl.ANY)],
        out_specs=VMEM_SPEC,
        out_shape=jax.ShapeDtypeStruct((total_cols, slot), F32),
        compiler_params=PARAMS,
        name="weigh",
    )(pole_weights, diag_inverse[0], own[-1])
    terms = lax.all_gather(term, "pole", axis=0)

    keep_d, send_d, keep_t, send_t = pl.pallas_call(
        functools.partial(compute_kernel, (row_count, col_count), supernodes, slot),
        in_specs=[SMEM_SPEC] * 3 + [VMEM_SPEC] * (1 + row_count + col_count),
        out_specs=[VMEM_SPEC] * 4,
        out_shape=[jax.ShapeDtypeStruct((half, local_rows), F32)] * 2
        + [jax.ShapeDtypeStruct((half, slot), F32)] * 2,
        scratch_shapes=[
            pltpu.VMEM((local_rows // slot, packed_width + slot, slot), F32),
            pltpu.VMEM((local_rows // slot, packed_width + slot, slot), F32),
        ],
        compiler_params=PARAMS,
        name="compute",
    )(
        sup_widths, pole_weights, place, straight,
        *[blocks[shift] for shift in range(row_count)], *own,
    )

    tie = lax.optimization_barrier
    products, send_d = tie((keep_t + swap(send_t, "col", top), send_d))
    products = scatter_rest(products, "col")
    for bit in bits_of(row_count):
        products = products + swap(products, "row", bit)
    density = scatter_rest(keep_d + swap(send_d, "col", top), "col")
    density = sum_direct(density, "pole")
    products, density, terms = tie((products, density, terms))
    products = sum_direct(products, "pole")
    density = gather_but_last(density, "col")
    products = gather_but_last(products, "col")

    return pl.pallas_call(
        functools.partial(expand_kernel, col_count, slot),
        in_specs=[SMEM_SPEC] * 2 + [VMEM_SPEC] * 5,
        out_specs=[VMEM_SPEC] * 2,
        out_shape=[
            jax.ShapeDtypeStruct((total_cols // col_count, local_rows), F32),
            jax.ShapeDtypeStruct((total_cols, slot), F32),
        ],
        scratch_shapes=[pltpu.VMEM((local_rows // slot + 1, packed_width + slot, slot), F32)],
        compiler_params=PARAMS,
        name="expand",
    )(
        sup_widths, place, density, swap(density, "col", top),
        products, swap(products, "col", top), terms,
    )


def solution(mesh):
    in_specs = (
        P("pole", None, "row", None, "col", None),
        P("pole", None, ("row", "col"), None),
        P(("row", "col"), None),
        P(),
        P("pole", None, None, None),
        P("pole", None),
    )
    out_specs = (P("col", "row"), P())
    return jax.shard_map(
        per_device, mesh=mesh, in_specs=in_specs, out_specs=out_specs, check_vma=False
    )
```

```python
import functools

import jax
import jax.numpy as jnp
from jax import lax
from jax.experimental import pallas as pl
from jax.experimental.pallas import tpu as pltpu
from jax.sharding import PartitionSpec as P

F32 = jnp.float32
BF16 = jnp.bfloat16
VMEM_SPEC = pl.BlockSpec(memory_space=pltpu.VMEM)
SMEM_SPEC = pl.BlockSpec(memory_space=pltpu.SMEM)
PARAMS = pltpu.CompilerParams(vmem_limit_bytes=48 * 1024 * 1024)


def rows_by_rows(left, right):
    return lax.dot_general(left, right, (((1,), (1,)), ((), ())), preferred_element_type=F32)


def offsets_of(widths_ref, supernodes):
    offsets = [0]
    for k in range(supernodes):
        offsets.append(offsets[-1] + widths_ref[k])
    return offsets


def pack_kernel(supernodes, slot, pattern_ref, widths_ref, panel_ref, packed_ref):
    packed_width = packed_ref.shape[0] // 2
    offsets = offsets_of(widths_ref, supernodes)
    lane = lax.broadcasted_iota(jnp.int32, (1, slot), 1)
    place = []
    for k in range(supernodes):
        valid = (lane < widths_ref[k]) & (pattern_ref[0, k] == 1)
        place.append(jnp.where(valid, offsets[k] + lane, -1))
    place = jnp.concatenate(place, axis=1)
    target = lax.broadcasted_iota(jnp.int32, (packed_width, supernodes * slot), 0)
    select = jnp.where(target == place, 1.0, 0.0).astype(BF16)
    for part in range(2):
        packed_ref[part * packed_width:(part + 1) * packed_width, :] = rows_by_rows(
            select, panel_ref[part]
        ).astype(BF16)


def prepare_kernel(row_count, place_ref, inverse_ref, straight_ref):
    block = inverse_ref.shape[1]
    local_rows = straight_ref.shape[1]
    row_index = place_ref[0]
    group = max(8, 256 // row_count)
    span = group * row_count
    row_id = lax.broadcasted_iota(jnp.int32, (span, span), 0)
    col_id = lax.broadcasted_iota(jnp.int32, (span, span), 1)
    source = (row_id % group) * row_count + (row_id // group + row_index) % row_count
    order = jnp.where(col_id == source, 1.0, 0.0).astype(BF16)
    for part in range(2):
        for chunk in range(local_rows // group):
            base = (part * local_rows + chunk * group) * row_count
            mixed = inverse_ref[base:base + span, :]
            sorted_rows = jnp.dot(order, mixed, preferred_element_type=F32).astype(BF16)
            for owner in range(row_count):
                straight_ref[
                    part, chunk * group:(chunk + 1) * group, owner * block:(owner + 1) * block
                ] = sorted_rows[owner * group:(owner + 1) * group]


def compute_kernel(
    counts, supernodes, slot, widths_ref, weights_ref, place_ref, straight_ref, diag_ref, *refs
):
    row_count, col_count = counts
    block_refs, refs = refs[:row_count], refs[row_count:]
    own_refs, refs = refs[:col_count], refs[col_count:]
    keep_d_ref, send_d_ref, keep_t_ref, send_t_ref, term_ref, x_ref, y_ref = refs
    packed_width = block_refs[0].shape[0] // 2
    local_rows = straight_ref.shape[1]
    strips = local_rows // slot
    w_real = weights_ref[0, 0]
    w_imag = weights_ref[0, 1]
    col_index = place_ref[1]

    panel = jnp.concatenate([ref[...] for ref in block_refs], axis=1)
    with_real = rows_by_rows(panel, straight_ref[0])
    with_imag = rows_by_rows(panel, straight_ref[1])
    u_real = with_imag[packed_width:] - with_real[:packed_width]
    u_imag = -(with_real[packed_width:] + with_imag[:packed_width])
    weighted = w_real * u_real - w_imag * u_imag
    turned = w_real * u_imag + w_imag * u_real

    half = packed_width // 2
    upper = (col_index & (col_count // 2)) != 0
    keep_d_ref[...] = jnp.where(upper, weighted[half:], weighted[:half])
    send_d_ref[...] = jnp.where(upper, weighted[:half], weighted[half:])

    for ref, value in ((x_ref, weighted), (y_ref, turned)):
        for s in range(strips):
            ref[s, :packed_width] = value[:, s * slot:(s + 1) * slot]
            ref[s, packed_width:] = jnp.zeros((slot, slot), F32)

    own = [jnp.zeros((), BF16)] * col_count
    for c in range(col_count):
        block_of = own_refs[0][...]
        for other in range(1, col_count):
            block_of = jnp.where((col_index ^ c) == other, own_refs[other][...], block_of)
        own[c] = block_of
    own = jnp.concatenate(own, axis=1)
    offsets = offsets_of(widths_ref, supernodes)
    row_in_slot = lax.broadcasted_iota(jnp.int32, (slot, 1), 0)
    row_packed = lax.broadcasted_iota(jnp.int32, (packed_width, 1), 0)
    total = jnp.zeros((packed_width, slot), F32)
    for k in range(supernodes):
        valid = row_in_slot < widths_ref[k]
        x, y = (
            jnp.concatenate(
                [jnp.where(valid, ref[s, pl.ds(offsets[k], slot), :], 0.0) for s in range(strips)],
                axis=1,
            )
            for ref in (x_ref, y_ref)
        )
        x_high, y_high = x.astype(BF16), y.astype(BF16)
        x_low = (x - x_high.astype(F32)).astype(BF16)
        y_low = (y - y_high.astype(F32)).astype(BF16)
        product = (
            rows_by_rows(own[:packed_width], x_high) - rows_by_rows(own[packed_width:], y_high)
        ) + (rows_by_rows(own[:packed_width], x_low) - rows_by_rows(own[packed_width:], y_low))
        inside = (row_packed >= offsets[k]) & (row_packed < offsets[k + 1])
        total = jnp.where(inside, product, total)
    keep_t_ref[...] = jnp.where(upper, total[half:], total[:half])
    send_t_ref[...] = jnp.where(upper, total[:half], total[half:])

    folded = term_ref.shape[0]
    for s in range(strips):
        first = pl.multiple_of((col_index * strips + s) * folded, folded)
        term_ref[:, s * slot:(s + 1) * slot] = w_real * diag_ref[
            0, pl.ds(first, folded), :
        ].astype(F32) - w_imag * diag_ref[1, pl.ds(first, folded), :].astype(F32)


def expand_kernel(
    pole_count, col_count, slot, widths_ref, place_ref, mine_d_ref, other_d_ref, mine_t_ref, other_t_ref,
    density_ref, diagonal_ref, strip_ref,
):
    supernodes = diagonal_ref.shape[0] // slot
    per_col, local_rows = density_ref.shape
    strips = local_rows // slot
    folded = per_col // strips
    share = col_count // 2
    tall = mine_d_ref.shape[0] // share
    part = tall - folded
    col_index = place_ref[1]
    upper = (col_index & share) != 0
    for side in range(2):
        own_side = upper if side else jnp.logical_not(upper)
        d_value = jnp.where(own_side, mine_d_ref[...], other_d_ref[...])
        t_value = jnp.where(own_side, mine_t_ref[...], other_t_ref[...])
        for q in range(share):
            owner = side * share + q
            base = owner * part
            for s in range(strips):
                lanes = slice(s * slot, (s + 1) * slot)
                strip_ref[s, base:base + part] = d_value[q * tall:q * tall + part, lanes]
                first = (owner * strips + s) * folded
                diagonal_ref[first:first + folded] = d_value[q * tall + part:(q + 1) * tall, lanes]
            step = part // pole_count
            for j in range(pole_count):
                first = base + (place_ref[2] ^ j) * step
                if step % 8 == 0:
                    first = pl.multiple_of(first, 8)
                strip_ref[strips, pl.ds(first, step), :] = t_value[
                    q * part + j * step:q * part + (j + 1) * step
                ]
    for s in range(strips + 1):
        strip_ref[s, col_count * part:] = jnp.zeros((slot, slot), F32)
    offsets = offsets_of(widths_ref, supernodes)
    row_in_slot = lax.broadcasted_iota(jnp.int32, (slot, 1), 0)
    for k in range(supernodes):
        product = strip_ref[strips, pl.ds(offsets[k], slot), :]
        product = jnp.where(row_in_slot < widths_ref[k], product, 0.0)
        diagonal_ref[k * slot:(k + 1) * slot] = diagonal_ref[k * slot:(k + 1) * slot] - product
    size = min(per_col, slot)
    row_in_part = lax.broadcasted_iota(jnp.int32, (size, 1), 0)
    for part in range(per_col // size):
        first = col_index * per_col + part * size
        owner = first // slot
        within = first % slot
        start, count = 0, 0
        for k in range(supernodes):
            start = start + jnp.where(k < owner, widths_ref[k], 0)
            count = count + jnp.where(k == owner, widths_ref[k], 0)
        for s in range(strips):
            piece = strip_ref[s, pl.ds(start + within, size), :]
            density_ref[part * size:(part + 1) * size, s * slot:(s + 1) * slot] = jnp.where(
                row_in_part < count - within, piece, 0.0
            )


def bits_of(count):
    return [1 << k for k in range(count.bit_length() - 1)]


def swap(value, axis, bit):
    return lax.ppermute(value, axis, [(i, i ^ bit) for i in range(lax.axis_size(axis))])


def halves_of(value):
    half = value.shape[0] // 2
    return value[:half], value[half:]


def tree_sum(terms):
    while len(terms) > 1:
        terms = [terms[j] + terms[j + 1] for j in range(0, len(terms), 2)]
    return terms[0]


def scatter_sum(value, axis):
    count = lax.axis_size(axis)
    index = lax.axis_index(axis)
    shares = value.reshape(count, value.shape[0] // count, value.shape[1])
    shares = [lax.dynamic_index_in_dim(shares, index ^ j, 0, False) for j in range(count)]
    return tree_sum([shares[0]] + [swap(shares[j], axis, j) for j in range(1, count)])


def gather_direct(share, axis):
    others = [swap(share, axis, j) for j in range(1, lax.axis_size(axis))]
    return jnp.concatenate([share] + others, axis=0)


def scatter_rest(value, axis):
    index = lax.axis_index(axis)
    for bit in bits_of(lax.axis_size(axis))[:-1][::-1]:
        half = value.shape[0] // 2
        upper = (index & bit) != 0
        keep = jnp.where(upper, value[half:], value[:half])
        value = keep + swap(jnp.where(upper, value[:half], value[half:]), axis, bit)
    return value


def gather_but_last(value, axis):
    index = lax.axis_index(axis)
    for bit in bits_of(lax.axis_size(axis))[:-1]:
        other = swap(value, axis, bit)
        upper = (index & bit) != 0
        value = jnp.concatenate(
            [jnp.where(upper, other, value), jnp.where(upper, value, other)], axis=0
        )
    return value


def per_device(found_inverse, l_panel, block_pattern, sup_widths, diag_inverse, pole_weights):
    slot = diag_inverse.shape[-1]
    total_cols = l_panel.shape[-1]
    supernodes = total_cols // slot
    packed_width = slot + (supernodes - 1) * (slot // 2)
    half = packed_width // 2
    local_rows = found_inverse.shape[2]
    block = l_panel.shape[2]
    row_count = lax.axis_size("row")
    col_count = lax.axis_size("col")
    top = col_count // 2
    place = jnp.stack([lax.axis_index(axis) for axis in ("row", "col", "pole")]).astype(jnp.int32)

    packed = pl.pallas_call(
        functools.partial(pack_kernel, supernodes, slot),
        in_specs=[SMEM_SPEC, SMEM_SPEC, VMEM_SPEC],
        out_specs=VMEM_SPEC,
        out_shape=jax.ShapeDtypeStruct((2 * packed_width, block), BF16),
        name="pack",
    )(block_pattern, sup_widths, l_panel[0])

    blocks = {0: packed}
    for shift in sorted(range(1, row_count), key=lambda s: -min(s, row_count - s)):
        pairs = [((i + shift) % row_count, i) for i in range(row_count)]
        blocks[shift] = lax.ppermute(packed, "row", pairs)
    own = [packed] + [swap(packed, "col", other) for other in range(1, col_count)]

    straight = pl.pallas_call(
        functools.partial(prepare_kernel, row_count),
        in_specs=[SMEM_SPEC, VMEM_SPEC],
        out_specs=VMEM_SPEC,
        out_shape=jax.ShapeDtypeStruct((2, local_rows, row_count * block), BF16),
        compiler_params=PARAMS,
        cost_estimate=pl.CostEstimate(
            flops=4 * 256 * local_rows * row_count * block,
            bytes_accessed=8 * local_rows * row_count * block,
            transcendentals=0,
        ),
        name="prepare",
    )(place, found_inverse.reshape(2 * local_rows * row_count, block))

    keep_d, send_d, keep_t, send_t, term = pl.pallas_call(
        functools.partial(compute_kernel, (row_count, col_count), supernodes, slot),
        in_specs=[SMEM_SPEC] * 3 + [VMEM_SPEC] * (2 + row_count + col_count),
        out_specs=[VMEM_SPEC] * 5,
        out_shape=[jax.ShapeDtypeStruct((half, local_rows), F32)] * 2
        + [jax.ShapeDtypeStruct((half, slot), F32)] * 2
        + [jax.ShapeDtypeStruct((total_cols * slot // (col_count * local_rows), local_rows), F32)],
        scratch_shapes=[
            pltpu.VMEM((local_rows // slot, packed_width + slot, slot), F32),
            pltpu.VMEM((local_rows // slot, packed_width + slot, slot), F32),
        ],
        compiler_params=PARAMS,
        name="compute",
    )(
        sup_widths, pole_weights, place, straight, diag_inverse[0],
        *[blocks[shift] for shift in range(row_count)], *own,
    )

    tie = lax.optimization_barrier
    products = scatter_rest(keep_t + swap(send_t, "col", top), "col")
    density = scatter_rest(keep_d + swap(send_d, "col", top), "col")
    low, high = halves_of(jnp.concatenate([density, term], axis=0))
    products, low, high = tie((products, low, high))
    bits = bits_of(lax.axis_size("pole"))
    for step, bit in enumerate(bits):
        low, high = low + swap(low, "pole", bit), high + swap(high, "pole", bits[-1 - step])
        if step == 0:
            products = scatter_sum(products, "pole")
            products, low, high = tie((products, low, high))
    for bit in bits_of(row_count):
        products = products + swap(products, "row", bit)
    products, low, high = tie((products, low, high))
    density = jnp.concatenate([low, high], axis=0)
    products = gather_direct(products, "pole")
    density = gather_but_last(density, "col")
    products = gather_but_last(products, "col")

    return pl.pallas_call(
        functools.partial(expand_kernel, lax.axis_size("pole"), col_count, slot),
        in_specs=[SMEM_SPEC] * 2 + [VMEM_SPEC] * 4,
        out_specs=[VMEM_SPEC] * 2,
        out_shape=[
            jax.ShapeDtypeStruct((total_cols // col_count, local_rows), F32),
            jax.ShapeDtypeStruct((total_cols, slot), F32),
        ],
        scratch_shapes=[pltpu.VMEM((local_rows // slot + 1, packed_width + slot, slot), F32)],
        compiler_params=PARAMS,
        name="expand",
    )(
        sup_widths, place, density, swap(density, "col", top),
        products, swap(products, "col", top),
    )


def solution(mesh):
    in_specs = (
        P("pole", None, "row", None, "col", None),
        P("pole", None, ("row", "col"), None),
        P(("row", "col"), None),
        P(),
        P("pole", None, None, None),
        P("pole", None),
    )
    out_specs = (P("col", "row"), P())
    return jax.shard_map(
        per_device, mesh=mesh, in_specs=in_specs, out_specs=out_specs, check_vma=False
    )
```

```python
import functools

import jax
import jax.numpy as jnp
from jax import lax
from jax.experimental import pallas as pl
from jax.experimental.pallas import tpu as pltpu
from jax.sharding import PartitionSpec as P

F32 = jnp.float32
BF16 = jnp.bfloat16
VMEM_SPEC = pl.BlockSpec(memory_space=pltpu.VMEM)
SMEM_SPEC = pl.BlockSpec(memory_space=pltpu.SMEM)
PARAMS = pltpu.CompilerParams(vmem_limit_bytes=48 * 1024 * 1024)


def rows_by_rows(left, right):
    return lax.dot_general(left, right, (((1,), (1,)), ((), ())), preferred_element_type=F32)


def offsets_of(widths_ref, supernodes):
    offsets = [0]
    for k in range(supernodes):
        offsets.append(offsets[-1] + widths_ref[k])
    return offsets


def pack_kernel(supernodes, slot, pattern_ref, widths_ref, panel_ref, packed_ref):
    packed_width = packed_ref.shape[0] // 2
    offsets = offsets_of(widths_ref, supernodes)
    lane = lax.broadcasted_iota(jnp.int32, (1, slot), 1)
    place = []
    for k in range(supernodes):
        valid = (lane < widths_ref[k]) & (pattern_ref[0, k] == 1)
        place.append(jnp.where(valid, offsets[k] + lane, -1))
    place = jnp.concatenate(place, axis=1)
    target = lax.broadcasted_iota(jnp.int32, (packed_width, supernodes * slot), 0)
    select = jnp.where(target == place, 1.0, 0.0).astype(BF16)
    for part in range(2):
        packed_ref[part * packed_width:(part + 1) * packed_width, :] = rows_by_rows(
            select, panel_ref[part]
        ).astype(BF16)


def prepare_kernel(
    row_count, weights_ref, place_ref, inverse_ref, diag_ref, straight_ref, term_ref
):
    block = inverse_ref.shape[1]
    local_rows = straight_ref.shape[1]
    row_index = place_ref[0]
    group = max(8, 256 // row_count)
    span = group * row_count
    row_id = lax.broadcasted_iota(jnp.int32, (span, span), 0)
    col_id = lax.broadcasted_iota(jnp.int32, (span, span), 1)
    source = (row_id % group) * row_count + (row_id // group + row_index) % row_count
    order = jnp.where(col_id == source, 1.0, 0.0).astype(BF16)
    for part in range(2):
        for chunk in range(local_rows // group):
            base = (part * local_rows + chunk * group) * row_count
            mixed = inverse_ref[base:base + span, :]
            sorted_rows = jnp.dot(order, mixed, preferred_element_type=F32).astype(BF16)
            for owner in range(row_count):
                straight_ref[
                    part, chunk * group:(chunk + 1) * group, owner * block:(owner + 1) * block
                ] = sorted_rows[owner * group:(owner + 1) * group]
    per_col = term_ref.shape[0]
    first = pl.multiple_of(place_ref[1] * per_col, per_col)
    term_ref[...] = weights_ref[0, 0] * diag_ref[0, pl.ds(first, per_col), :].astype(
        F32
    ) - weights_ref[0, 1] * diag_ref[1, pl.ds(first, per_col), :].astype(F32)


def compute_kernel(
    counts, supernodes, slot, widths_ref, weights_ref, place_ref, straight_ref, *refs
):
    row_count, col_count = counts
    block_refs, refs = refs[:row_count], refs[row_count:]
    own_refs, refs = refs[:col_count], refs[col_count:]
    keep_d_ref, send_d_ref, keep_t_ref, send_t_ref, x_ref, y_ref = refs
    packed_width = block_refs[0].shape[0] // 2
    local_rows = straight_ref.shape[1]
    strips = local_rows // slot
    w_real = weights_ref[0, 0]
    w_imag = weights_ref[0, 1]
    col_index = place_ref[1]

    panel = jnp.concatenate([ref[...] for ref in block_refs], axis=1)
    with_real = rows_by_rows(panel, straight_ref[0])
    with_imag = rows_by_rows(panel, straight_ref[1])
    u_real = with_imag[packed_width:] - with_real[:packed_width]
    u_imag = -(with_real[packed_width:] + with_imag[:packed_width])
    weighted = w_real * u_real - w_imag * u_imag
    turned = w_real * u_imag + w_imag * u_real

    half = packed_width // 2
    upper = (col_index & (col_count // 2)) != 0
    keep_d_ref[...] = jnp.where(upper, weighted[half:], weighted[:half])
    send_d_ref[...] = jnp.where(upper, weighted[:half], weighted[half:])

    for ref, value in ((x_ref, weighted), (y_ref, turned)):
        for s in range(strips):
            ref[s, :packed_width] = value[:, s * slot:(s + 1) * slot]
            ref[s, packed_width:] = jnp.zeros((slot, slot), F32)

    own = [jnp.zeros((), BF16)] * col_count
    for c in range(col_count):
        block_of = own_refs[0][...]
        for other in range(1, col_count):
            block_of = jnp.where((col_index ^ c) == other, own_refs[other][...], block_of)
        own[c] = block_of
    own = jnp.concatenate(own, axis=1)
    offsets = offsets_of(widths_ref, supernodes)
    row_in_slot = lax.broadcasted_iota(jnp.int32, (slot, 1), 0)
    row_packed = lax.broadcasted_iota(jnp.int32, (packed_width, 1), 0)
    total = jnp.zeros((packed_width, slot), F32)
    for k in range(supernodes):
        valid = row_in_slot < widths_ref[k]
        x, y = (
            jnp.concatenate(
                [jnp.where(valid, ref[s, pl.ds(offsets[k], slot), :], 0.0) for s in range(strips)],
                axis=1,
            )
            for ref in (x_ref, y_ref)
        )
        x_high, y_high = x.astype(BF16), y.astype(BF16)
        x_low = (x - x_high.astype(F32)).astype(BF16)
        y_low = (y - y_high.astype(F32)).astype(BF16)
        product = (
            rows_by_rows(own[:packed_width], x_high) - rows_by_rows(own[packed_width:], y_high)
        ) + (rows_by_rows(own[:packed_width], x_low) - rows_by_rows(own[packed_width:], y_low))
        inside = (row_packed >= offsets[k]) & (row_packed < offsets[k + 1])
        total = jnp.where(inside, product, total)
    keep_t_ref[...] = jnp.where(upper, total[half:], total[:half])
    send_t_ref[...] = jnp.where(upper, total[:half], total[half:])


def expand_kernel(
    col_count, slot, widths_ref, place_ref, mine_d_ref, other_d_ref, mine_t_ref, other_t_ref,
    mine_term_ref, other_term_ref, density_ref, diagonal_ref, strip_ref,
):
    supernodes = diagonal_ref.shape[0] // slot
    per_col, local_rows = density_ref.shape
    strips = local_rows // slot
    share = col_count // 2
    part = mine_d_ref.shape[0] // share
    col_index = place_ref[1]
    upper = (col_index & share) != 0
    for side in range(2):
        own_side = upper if side else jnp.logical_not(upper)
        d_value = jnp.where(own_side, mine_d_ref[...], other_d_ref[...])
        t_value = jnp.where(own_side, mine_t_ref[...], other_t_ref[...])
        rows = mine_term_ref.shape[0]
        diagonal_ref[side * rows:(side + 1) * rows] = jnp.where(
            own_side, mine_term_ref[...], other_term_ref[...]
        )
        for q in range(share):
            owner = side * share + q
            base = owner * part
            for s in range(strips):
                lanes = slice(s * slot, (s + 1) * slot)
                strip_ref[s, base:base + part] = d_value[q * part:(q + 1) * part, lanes]
            strip_ref[strips, base:base + part] = t_value[q * part:(q + 1) * part]
    for s in range(strips + 1):
        strip_ref[s, col_count * part:] = jnp.zeros((slot, slot), F32)
    offsets = offsets_of(widths_ref, supernodes)
    row_in_slot = lax.broadcasted_iota(jnp.int32, (slot, 1), 0)
    for k in range(supernodes):
        product = strip_ref[strips, pl.ds(offsets[k], slot), :]
        product = jnp.where(row_in_slot < widths_ref[k], product, 0.0)
        diagonal_ref[k * slot:(k + 1) * slot] -= product
    size = min(per_col, slot)
    row_in_part = lax.broadcasted_iota(jnp.int32, (size, 1), 0)
    for part in range(per_col // size):
        first = col_index * per_col + part * size
        owner = first // slot
        within = first % slot
        start, count = 0, 0
        for k in range(supernodes):
            start = start + jnp.where(k < owner, widths_ref[k], 0)
            count = count + jnp.where(k == owner, widths_ref[k], 0)
        for s in range(strips):
            piece = strip_ref[s, pl.ds(start + within, size), :]
            density_ref[part * size:(part + 1) * size, s * slot:(s + 1) * slot] = jnp.where(
                row_in_part < count - within, piece, 0.0
            )


def bits_of(count):
    return [1 << k for k in range(count.bit_length() - 1)]


def swap(value, axis, bit):
    return lax.ppermute(value, axis, [(i, i ^ bit) for i in range(lax.axis_size(axis))])


def tree_sum(terms):
    while len(terms) > 1:
        terms = [terms[j] + terms[j + 1] for j in range(0, len(terms), 2)]
    return terms[0]


def sum_direct(value, axis):
    return tree_sum([value] + [swap(value, axis, j) for j in range(1, lax.axis_size(axis))])


def scatter_rest(value, axis):
    index = lax.axis_index(axis)
    for bit in bits_of(lax.axis_size(axis))[:-1][::-1]:
        half = value.shape[0] // 2
        upper = (index & bit) != 0
        keep = jnp.where(upper, value[half:], value[:half])
        value = keep + swap(jnp.where(upper, value[:half], value[half:]), axis, bit)
    return value


def gather_but_last(value, axis):
    index = lax.axis_index(axis)
    for bit in bits_of(lax.axis_size(axis))[:-1]:
        other = swap(value, axis, bit)
        upper = (index & bit) != 0
        value = jnp.concatenate(
            [jnp.where(upper, other, value), jnp.where(upper, value, other)], axis=0
        )
    return value


def per_device(found_inverse, l_panel, block_pattern, sup_widths, diag_inverse, pole_weights):
    slot = diag_inverse.shape[-1]
    total_cols = l_panel.shape[-1]
    supernodes = total_cols // slot
    packed_width = slot + (supernodes - 1) * (slot // 2)
    half = packed_width // 2
    local_rows = found_inverse.shape[2]
    block = l_panel.shape[2]
    row_count = lax.axis_size("row")
    col_count = lax.axis_size("col")
    top = col_count // 2
    place = jnp.stack([lax.axis_index("row"), lax.axis_index("col")]).astype(jnp.int32)

    packed = pl.pallas_call(
        functools.partial(pack_kernel, supernodes, slot),
        in_specs=[SMEM_SPEC, SMEM_SPEC, VMEM_SPEC],
        out_specs=VMEM_SPEC,
        out_shape=jax.ShapeDtypeStruct((2 * packed_width, block), BF16),
        name="pack",
    )(block_pattern, sup_widths, l_panel[0])

    blocks = {0: packed}
    for shift in sorted(range(1, row_count), key=lambda s: -min(s, row_count - s)):
        pairs = [((i + shift) % row_count, i) for i in range(row_count)]
        blocks[shift] = lax.ppermute(packed, "row", pairs)
    own = [packed] + [swap(packed, "col", other) for other in range(1, col_count)]

    straight, term = pl.pallas_call(
        functools.partial(prepare_kernel, row_count),
        in_specs=[SMEM_SPEC] * 2 + [VMEM_SPEC] * 2,
        out_specs=[VMEM_SPEC] * 2,
        out_shape=[
            jax.ShapeDtypeStruct((2, local_rows, row_count * block), BF16),
            jax.ShapeDtypeStruct((total_cols // col_count, slot), F32),
        ],
        compiler_params=PARAMS,
        cost_estimate=pl.CostEstimate(
            flops=4 * 256 * local_rows * row_count * block,
            bytes_accessed=8 * local_rows * row_count * block,
            transcendentals=0,
        ),
        name="prepare",
    )(
        pole_weights, place, found_inverse.reshape(2 * local_rows * row_count, block),
        diag_inverse[0],
    )
    first_arrival = min(blocks, key=lambda shift: (shift == 0, -min(shift, row_count - shift)))
    term, blocks[first_arrival] = lax.optimization_barrier((term, blocks[first_arrival]))
    term = sum_direct(term, "pole")

    keep_d, send_d, keep_t, send_t = pl.pallas_call(
        functools.partial(compute_kernel, (row_count, col_count), supernodes, slot),
        in_specs=[SMEM_SPEC] * 3 + [VMEM_SPEC] * (1 + row_count + col_count),
        out_specs=[VMEM_SPEC] * 4,
        out_shape=[jax.ShapeDtypeStruct((half, local_rows), F32)] * 2
        + [jax.ShapeDtypeStruct((half, slot), F32)] * 2,
        scratch_shapes=[
            pltpu.VMEM((local_rows // slot, packed_width + slot, slot), F32),
            pltpu.VMEM((local_rows // slot, packed_width + slot, slot), F32),
        ],
        compiler_params=PARAMS,
        name="compute",
    )(
        sup_widths, pole_weights, place, straight,
        *[blocks[shift] for shift in range(row_count)], *own,
    )

    tie = lax.optimization_barrier
    products, send_d, term = tie((keep_t + swap(send_t, "col", top), send_d, term))
    term = gather_but_last(term, "col")
    products = scatter_rest(products, "col")
    for bit in bits_of(row_count):
        products = products + swap(products, "row", bit)
    density = scatter_rest(keep_d + swap(send_d, "col", top), "col")
    density = sum_direct(density, "pole")
    products, density = tie((products, density))
    products = sum_direct(products, "pole")
    density = gather_but_last(density, "col")
    products = gather_but_last(products, "col")

    return pl.pallas_call(
        functools.partial(expand_kernel, col_count, slot),
        in_specs=[SMEM_SPEC] * 2 + [VMEM_SPEC] * 6,
        out_specs=[VMEM_SPEC] * 2,
        out_shape=[
            jax.ShapeDtypeStruct((total_cols // col_count, local_rows), F32),
            jax.ShapeDtypeStruct((total_cols, slot), F32),
        ],
        scratch_shapes=[pltpu.VMEM((local_rows // slot + 1, packed_width + slot, slot), F32)],
        compiler_params=PARAMS,
        name="expand",
    )(
        sup_widths, place, density, swap(density, "col", top),
        products, swap(products, "col", top), term, swap(term, "col", top),
    )


def solution(mesh):
    in_specs = (
        P("pole", None, "row", None, "col", None),
        P("pole", None, ("row", "col"), None),
        P(("row", "col"), None),
        P(),
        P("pole", None, None, None),
        P("pole", None),
    )
    out_specs = (P("col", "row"), P())
    return jax.shard_map(
        per_device, mesh=mesh, in_specs=in_specs, out_specs=out_specs, check_vma=False
    )
```

```python
import functools

import jax
import jax.numpy as jnp
from jax import lax
from jax.experimental import pallas as pl
from jax.experimental.pallas import tpu as pltpu
from jax.sharding import PartitionSpec as P

F32 = jnp.float32
BF16 = jnp.bfloat16
VMEM_SPEC = pl.BlockSpec(memory_space=pltpu.VMEM)
SMEM_SPEC = pl.BlockSpec(memory_space=pltpu.SMEM)
PARAMS = pltpu.CompilerParams(vmem_limit_bytes=48 * 1024 * 1024)


def rows_by_rows(left, right):
    return lax.dot_general(left, right, (((1,), (1,)), ((), ())), preferred_element_type=F32)


def offsets_of(widths_ref, supernodes):
    offsets = [0]
    for k in range(supernodes):
        offsets.append(offsets[-1] + widths_ref[k])
    return offsets


def pack_kernel(supernodes, slot, pattern_ref, widths_ref, panel_ref, packed_ref):
    packed_width = packed_ref.shape[0] // 2
    offsets = offsets_of(widths_ref, supernodes)
    lane = lax.broadcasted_iota(jnp.int32, (1, slot), 1)
    place = []
    for k in range(supernodes):
        valid = (lane < widths_ref[k]) & (pattern_ref[0, k] == 1)
        place.append(jnp.where(valid, offsets[k] + lane, -1))
    place = jnp.concatenate(place, axis=1)
    target = lax.broadcasted_iota(jnp.int32, (packed_width, supernodes * slot), 0)
    select = jnp.where(target == place, 1.0, 0.0).astype(BF16)
    for part in range(2):
        packed_ref[part * packed_width:(part + 1) * packed_width, :] = rows_by_rows(
            select, panel_ref[part]
        ).astype(BF16)


def prepare_kernel(
    row_count, weights_ref, place_ref, inverse_ref, diag_ref, straight_ref, term_ref
):
    block = inverse_ref.shape[1]
    local_rows = straight_ref.shape[1]
    row_index = place_ref[0]
    group = max(8, 256 // row_count)
    span = group * row_count
    row_id = lax.broadcasted_iota(jnp.int32, (span, span), 0)
    col_id = lax.broadcasted_iota(jnp.int32, (span, span), 1)
    source = (row_id % group) * row_count + (row_id // group + row_index) % row_count
    order = jnp.where(col_id == source, 1.0, 0.0).astype(BF16)
    for part in range(2):
        for chunk in range(local_rows // group):
            base = (part * local_rows + chunk * group) * row_count
            mixed = inverse_ref[base:base + span, :]
            sorted_rows = jnp.dot(order, mixed, preferred_element_type=F32).astype(BF16)
            for owner in range(row_count):
                straight_ref[
                    part, chunk * group:(chunk + 1) * group, owner * block:(owner + 1) * block
                ] = sorted_rows[owner * group:(owner + 1) * group]
    per_col = term_ref.shape[0]
    first = pl.multiple_of(place_ref[1] * per_col, per_col)
    term_ref[...] = weights_ref[0, 0] * diag_ref[0, pl.ds(first, per_col), :].astype(
        F32
    ) - weights_ref[0, 1] * diag_ref[1, pl.ds(first, per_col), :].astype(F32)


def compute_kernel(
    counts, supernodes, slot, widths_ref, weights_ref, place_ref, straight_ref, *refs
):
    row_count, col_count = counts
    block_refs, refs = refs[:row_count], refs[row_count:]
    own_refs, refs = refs[:col_count], refs[col_count:]
    keep_d_ref, send_d_ref, keep_t_ref, send_t_ref, x_ref, y_ref = refs
    packed_width = block_refs[0].shape[0] // 2
    local_rows = straight_ref.shape[1]
    strips = local_rows // slot
    w_real = weights_ref[0, 0]
    w_imag = weights_ref[0, 1]
    col_index = place_ref[1]

    panel = jnp.concatenate([ref[...] for ref in block_refs], axis=1)
    with_real = rows_by_rows(panel, straight_ref[0])
    with_imag = rows_by_rows(panel, straight_ref[1])
    u_real = with_imag[packed_width:] - with_real[:packed_width]
    u_imag = -(with_real[packed_width:] + with_imag[:packed_width])
    weighted = w_real * u_real - w_imag * u_imag
    turned = w_real * u_imag + w_imag * u_real

    half = packed_width // 2
    upper = (col_index & (col_count // 2)) != 0
    keep_d_ref[...] = jnp.where(upper, weighted[half:], weighted[:half])
    send_d_ref[...] = jnp.where(upper, weighted[:half], weighted[half:])

    for ref, value in ((x_ref, weighted), (y_ref, turned)):
        for s in range(strips):
            ref[s, :packed_width] = value[:, s * slot:(s + 1) * slot]
            ref[s, packed_width:] = jnp.zeros((slot, slot), F32)

    own = [jnp.zeros((), BF16)] * col_count
    for c in range(col_count):
        block_of = own_refs[0][...]
        for other in range(1, col_count):
            block_of = jnp.where((col_index ^ c) == other, own_refs[other][...], block_of)
        own[c] = block_of
    own = jnp.concatenate(own, axis=1)
    offsets = offsets_of(widths_ref, supernodes)
    row_in_slot = lax.broadcasted_iota(jnp.int32, (slot, 1), 0)
    row_packed = lax.broadcasted_iota(jnp.int32, (packed_width, 1), 0)
    total = jnp.zeros((packed_width, slot), F32)
    for k in range(supernodes):
        valid = row_in_slot < widths_ref[k]
        x, y = (
            jnp.concatenate(
                [jnp.where(valid, ref[s, pl.ds(offsets[k], slot), :], 0.0) for s in range(strips)],
                axis=1,
            )
            for ref in (x_ref, y_ref)
        )
        x_high, y_high = x.astype(BF16), y.astype(BF16)
        x_low = (x - x_high.astype(F32)).astype(BF16)
        y_low = (y - y_high.astype(F32)).astype(BF16)
        product = (
            rows_by_rows(own[:packed_width], x_high) - rows_by_rows(own[packed_width:], y_high)
        ) + (rows_by_rows(own[:packed_width], x_low) - rows_by_rows(own[packed_width:], y_low))
        inside = (row_packed >= offsets[k]) & (row_packed < offsets[k + 1])
        total = jnp.where(inside, product, total)
    keep_t_ref[...] = jnp.where(upper, total[half:], total[:half])
    send_t_ref[...] = jnp.where(upper, total[:half], total[half:])


def expand_kernel(
    col_count, slot, widths_ref, place_ref, mine_d_ref, other_d_ref, mine_t_ref, other_t_ref,
    mine_term_ref, other_term_ref, density_ref, diagonal_ref, strip_ref,
):
    supernodes = diagonal_ref.shape[0] // slot
    per_col, local_rows = density_ref.shape
    strips = local_rows // slot
    share = col_count // 2
    part = mine_d_ref.shape[0] // share
    col_index = place_ref[1]
    upper = (col_index & share) != 0
    for side in range(2):
        own_side = upper if side else jnp.logical_not(upper)
        d_value = jnp.where(own_side, mine_d_ref[...], other_d_ref[...])
        t_value = jnp.where(own_side, mine_t_ref[...], other_t_ref[...])
        rows = mine_term_ref.shape[0]
        diagonal_ref[side * rows:(side + 1) * rows] = jnp.where(
            own_side, mine_term_ref[...], other_term_ref[...]
        )
        for q in range(share):
            owner = side * share + q
            base = owner * part
            for s in range(strips):
                lanes = slice(s * slot, (s + 1) * slot)
                strip_ref[s, base:base + part] = d_value[q * part:(q + 1) * part, lanes]
            strip_ref[strips, base:base + part] = t_value[q * part:(q + 1) * part]
    for s in range(strips + 1):
        strip_ref[s, col_count * part:] = jnp.zeros((slot, slot), F32)
    offsets = offsets_of(widths_ref, supernodes)
    row_in_slot = lax.broadcasted_iota(jnp.int32, (slot, 1), 0)
    for k in range(supernodes):
        product = strip_ref[strips, pl.ds(offsets[k], slot), :]
        product = jnp.where(row_in_slot < widths_ref[k], product, 0.0)
        diagonal_ref[k * slot:(k + 1) * slot] -= product
    size = min(per_col, slot)
    row_in_part = lax.broadcasted_iota(jnp.int32, (size, 1), 0)
    for part in range(per_col // size):
        first = col_index * per_col + part * size
        owner = first // slot
        within = first % slot
        start, count = 0, 0
        for k in range(supernodes):
            start = start + jnp.where(k < owner, widths_ref[k], 0)
            count = count + jnp.where(k == owner, widths_ref[k], 0)
        for s in range(strips):
            piece = strip_ref[s, pl.ds(start + within, size), :]
            density_ref[part * size:(part + 1) * size, s * slot:(s + 1) * slot] = jnp.where(
                row_in_part < count - within, piece, 0.0
            )


def bits_of(count):
    return [1 << k for k in range(count.bit_length() - 1)]


def swap(value, axis, bit):
    return lax.ppermute(value, axis, [(i, i ^ bit) for i in range(lax.axis_size(axis))])


def tree_sum(terms):
    while len(terms) > 1:
        terms = [terms[j] + terms[j + 1] for j in range(0, len(terms), 2)]
    return terms[0]


def sum_direct(value, axis):
    return tree_sum([value] + [swap(value, axis, j) for j in range(1, lax.axis_size(axis))])


def scatter_rest(value, axis):
    index = lax.axis_index(axis)
    for bit in bits_of(lax.axis_size(axis))[:-1][::-1]:
        half = value.shape[0] // 2
        upper = (index & bit) != 0
        keep = jnp.where(upper, value[half:], value[:half])
        value = keep + swap(jnp.where(upper, value[:half], value[half:]), axis, bit)
    return value


def gather_but_last(value, axis):
    index = lax.axis_index(axis)
    for bit in bits_of(lax.axis_size(axis))[:-1]:
        other = swap(value, axis, bit)
        upper = (index & bit) != 0
        value = jnp.concatenate(
            [jnp.where(upper, other, value), jnp.where(upper, value, other)], axis=0
        )
    return value


def per_device(found_inverse, l_panel, block_pattern, sup_widths, diag_inverse, pole_weights):
    slot = diag_inverse.shape[-1]
    total_cols = l_panel.shape[-1]
    supernodes = total_cols // slot
    packed_width = slot + (supernodes - 1) * (slot // 2)
    half = packed_width // 2
    local_rows = found_inverse.shape[2]
    block = l_panel.shape[2]
    row_count = lax.axis_size("row")
    col_count = lax.axis_size("col")
    top = col_count // 2
    place = jnp.stack([lax.axis_index("row"), lax.axis_index("col")]).astype(jnp.int32)

    packed = pl.pallas_call(
        functools.partial(pack_kernel, supernodes, slot),
        in_specs=[SMEM_SPEC, SMEM_SPEC, VMEM_SPEC],
        out_specs=VMEM_SPEC,
        out_shape=jax.ShapeDtypeStruct((2 * packed_width, block), BF16),
        name="pack",
    )(block_pattern, sup_widths, l_panel[0])

    blocks = {0: packed}
    for shift in sorted(range(1, row_count), key=lambda s: -min(s, row_count - s)):
        pairs = [((i + shift) % row_count, i) for i in range(row_count)]
        blocks[shift] = lax.ppermute(packed, "row", pairs)
    own = [packed] + [swap(packed, "col", other) for other in range(1, col_count)]

    straight, term = pl.pallas_call(
        functools.partial(prepare_kernel, row_count),
        in_specs=[SMEM_SPEC] * 2 + [VMEM_SPEC] * 2,
        out_specs=[VMEM_SPEC] * 2,
        out_shape=[
            jax.ShapeDtypeStruct((2, local_rows, row_count * block), BF16),
            jax.ShapeDtypeStruct((total_cols // col_count, slot), F32),
        ],
        compiler_params=PARAMS,
        cost_estimate=pl.CostEstimate(
            flops=4 * 256 * local_rows * row_count * block,
            bytes_accessed=8 * local_rows * row_count * block,
            transcendentals=0,
        ),
        name="prepare",
    )(
        pole_weights, place, found_inverse.reshape(2 * local_rows * row_count, block),
        diag_inverse[0],
    )
    first_arrival = min(blocks, key=lambda shift: (shift == 0, -min(shift, row_count - shift)))
    term, blocks[first_arrival] = lax.optimization_barrier((term, blocks[first_arrival]))
    term = sum_direct(term, "pole")

    keep_d, send_d, keep_t, send_t = pl.pallas_call(
        functools.partial(compute_kernel, (row_count, col_count), supernodes, slot),
        in_specs=[SMEM_SPEC] * 3 + [VMEM_SPEC] * (1 + row_count + col_count),
        out_specs=[VMEM_SPEC] * 4,
        out_shape=[jax.ShapeDtypeStruct((half, local_rows), F32)] * 2
        + [jax.ShapeDtypeStruct((half, slot), F32)] * 2,
        scratch_shapes=[
            pltpu.VMEM((local_rows // slot, packed_width + slot, slot), F32),
            pltpu.VMEM((local_rows // slot, packed_width + slot, slot), F32),
        ],
        compiler_params=PARAMS,
        name="compute",
    )(
        sup_widths, pole_weights, place, straight,
        *[blocks[shift] for shift in range(row_count)], *own,
    )

    tie = lax.optimization_barrier
    products, send_d, term = tie((keep_t + swap(send_t, "col", top), send_d, term))
    term = gather_but_last(term, "col")
    products = scatter_rest(products, "col")
    products = sum_direct(products, "row")
    density = scatter_rest(keep_d + swap(send_d, "col", top), "col")
    density = sum_direct(density, "pole")
    products = sum_direct(products, "pole")
    density = gather_but_last(density, "col")
    products = gather_but_last(products, "col")

    return pl.pallas_call(
        functools.partial(expand_kernel, col_count, slot),
        in_specs=[SMEM_SPEC] * 2 + [VMEM_SPEC] * 6,
        out_specs=[VMEM_SPEC] * 2,
        out_shape=[
            jax.ShapeDtypeStruct((total_cols // col_count, local_rows), F32),
            jax.ShapeDtypeStruct((total_cols, slot), F32),
        ],
        scratch_shapes=[pltpu.VMEM((local_rows // slot + 1, packed_width + slot, slot), F32)],
        compiler_params=PARAMS,
        name="expand",
    )(
        sup_widths, place, density, swap(density, "col", top),
        products, swap(products, "col", top), term, swap(term, "col", top),
    )


def solution(mesh):
    in_specs = (
        P("pole", None, "row", None, "col", None),
        P("pole", None, ("row", "col"), None),
        P(("row", "col"), None),
        P(),
        P("pole", None, None, None),
        P("pole", None),
    )
    out_specs = (P("col", "row"), P())
    return jax.shard_map(
        per_device, mesh=mesh, in_specs=in_specs, out_specs=out_specs, check_vma=False
    )
```

```python
import functools

import jax
import jax.numpy as jnp
from jax import lax
from jax.experimental import pallas as pl
from jax.experimental.pallas import tpu as pltpu
from jax.sharding import PartitionSpec as P

F32 = jnp.float32
BF16 = jnp.bfloat16
VMEM_SPEC = pl.BlockSpec(memory_space=pltpu.VMEM)
SMEM_SPEC = pl.BlockSpec(memory_space=pltpu.SMEM)
PARAMS = pltpu.CompilerParams(vmem_limit_bytes=48 * 1024 * 1024)


def rows_by_rows(left, right):
    return lax.dot_general(left, right, (((1,), (1,)), ((), ())), preferred_element_type=F32)


def offsets_of(widths_ref, supernodes):
    offsets = [0]
    for k in range(supernodes):
        offsets.append(offsets[-1] + widths_ref[k])
    return offsets


def pack_kernel(supernodes, slot, pattern_ref, widths_ref, panel_ref, packed_ref):
    packed_width = packed_ref.shape[0] // 2
    offsets = offsets_of(widths_ref, supernodes)
    lane = lax.broadcasted_iota(jnp.int32, (1, slot), 1)
    place = []
    for k in range(supernodes):
        valid = (lane < widths_ref[k]) & (pattern_ref[0, k] == 1)
        place.append(jnp.where(valid, offsets[k] + lane, -1))
    place = jnp.concatenate(place, axis=1)
    target = lax.broadcasted_iota(jnp.int32, (packed_width, supernodes * slot), 0)
    select = jnp.where(target == place, 1.0, 0.0).astype(BF16)
    for part in range(2):
        packed_ref[part * packed_width:(part + 1) * packed_width, :] = rows_by_rows(
            select, panel_ref[part]
        ).astype(BF16)


def prepare_kernel(
    row_count, weights_ref, place_ref, inverse_ref, diag_ref, straight_ref, term_ref
):
    block = inverse_ref.shape[1]
    local_rows = straight_ref.shape[1]
    row_index = place_ref[0]
    group = max(8, 256 // row_count)
    span = group * row_count
    row_id = lax.broadcasted_iota(jnp.int32, (span, span), 0)
    col_id = lax.broadcasted_iota(jnp.int32, (span, span), 1)
    source = (row_id % group) * row_count + (row_id // group + row_index) % row_count
    order = jnp.where(col_id == source, 1.0, 0.0).astype(BF16)
    for part in range(2):
        for chunk in range(local_rows // group):
            base = (part * local_rows + chunk * group) * row_count
            mixed = inverse_ref[base:base + span, :]
            sorted_rows = jnp.dot(order, mixed, preferred_element_type=F32).astype(BF16)
            for owner in range(row_count):
                straight_ref[
                    part, chunk * group:(chunk + 1) * group, owner * block:(owner + 1) * block
                ] = sorted_rows[owner * group:(owner + 1) * group]
    per_col = term_ref.shape[0]
    first = pl.multiple_of(place_ref[1] * per_col, per_col)
    term_ref[...] = weights_ref[0, 0] * diag_ref[0, pl.ds(first, per_col), :].astype(
        F32
    ) - weights_ref[0, 1] * diag_ref[1, pl.ds(first, per_col), :].astype(F32)


def compute_kernel(
    counts, supernodes, slot, widths_ref, weights_ref, place_ref, straight_ref, *refs
):
    row_count, col_count = counts
    block_refs, refs = refs[:row_count], refs[row_count:]
    own_refs, refs = refs[:col_count], refs[col_count:]
    keep_d_ref, send_d_ref, keep_t_ref, send_t_ref, x_ref, y_ref = refs
    packed_width = block_refs[0].shape[0] // 2
    local_rows = straight_ref.shape[1]
    strips = local_rows // slot
    w_real = weights_ref[0, 0]
    w_imag = weights_ref[0, 1]
    col_index = place_ref[1]

    panel = jnp.concatenate([ref[...] for ref in block_refs], axis=1)
    with_real = rows_by_rows(panel, straight_ref[0])
    with_imag = rows_by_rows(panel, straight_ref[1])
    u_real = with_imag[packed_width:] - with_real[:packed_width]
    u_imag = -(with_real[packed_width:] + with_imag[:packed_width])
    weighted = w_real * u_real - w_imag * u_imag
    turned = w_real * u_imag + w_imag * u_real

    half = packed_width // 2
    upper = (col_index & (col_count // 2)) != 0
    keep_d_ref[...] = jnp.where(upper, weighted[half:], weighted[:half])
    send_d_ref[...] = jnp.where(upper, weighted[:half], weighted[half:])

    for ref, value in ((x_ref, weighted), (y_ref, turned)):
        for s in range(strips):
            ref[s, :packed_width] = value[:, s * slot:(s + 1) * slot]
            ref[s, packed_width:] = jnp.zeros((slot, slot), F32)

    own = [jnp.zeros((), BF16)] * col_count
    for c in range(col_count):
        block_of = own_refs[0][...]
        for other in range(1, col_count):
            block_of = jnp.where((col_index ^ c) == other, own_refs[other][...], block_of)
        own[c] = block_of
    own = jnp.concatenate(own, axis=1)
    offsets = offsets_of(widths_ref, supernodes)
    row_in_slot = lax.broadcasted_iota(jnp.int32, (slot, 1), 0)
    row_packed = lax.broadcasted_iota(jnp.int32, (packed_width, 1), 0)
    total = jnp.zeros((packed_width, slot), F32)
    for k in range(supernodes):
        valid = row_in_slot < widths_ref[k]
        x, y = (
            jnp.concatenate(
                [jnp.where(valid, ref[s, pl.ds(offsets[k], slot), :], 0.0) for s in range(strips)],
                axis=1,
            )
            for ref in (x_ref, y_ref)
        )
        x_high, y_high = x.astype(BF16), y.astype(BF16)
        x_low = (x - x_high.astype(F32)).astype(BF16)
        y_low = (y - y_high.astype(F32)).astype(BF16)
        product = (
            rows_by_rows(own[:packed_width], x_high) - rows_by_rows(own[packed_width:], y_high)
        ) + (rows_by_rows(own[:packed_width], x_low) - rows_by_rows(own[packed_width:], y_low))
        inside = (row_packed >= offsets[k]) & (row_packed < offsets[k + 1])
        total = jnp.where(inside, product, total)
    keep_t_ref[...] = jnp.where(upper, total[half:], total[:half])
    send_t_ref[...] = jnp.where(upper, total[:half], total[half:])


def fill_strips(strip_ref, mine_ref, other_ref, col_count, slot, upper):
    half, width = mine_ref.shape
    for side in range(2):
        value = jnp.where(upper if side else jnp.logical_not(upper), mine_ref[...], other_ref[...])
        for s in range(width // slot):
            strip_ref[s, side * half:(side + 1) * half] = value[:, s * slot:(s + 1) * slot]
    for s in range(width // slot):
        strip_ref[s, 2 * half:] = jnp.zeros((slot, slot), F32)


def density_kernel(
    col_count, slot, widths_ref, place_ref, mine_ref, other_ref, density_ref, strip_ref
):
    per_col, local_rows = density_ref.shape
    supernodes = per_col * col_count // slot
    col_index = place_ref[1]
    upper = (col_index & (col_count // 2)) != 0
    fill_strips(strip_ref, mine_ref, other_ref, col_count, slot, upper)
    size = min(per_col, slot)
    row_in_part = lax.broadcasted_iota(jnp.int32, (size, 1), 0)
    for part in range(per_col // size):
        first = col_index * per_col + part * size
        owner = first // slot
        within = first % slot
        start, count = 0, 0
        for k in range(supernodes):
            start = start + jnp.where(k < owner, widths_ref[k], 0)
            count = count + jnp.where(k == owner, widths_ref[k], 0)
        for s in range(local_rows // slot):
            piece = strip_ref[s, pl.ds(start + within, size), :]
            density_ref[part * size:(part + 1) * size, s * slot:(s + 1) * slot] = jnp.where(
                row_in_part < count - within, piece, 0.0
            )


def diagonal_kernel(
    col_count, slot, widths_ref, place_ref, mine_ref, other_ref, mine_term_ref, other_term_ref,
    diagonal_ref, strip_ref,
):
    supernodes = diagonal_ref.shape[0] // slot
    upper = (place_ref[1] & (col_count // 2)) != 0
    fill_strips(strip_ref, mine_ref, other_ref, col_count, slot, upper)
    rows = mine_term_ref.shape[0]
    for side in range(2):
        diagonal_ref[side * rows:(side + 1) * rows] = jnp.where(
            upper if side else jnp.logical_not(upper), mine_term_ref[...], other_term_ref[...]
        )
    offsets = offsets_of(widths_ref, supernodes)
    row_in_slot = lax.broadcasted_iota(jnp.int32, (slot, 1), 0)
    for k in range(supernodes):
        product = strip_ref[0, pl.ds(offsets[k], slot), :]
        product = jnp.where(row_in_slot < widths_ref[k], product, 0.0)
        diagonal_ref[k * slot:(k + 1) * slot] -= product


def bits_of(count):
    return [1 << k for k in range(count.bit_length() - 1)]


def swap(value, axis, bit):
    return lax.ppermute(value, axis, [(i, i ^ bit) for i in range(lax.axis_size(axis))])


def tree_sum(terms):
    while len(terms) > 1:
        terms = [terms[j] + terms[j + 1] for j in range(0, len(terms), 2)]
    return terms[0]


def sum_direct(value, axis):
    return tree_sum([value] + [swap(value, axis, j) for j in range(1, lax.axis_size(axis))])


def scatter_rest(value, axis):
    index = lax.axis_index(axis)
    for bit in bits_of(lax.axis_size(axis))[:-1][::-1]:
        half = value.shape[0] // 2
        upper = (index & bit) != 0
        keep = jnp.where(upper, value[half:], value[:half])
        value = keep + swap(jnp.where(upper, value[:half], value[half:]), axis, bit)
    return value


def gather_but_last(value, axis):
    index = lax.axis_index(axis)
    for bit in bits_of(lax.axis_size(axis))[:-1]:
        other = swap(value, axis, bit)
        upper = (index & bit) != 0
        value = jnp.concatenate(
            [jnp.where(upper, other, value), jnp.where(upper, value, other)], axis=0
        )
    return value


def per_device(found_inverse, l_panel, block_pattern, sup_widths, diag_inverse, pole_weights):
    slot = diag_inverse.shape[-1]
    total_cols = l_panel.shape[-1]
    supernodes = total_cols // slot
    packed_width = slot + (supernodes - 1) * (slot // 2)
    half = packed_width // 2
    local_rows = found_inverse.shape[2]
    block = l_panel.shape[2]
    row_count = lax.axis_size("row")
    col_count = lax.axis_size("col")
    top = col_count // 2
    place = jnp.stack([lax.axis_index("row"), lax.axis_index("col")]).astype(jnp.int32)

    packed = pl.pallas_call(
        functools.partial(pack_kernel, supernodes, slot),
        in_specs=[SMEM_SPEC, SMEM_SPEC, VMEM_SPEC],
        out_specs=VMEM_SPEC,
        out_shape=jax.ShapeDtypeStruct((2 * packed_width, block), BF16),
        name="pack",
    )(block_pattern, sup_widths, l_panel[0])

    blocks = {0: packed}
    for shift in sorted(range(1, row_count), key=lambda s: -min(s, row_count - s)):
        pairs = [((i + shift) % row_count, i) for i in range(row_count)]
        blocks[shift] = lax.ppermute(packed, "row", pairs)
    own = [packed] + [swap(packed, "col", other) for other in range(1, col_count)]

    straight, term = pl.pallas_call(
        functools.partial(prepare_kernel, row_count),
        in_specs=[SMEM_SPEC] * 2 + [VMEM_SPEC] * 2,
        out_specs=[VMEM_SPEC] * 2,
        out_shape=[
            jax.ShapeDtypeStruct((2, local_rows, row_count * block), BF16),
            jax.ShapeDtypeStruct((total_cols // col_count, slot), F32),
        ],
        compiler_params=PARAMS,
        cost_estimate=pl.CostEstimate(
            flops=4 * 256 * local_rows * row_count * block,
            bytes_accessed=8 * local_rows * row_count * block,
            transcendentals=0,
        ),
        name="prepare",
    )(
        pole_weights, place, found_inverse.reshape(2 * local_rows * row_count, block),
        diag_inverse[0],
    )
    first_arrival = min(blocks, key=lambda shift: (shift == 0, -min(shift, row_count - shift)))
    term, blocks[first_arrival] = lax.optimization_barrier((term, blocks[first_arrival]))
    term = sum_direct(term, "pole")

    keep_d, send_d, keep_t, send_t = pl.pallas_call(
        functools.partial(compute_kernel, (row_count, col_count), supernodes, slot),
        in_specs=[SMEM_SPEC] * 3 + [VMEM_SPEC] * (1 + row_count + col_count),
        out_specs=[VMEM_SPEC] * 4,
        out_shape=[jax.ShapeDtypeStruct((half, local_rows), F32)] * 2
        + [jax.ShapeDtypeStruct((half, slot), F32)] * 2,
        scratch_shapes=[
            pltpu.VMEM((local_rows // slot, packed_width + slot, slot), F32),
            pltpu.VMEM((local_rows // slot, packed_width + slot, slot), F32),
        ],
        compiler_params=PARAMS,
        name="compute",
    )(
        sup_widths, pole_weights, place, straight,
        *[blocks[shift] for shift in range(row_count)], *own,
    )

    tie = lax.optimization_barrier
    products, send_d, term = tie((keep_t + swap(send_t, "col", top), send_d, term))
    products = scatter_rest(products, "col")
    density = scatter_rest(keep_d + swap(send_d, "col", top), "col")
    for bit in bits_of(row_count):
        products = products + swap(products, "row", bit)
    bits = bits_of(lax.axis_size("pole"))
    for step, bit in enumerate(bits):
        density = density + swap(density, "pole", bit)
        if step < len(bits) - 1:
            density, _ = tie((density, products))
            products = products + swap(products, "pole", bit)
    products, density = tie((products, density))
    density = gather_but_last(density, "col")
    grown = [pltpu.VMEM((count, packed_width + slot, slot), F32) for count in (local_rows // slot, 1)]
    density = pl.pallas_call(
        functools.partial(density_kernel, col_count, slot),
        in_specs=[SMEM_SPEC] * 2 + [VMEM_SPEC] * 2,
        out_specs=VMEM_SPEC,
        out_shape=jax.ShapeDtypeStruct((total_cols // col_count, local_rows), F32),
        scratch_shapes=[grown[0]],
        compiler_params=PARAMS,
        cost_estimate=pl.CostEstimate(
            flops=0, bytes_accessed=16 * total_cols * local_rows, transcendentals=0
        ),
        name="expand_density",
    )(sup_widths, place, density, swap(density, "col", top))
    density, arrived = tie((density, swap(products, "pole", bits[-1])))
    products = gather_but_last(products + arrived, "col")
    term = gather_but_last(term, "col")
    diagonal = pl.pallas_call(
        functools.partial(diagonal_kernel, col_count, slot),
        in_specs=[SMEM_SPEC] * 2 + [VMEM_SPEC] * 4,
        out_specs=VMEM_SPEC,
        out_shape=jax.ShapeDtypeStruct((total_cols, slot), F32),
        scratch_shapes=[grown[1]],
        compiler_params=PARAMS,
        name="expand_diagonal",
    )(
        sup_widths, place, products, swap(products, "col", top), term, swap(term, "col", top)
    )
    return (density, diagonal)


def solution(mesh):
    in_specs = (
        P("pole", None, "row", None, "col", None),
        P("pole", None, ("row", "col"), None),
        P(("row", "col"), None),
        P(),
        P("pole", None, None, None),
        P("pole", None),
    )
    out_specs = (P("col", "row"), P())
    return jax.shard_map(
        per_device, mesh=mesh, in_specs=in_specs, out_specs=out_specs, check_vma=False
    )
```

```python
import functools

import jax
import jax.numpy as jnp
from jax import lax
from jax.experimental import pallas as pl
from jax.experimental.pallas import tpu as pltpu
from jax.sharding import PartitionSpec as P

F32 = jnp.float32
BF16 = jnp.bfloat16
VMEM_SPEC = pl.BlockSpec(memory_space=pltpu.VMEM)
SMEM_SPEC = pl.BlockSpec(memory_space=pltpu.SMEM)
PARAMS = pltpu.CompilerParams(vmem_limit_bytes=48 * 1024 * 1024)


def rows_by_rows(left, right):
    return lax.dot_general(left, right, (((1,), (1,)), ((), ())), preferred_element_type=F32)


def offsets_of(widths_ref, supernodes):
    offsets = [0]
    for k in range(supernodes):
        offsets.append(offsets[-1] + widths_ref[k])
    return offsets


def pack_kernel(
    supernodes, slot, pattern_ref, widths_ref, panel_ref, packed_ref, held_ref, arrived
):
    packed_width = packed_ref.shape[0] // 2
    copies = [
        pltpu.make_async_copy(panel_ref.at[part], held_ref.at[part], arrived.at[part])
        for part in range(2)
    ]
    for copy in copies:
        copy.start()
    offsets = offsets_of(widths_ref, supernodes)
    lane = lax.broadcasted_iota(jnp.int32, (1, slot), 1)
    place = []
    for k in range(supernodes):
        valid = (lane < widths_ref[k]) & (pattern_ref[0, k] == 1)
        place.append(jnp.where(valid, offsets[k] + lane, -1))
    place = jnp.concatenate(place, axis=1)
    target = lax.broadcasted_iota(jnp.int32, (packed_width, supernodes * slot), 0)
    select = jnp.where(target == place, 1.0, 0.0).astype(BF16)
    for part in range(2):
        copies[part].wait()
        packed_ref[part * packed_width:(part + 1) * packed_width, :] = rows_by_rows(
            select, held_ref[part]
        ).astype(BF16)


def prepare_kernel(
    counts, widths_ref, weights_ref, place_ref, inverse_ref, diag_ref, *refs
):
    row_count, col_count = counts
    own_refs, (straight_ref, own_wide_ref, term_ref) = refs[:col_count], refs[col_count:]
    packed_width = own_refs[0].shape[0] // 2
    col_index = place_ref[1]
    block = inverse_ref.shape[1]
    local_rows = straight_ref.shape[1]
    row_index = place_ref[0]
    group = max(8, 256 // row_count)
    span = group * row_count
    row_id = lax.broadcasted_iota(jnp.int32, (span, span), 0)
    col_id = lax.broadcasted_iota(jnp.int32, (span, span), 1)
    source = (row_id % group) * row_count + (row_id // group + row_index) % row_count
    order = jnp.where(col_id == source, 1.0, 0.0).astype(BF16)
    for part in range(2):
        for chunk in range(local_rows // group):
            base = (part * local_rows + chunk * group) * row_count
            mixed = inverse_ref[base:base + span, :]
            sorted_rows = jnp.dot(order, mixed, preferred_element_type=F32).astype(BF16)
            for owner in range(row_count):
                straight_ref[
                    part, chunk * group:(chunk + 1) * group, owner * block:(owner + 1) * block
                ] = sorted_rows[owner * group:(owner + 1) * group]
    own = []
    for c in range(col_count):
        block_of = own_refs[0][...]
        for other in range(1, col_count):
            block_of = jnp.where((col_index ^ c) == other, own_refs[other][...], block_of)
        own.append(block_of)
    own = jnp.concatenate(own, axis=1)
    total_cols = own_wide_ref.shape[0]
    slot = diag_ref.shape[2]
    offsets = offsets_of(widths_ref, total_cols // slot)
    row_in_slot = lax.broadcasted_iota(jnp.int32, (slot, packed_width), 0)
    column = lax.broadcasted_iota(jnp.int32, (slot, packed_width), 1)
    for k in range(total_cols // slot):
        chosen = (column == row_in_slot + offsets[k]) & (row_in_slot < widths_ref[k])
        chosen = jnp.where(chosen, 1.0, 0.0).astype(BF16)
        for part, sign in enumerate((1.0, -1.0)):
            rows = own[part * packed_width:(part + 1) * packed_width]
            own_wide_ref[k * slot:(k + 1) * slot, part * local_rows:(part + 1) * local_rows] = (
                sign * jnp.dot(chosen, rows, preferred_element_type=F32)
            ).astype(BF16)
    per_col = term_ref.shape[0]
    first = pl.multiple_of(col_index * per_col, per_col)
    term_ref[...] = weights_ref[0, 0] * diag_ref[0, pl.ds(first, per_col), :].astype(
        F32
    ) - weights_ref[0, 1] * diag_ref[1, pl.ds(first, per_col), :].astype(F32)


def compute_kernel(
    col_count, supernodes, slot, widths_ref, weights_ref, place_ref, straight_ref, own_wide_ref,
    *refs
):
    block_refs, refs = refs[:-7], refs[-7:]
    keep_d_ref, send_d_ref, keep_t_ref, send_t_ref, x_ref, y_ref, t_ref = refs
    packed_width = block_refs[0].shape[0] // 2
    local_rows = straight_ref.shape[1]
    strips = local_rows // slot
    w_real = weights_ref[0, 0]
    w_imag = weights_ref[0, 1]
    col_index = place_ref[1]

    panel = jnp.concatenate([ref[...] for ref in block_refs], axis=1)
    with_real = rows_by_rows(panel, straight_ref[0])
    with_imag = rows_by_rows(panel, straight_ref[1])
    u_real = with_imag[packed_width:] - with_real[:packed_width]
    u_imag = -(with_real[packed_width:] + with_imag[:packed_width])
    weighted = w_real * u_real - w_imag * u_imag
    turned = w_real * u_imag + w_imag * u_real

    half = packed_width // 2
    upper = (col_index & (col_count // 2)) != 0
    keep_d_ref[...] = jnp.where(upper, weighted[half:], weighted[:half])
    send_d_ref[...] = jnp.where(upper, weighted[:half], weighted[half:])

    for ref, value in ((x_ref, weighted), (y_ref, turned)):
        for s in range(strips):
            ref[s, :packed_width] = value[:, s * slot:(s + 1) * slot]
            ref[s, packed_width:] = jnp.zeros((slot, slot), F32)

    offsets = offsets_of(widths_ref, supernodes)
    for k in range(supernodes):
        right = jnp.concatenate(
            [ref[s, pl.ds(offsets[k], slot), :] for ref in (x_ref, y_ref) for s in range(strips)],
            axis=1,
        )
        high = right.astype(BF16)
        low = (right - high.astype(F32)).astype(BF16)
        product = rows_by_rows(
            own_wide_ref[k * slot:(k + 1) * slot, :], jnp.concatenate([high, low], axis=0)
        )
        t_ref[pl.ds(offsets[k], slot), :] = product[:, :slot] + product[:, slot:]
    keep_t_ref[...] = jnp.where(upper, t_ref[half:2 * half], t_ref[:half])
    send_t_ref[...] = jnp.where(upper, t_ref[:half], t_ref[half:2 * half])


def expand_kernel(
    col_count, slot, widths_ref, place_ref, mine_d_ref, other_d_ref, mine_t_ref, other_t_ref,
    mine_term_ref, other_term_ref, density_ref, diagonal_ref, strip_ref,
):
    supernodes = diagonal_ref.shape[0] // slot
    per_col, local_rows = density_ref.shape
    strips = local_rows // slot
    share = col_count // 2
    part = mine_d_ref.shape[0] // share
    col_index = place_ref[1]
    upper = (col_index & share) != 0
    for side in range(2):
        own_side = upper if side else jnp.logical_not(upper)
        d_value = jnp.where(own_side, mine_d_ref[...], other_d_ref[...])
        t_value = jnp.where(own_side, mine_t_ref[...], other_t_ref[...])
        rows = mine_term_ref.shape[0]
        diagonal_ref[side * rows:(side + 1) * rows] = jnp.where(
            own_side, mine_term_ref[...], other_term_ref[...]
        )
        for q in range(share):
            owner = side * share + q
            base = owner * part
            for s in range(strips):
                lanes = slice(s * slot, (s + 1) * slot)
                strip_ref[s, base:base + part] = d_value[q * part:(q + 1) * part, lanes]
            strip_ref[strips, base:base + part] = t_value[q * part:(q + 1) * part]
    for s in range(strips + 1):
        strip_ref[s, col_count * part:] = jnp.zeros((slot, slot), F32)
    offsets = offsets_of(widths_ref, supernodes)
    lane = lax.broadcasted_iota(jnp.int32, (1, slot), 1)
    row_in_slot = lax.broadcasted_iota(jnp.int32, (slot, 1), 0)
    for k in range(supernodes):
        product = strip_ref[strips, pl.ds(offsets[k], slot), :]
        valid = (row_in_slot < widths_ref[k]) & (lane < widths_ref[k])
        product = jnp.where(valid, product, 0.0)
        diagonal_ref[k * slot:(k + 1) * slot] -= product
    size = min(per_col, slot)
    row_in_part = lax.broadcasted_iota(jnp.int32, (size, 1), 0)
    for part in range(per_col // size):
        first = col_index * per_col + part * size
        owner = first // slot
        within = first % slot
        start, count = 0, 0
        for k in range(supernodes):
            start = start + jnp.where(k < owner, widths_ref[k], 0)
            count = count + jnp.where(k == owner, widths_ref[k], 0)
        for s in range(strips):
            piece = strip_ref[s, pl.ds(start + within, size), :]
            density_ref[part * size:(part + 1) * size, s * slot:(s + 1) * slot] = jnp.where(
                row_in_part < count - within, piece, 0.0
            )


def bits_of(count):
    return [1 << k for k in range(count.bit_length() - 1)]


def swap(value, axis, bit):
    return lax.ppermute(value, axis, [(i, i ^ bit) for i in range(lax.axis_size(axis))])


def tree_sum(terms):
    while len(terms) > 1:
        terms = [terms[j] + terms[j + 1] for j in range(0, len(terms), 2)]
    return terms[0]


def sum_direct(value, axis):
    return tree_sum([value] + [swap(value, axis, j) for j in range(1, lax.axis_size(axis))])


def scatter_rest(value, axis):
    index = lax.axis_index(axis)
    for bit in bits_of(lax.axis_size(axis))[:-1][::-1]:
        half = value.shape[0] // 2
        upper = (index & bit) != 0
        keep = jnp.where(upper, value[half:], value[:half])
        value = keep + swap(jnp.where(upper, value[:half], value[half:]), axis, bit)
    return value


def gather_but_last(value, axis):
    index = lax.axis_index(axis)
    for bit in bits_of(lax.axis_size(axis))[:-1]:
        other = swap(value, axis, bit)
        upper = (index & bit) != 0
        value = jnp.concatenate(
            [jnp.where(upper, other, value), jnp.where(upper, value, other)], axis=0
        )
    return value


def per_device(found_inverse, l_panel, block_pattern, sup_widths, diag_inverse, pole_weights):
    slot = diag_inverse.shape[-1]
    total_cols = l_panel.shape[-1]
    supernodes = total_cols // slot
    packed_width = slot + (supernodes - 1) * (slot // 2)
    half = packed_width // 2
    local_rows = found_inverse.shape[2]
    block = l_panel.shape[2]
    row_count = lax.axis_size("row")
    col_count = lax.axis_size("col")
    top = col_count // 2
    place = jnp.stack([lax.axis_index("row"), lax.axis_index("col")]).astype(jnp.int32)

    packed = pl.pallas_call(
        functools.partial(pack_kernel, supernodes, slot),
        in_specs=[SMEM_SPEC, SMEM_SPEC, pl.BlockSpec(memory_space=pl.ANY)],
        out_specs=VMEM_SPEC,
        out_shape=jax.ShapeDtypeStruct((2 * packed_width, block), BF16),
        scratch_shapes=[
            pltpu.VMEM((2, block, total_cols), BF16), pltpu.SemaphoreType.DMA((2,))
        ],
        name="pack",
    )(block_pattern, sup_widths, l_panel[0])

    blocks = {0: packed}
    for shift in sorted(range(1, row_count), key=lambda s: -min(s, row_count - s)):
        pairs = [((i + shift) % row_count, i) for i in range(row_count)]
        blocks[shift] = lax.ppermute(packed, "row", pairs)
    own = [packed] + [swap(packed, "col", other) for other in range(1, col_count)]

    straight, own_wide, term = pl.pallas_call(
        functools.partial(prepare_kernel, (row_count, col_count)),
        in_specs=[SMEM_SPEC] * 3 + [VMEM_SPEC] * (2 + col_count),
        out_specs=[VMEM_SPEC] * 3,
        out_shape=[
            jax.ShapeDtypeStruct((2, local_rows, row_count * block), BF16),
            jax.ShapeDtypeStruct((total_cols, 2 * local_rows), BF16),
            jax.ShapeDtypeStruct((total_cols // col_count, slot), F32),
        ],
        compiler_params=PARAMS,
        cost_estimate=pl.CostEstimate(
            flops=4 * 256 * local_rows * row_count * block,
            bytes_accessed=8 * local_rows * row_count * block,
            transcendentals=0,
        ),
        name="prepare",
    )(
        sup_widths, pole_weights, place,
        found_inverse.reshape(2 * local_rows * row_count, block), diag_inverse[0], *own,
    )
    first_arrival = min(blocks, key=lambda shift: (shift == 0, -min(shift, row_count - shift)))
    term, blocks[first_arrival] = lax.optimization_barrier((term, blocks[first_arrival]))
    term = sum_direct(term, "pole")

    keep_d, send_d, keep_t, send_t = pl.pallas_call(
        functools.partial(compute_kernel, col_count, supernodes, slot),
        in_specs=[SMEM_SPEC] * 3 + [VMEM_SPEC] * (2 + row_count),
        out_specs=[VMEM_SPEC] * 4,
        out_shape=[jax.ShapeDtypeStruct((half, local_rows), F32)] * 2
        + [jax.ShapeDtypeStruct((half, slot), F32)] * 2,
        scratch_shapes=[
            pltpu.VMEM((local_rows // slot, packed_width + slot, slot), F32),
            pltpu.VMEM((local_rows // slot, packed_width + slot, slot), F32),
            pltpu.VMEM((packed_width + slot, slot), F32),
        ],
        compiler_params=PARAMS,
        name="compute",
    )(
        sup_widths, pole_weights, place, straight, own_wide,
        *[blocks[shift] for shift in range(row_count)],
    )

    tie = lax.optimization_barrier
    products, send_d, term = tie((keep_t + swap(send_t, "col", top), send_d, term))
    term = gather_but_last(term, "col")
    products = scatter_rest(products, "col")
    for bit in bits_of(row_count):
        products = products + swap(products, "row", bit)
    density = scatter_rest(keep_d + swap(send_d, "col", top), "col")
    density = sum_direct(density, "pole")
    products, density = tie((products, density))
    products = sum_direct(products, "pole")
    density = gather_but_last(density, "col")
    products = gather_but_last(products, "col")

    return pl.pallas_call(
        functools.partial(expand_kernel, col_count, slot),
        in_specs=[SMEM_SPEC] * 2 + [VMEM_SPEC] * 6,
        out_specs=[VMEM_SPEC] * 2,
        out_shape=[
            jax.ShapeDtypeStruct((total_cols // col_count, local_rows), F32),
            jax.ShapeDtypeStruct((total_cols, slot), F32),
        ],
        scratch_shapes=[pltpu.VMEM((local_rows // slot + 1, packed_width + slot, slot), F32)],
        compiler_params=PARAMS,
        name="expand",
    )(
        sup_widths, place, density, swap(density, "col", top),
        products, swap(products, "col", top), term, swap(term, "col", top),
    )


def solution(mesh):
    in_specs = (
        P("pole", None, "row", None, "col", None),
        P("pole", None, ("row", "col"), None),
        P(("row", "col"), None),
        P(),
        P("pole", None, None, None),
        P("pole", None),
    )
    out_specs = (P("col", "row"), P())
    return jax.shard_map(
        per_device, mesh=mesh, in_specs=in_specs, out_specs=out_specs, check_vma=False
    )
```

```python
import functools

import jax
import jax.numpy as jnp
from jax import lax
from jax.experimental import pallas as pl
from jax.experimental.pallas import tpu as pltpu
from jax.sharding import PartitionSpec as P

F32 = jnp.float32
BF16 = jnp.bfloat16
VMEM_SPEC = pl.BlockSpec(memory_space=pltpu.VMEM)
SMEM_SPEC = pl.BlockSpec(memory_space=pltpu.SMEM)
PARAMS = pltpu.CompilerParams(vmem_limit_bytes=48 * 1024 * 1024)


def rows_by_rows(left, right):
    return lax.dot_general(left, right, (((1,), (1,)), ((), ())), preferred_element_type=F32)


def offsets_of(widths_ref, supernodes):
    offsets = [0]
    for k in range(supernodes):
        offsets.append(offsets[-1] + widths_ref[k])
    return offsets


def pack_kernel(supernodes, slot, pattern_ref, widths_ref, panel_ref, packed_ref):
    packed_width = packed_ref.shape[0] // 2
    offsets = offsets_of(widths_ref, supernodes)
    lane = lax.broadcasted_iota(jnp.int32, (1, slot), 1)
    place = []
    for k in range(supernodes):
        valid = (lane < widths_ref[k]) & (pattern_ref[0, k] == 1)
        place.append(jnp.where(valid, offsets[k] + lane, -1))
    place = jnp.concatenate(place, axis=1)
    target = lax.broadcasted_iota(jnp.int32, (packed_width, supernodes * slot), 0)
    select = jnp.where(target == place, 1.0, 0.0).astype(BF16)
    for part in range(2):
        packed_ref[part * packed_width:(part + 1) * packed_width, :] = rows_by_rows(
            select, panel_ref[part]
        ).astype(BF16)


def prepare_kernel(
    counts, widths_ref, weights_ref, place_ref, inverse_ref, diag_ref, *refs
):
    row_count, col_count = counts
    own_refs, (straight_ref, own_wide_ref, term_ref) = refs[:col_count], refs[col_count:]
    packed_width = own_refs[0].shape[0] // 2
    col_index = place_ref[1]
    block = inverse_ref.shape[1]
    local_rows = straight_ref.shape[1]
    row_index = place_ref[0]
    group = max(8, 256 // row_count)
    span = group * row_count
    row_id = lax.broadcasted_iota(jnp.int32, (span, span), 0)
    col_id = lax.broadcasted_iota(jnp.int32, (span, span), 1)
    source = (row_id % group) * row_count + (row_id // group + row_index) % row_count
    order = jnp.where(col_id == source, 1.0, 0.0).astype(BF16)
    for part in range(2):
        for chunk in range(local_rows // group):
            base = (part * local_rows + chunk * group) * row_count
            mixed = inverse_ref[base:base + span, :]
            sorted_rows = jnp.dot(order, mixed, preferred_element_type=F32).astype(BF16)
            for owner in range(row_count):
                straight_ref[
                    part, chunk * group:(chunk + 1) * group, owner * block:(owner + 1) * block
                ] = sorted_rows[owner * group:(owner + 1) * group]
    own = []
    for c in range(col_count):
        block_of = own_refs[0][...]
        for other in range(1, col_count):
            block_of = jnp.where((col_index ^ c) == other, own_refs[other][...], block_of)
        own.append(block_of)
    own = jnp.concatenate(own, axis=1)
    total_cols = own_wide_ref.shape[0]
    slot = diag_ref.shape[2]
    offsets = offsets_of(widths_ref, total_cols // slot)
    row_in_slot = lax.broadcasted_iota(jnp.int32, (slot, packed_width), 0)
    column = lax.broadcasted_iota(jnp.int32, (slot, packed_width), 1)
    for k in range(total_cols // slot):
        chosen = (column == row_in_slot + offsets[k]) & (row_in_slot < widths_ref[k])
        chosen = jnp.where(chosen, 1.0, 0.0).astype(BF16)
        for part, sign in enumerate((1.0, -1.0)):
            rows = own[part * packed_width:(part + 1) * packed_width]
            own_wide_ref[k * slot:(k + 1) * slot, part * local_rows:(part + 1) * local_rows] = (
                sign * jnp.dot(chosen, rows, preferred_element_type=F32)
            ).astype(BF16)
    per_col = term_ref.shape[0]
    first = pl.multiple_of(col_index * per_col, per_col)
    term_ref[...] = weights_ref[0, 0] * diag_ref[0, pl.ds(first, per_col), :].astype(
        F32
    ) - weights_ref[0, 1] * diag_ref[1, pl.ds(first, per_col), :].astype(F32)


def compute_kernel(
    col_count, supernodes, slot, widths_ref, weights_ref, place_ref, straight_ref, own_wide_ref,
    *refs
):
    block_refs, refs = refs[:-7], refs[-7:]
    keep_d_ref, send_d_ref, keep_t_ref, send_t_ref, x_ref, y_ref, t_ref = refs
    packed_width = block_refs[0].shape[0] // 2
    local_rows = straight_ref.shape[1]
    strips = local_rows // slot
    w_real = weights_ref[0, 0]
    w_imag = weights_ref[0, 1]
    col_index = place_ref[1]

    panel = jnp.concatenate([ref[...] for ref in block_refs], axis=1)
    with_real = rows_by_rows(panel, straight_ref[0])
    with_imag = rows_by_rows(panel, straight_ref[1])
    u_real = with_imag[packed_width:] - with_real[:packed_width]
    u_imag = -(with_real[packed_width:] + with_imag[:packed_width])
    weighted = w_real * u_real - w_imag * u_imag
    turned = w_real * u_imag + w_imag * u_real

    half = packed_width // 2
    upper = (col_index & (col_count // 2)) != 0
    keep_d_ref[...] = jnp.where(upper, weighted[half:], weighted[:half])
    send_d_ref[...] = jnp.where(upper, weighted[:half], weighted[half:])

    for ref, value in ((x_ref, weighted), (y_ref, turned)):
        for s in range(strips):
            ref[s, :packed_width] = value[:, s * slot:(s + 1) * slot]
            ref[s, packed_width:] = jnp.zeros((slot, slot), F32)

    offsets = offsets_of(widths_ref, supernodes)
    for k in range(supernodes):
        right = jnp.concatenate(
            [ref[s, pl.ds(offsets[k], slot), :] for ref in (x_ref, y_ref) for s in range(strips)],
            axis=1,
        )
        high = right.astype(BF16)
        low = (right - high.astype(F32)).astype(BF16)
        product = rows_by_rows(
            own_wide_ref[k * slot:(k + 1) * slot, :], jnp.concatenate([high, low], axis=0)
        )
        t_ref[pl.ds(offsets[k], slot), :] = product[:, :slot] + product[:, slot:]
    keep_t_ref[...] = jnp.where(upper, t_ref[half:2 * half], t_ref[:half])
    send_t_ref[...] = jnp.where(upper, t_ref[:half], t_ref[half:2 * half])


def expand_kernel(
    col_count, slot, widths_ref, place_ref, mine_d_ref, other_d_ref, mine_t_ref, other_t_ref,
    mine_term_ref, other_term_ref, density_ref, diagonal_ref, strip_ref,
):
    supernodes = diagonal_ref.shape[0] // slot
    per_col, local_rows = density_ref.shape
    strips = local_rows // slot
    share = col_count // 2
    part = mine_d_ref.shape[0] // share
    col_index = place_ref[1]
    upper = (col_index & share) != 0
    for side in range(2):
        own_side = upper if side else jnp.logical_not(upper)
        d_value = jnp.where(own_side, mine_d_ref[...], other_d_ref[...])
        t_value = jnp.where(own_side, mine_t_ref[...], other_t_ref[...])
        rows = mine_term_ref.shape[0]
        diagonal_ref[side * rows:(side + 1) * rows] = jnp.where(
            own_side, mine_term_ref[...], other_term_ref[...]
        )
        for q in range(share):
            owner = side * share + q
            base = owner * part
            for s in range(strips):
                lanes = slice(s * slot, (s + 1) * slot)
                strip_ref[s, base:base + part] = d_value[q * part:(q + 1) * part, lanes]
            strip_ref[strips, base:base + part] = t_value[q * part:(q + 1) * part]
    for s in range(strips + 1):
        strip_ref[s, col_count * part:] = jnp.zeros((slot, slot), F32)
    offsets = offsets_of(widths_ref, supernodes)
    lane = lax.broadcasted_iota(jnp.int32, (1, slot), 1)
    row_in_slot = lax.broadcasted_iota(jnp.int32, (slot, 1), 0)
    for k in range(supernodes):
        product = strip_ref[strips, pl.ds(offsets[k], slot), :]
        valid = (row_in_slot < widths_ref[k]) & (lane < widths_ref[k])
        product = jnp.where(valid, product, 0.0)
        diagonal_ref[k * slot:(k + 1) * slot] -= product
    size = min(per_col, slot)
    row_in_part = lax.broadcasted_iota(jnp.int32, (size, 1), 0)
    for part in range(per_col // size):
        first = col_index * per_col + part * size
        owner = first // slot
        within = first % slot
        start, count = 0, 0
        for k in range(supernodes):
            start = start + jnp.where(k < owner, widths_ref[k], 0)
            count = count + jnp.where(k == owner, widths_ref[k], 0)
        for s in range(strips):
            piece = strip_ref[s, pl.ds(start + within, size), :]
            density_ref[part * size:(part + 1) * size, s * slot:(s + 1) * slot] = jnp.where(
                row_in_part < count - within, piece, 0.0
            )


def bits_of(count):
    return [1 << k for k in range(count.bit_length() - 1)]


def swap(value, axis, bit):
    return lax.ppermute(value, axis, [(i, i ^ bit) for i in range(lax.axis_size(axis))])


def tree_sum(terms):
    while len(terms) > 1:
        terms = [terms[j] + terms[j + 1] for j in range(0, len(terms), 2)]
    return terms[0]


def sum_direct(value, axis):
    return tree_sum([value] + [swap(value, axis, j) for j in range(1, lax.axis_size(axis))])


def scatter_rest(value, axis):
    index = lax.axis_index(axis)
    for bit in bits_of(lax.axis_size(axis))[:-1][::-1]:
        half = value.shape[0] // 2
        upper = (index & bit) != 0
        keep = jnp.where(upper, value[half:], value[:half])
        value = keep + swap(jnp.where(upper, value[:half], value[half:]), axis, bit)
    return value


def gather_but_last(value, axis):
    index = lax.axis_index(axis)
    for bit in bits_of(lax.axis_size(axis))[:-1]:
        other = swap(value, axis, bit)
        upper = (index & bit) != 0
        value = jnp.concatenate(
            [jnp.where(upper, other, value), jnp.where(upper, value, other)], axis=0
        )
    return value


def per_device(found_inverse, l_panel, block_pattern, sup_widths, diag_inverse, pole_weights):
    slot = diag_inverse.shape[-1]
    total_cols = l_panel.shape[-1]
    supernodes = total_cols // slot
    packed_width = slot + (supernodes - 1) * (slot // 2)
    half = packed_width // 2
    local_rows = found_inverse.shape[2]
    block = l_panel.shape[2]
    row_count = lax.axis_size("row")
    col_count = lax.axis_size("col")
    top = col_count // 2
    place = jnp.stack([lax.axis_index("row"), lax.axis_index("col")]).astype(jnp.int32)

    packed = pl.pallas_call(
        functools.partial(pack_kernel, supernodes, slot),
        in_specs=[SMEM_SPEC, SMEM_SPEC, VMEM_SPEC],
        out_specs=VMEM_SPEC,
        out_shape=jax.ShapeDtypeStruct((2 * packed_width, block), BF16),
        name="pack",
    )(block_pattern, sup_widths, l_panel[0])

    blocks = {0: packed}
    for shift in sorted(range(1, row_count), key=lambda s: -min(s, row_count - s)):
        pairs = [((i + shift) % row_count, i) for i in range(row_count)]
        blocks[shift] = lax.ppermute(packed, "row", pairs)
    own = [packed] + [swap(packed, "col", other) for other in range(1, col_count)]

    straight, own_wide, term = pl.pallas_call(
        functools.partial(prepare_kernel, (row_count, col_count)),
        in_specs=[SMEM_SPEC] * 3 + [VMEM_SPEC] * (2 + col_count),
        out_specs=[VMEM_SPEC] * 3,
        out_shape=[
            jax.ShapeDtypeStruct((2, local_rows, row_count * block), BF16),
            jax.ShapeDtypeStruct((total_cols, 2 * local_rows), BF16),
            jax.ShapeDtypeStruct((total_cols // col_count, slot), F32),
        ],
        compiler_params=PARAMS,
        cost_estimate=pl.CostEstimate(
            flops=4 * 256 * local_rows * row_count * block,
            bytes_accessed=8 * local_rows * row_count * block,
            transcendentals=0,
        ),
        name="prepare",
    )(
        sup_widths, pole_weights, place,
        found_inverse.reshape(2 * local_rows * row_count, block), diag_inverse[0], *own,
    )
    term = sum_direct(term, "pole")

    keep_d, send_d, keep_t, send_t = pl.pallas_call(
        functools.partial(compute_kernel, col_count, supernodes, slot),
        in_specs=[SMEM_SPEC] * 3 + [VMEM_SPEC] * (2 + row_count),
        out_specs=[VMEM_SPEC] * 4,
        out_shape=[jax.ShapeDtypeStruct((half, local_rows), F32)] * 2
        + [jax.ShapeDtypeStruct((half, slot), F32)] * 2,
        scratch_shapes=[
            pltpu.VMEM((local_rows // slot, packed_width + slot, slot), F32),
            pltpu.VMEM((local_rows // slot, packed_width + slot, slot), F32),
            pltpu.VMEM((packed_width + slot, slot), F32),
        ],
        compiler_params=PARAMS,
        name="compute",
    )(
        sup_widths, pole_weights, place, straight, own_wide,
        *[blocks[shift] for shift in range(row_count)],
    )

    tie = lax.optimization_barrier
    products, send_d, term = tie((keep_t + swap(send_t, "col", top), send_d, term))
    term = gather_but_last(term, "col")
    products = scatter_rest(products, "col")
    for bit in bits_of(row_count):
        products = products + swap(products, "row", bit)
    density = scatter_rest(keep_d + swap(send_d, "col", top), "col")
    density = sum_direct(density, "pole")
    products, density = tie((products, density))
    products = sum_direct(products, "pole")
    density = gather_but_last(density, "col")
    products = gather_but_last(products, "col")

    return pl.pallas_call(
        functools.partial(expand_kernel, col_count, slot),
        in_specs=[SMEM_SPEC] * 2 + [VMEM_SPEC] * 6,
        out_specs=[VMEM_SPEC] * 2,
        out_shape=[
            jax.ShapeDtypeStruct((total_cols // col_count, local_rows), F32),
            jax.ShapeDtypeStruct((total_cols, slot), F32),
        ],
        scratch_shapes=[pltpu.VMEM((local_rows // slot + 1, packed_width + slot, slot), F32)],
        compiler_params=PARAMS,
        name="expand",
    )(
        sup_widths, place, density, swap(density, "col", top),
        products, swap(products, "col", top), term, swap(term, "col", top),
    )


def solution(mesh):
    in_specs = (
        P("pole", None, "row", None, "col", None),
        P("pole", None, ("row", "col"), None),
        P(("row", "col"), None),
        P(),
        P("pole", None, None, None),
        P("pole", None),
    )
    out_specs = (P("col", "row"), P())
    return jax.shard_map(
        per_device, mesh=mesh, in_specs=in_specs, out_specs=out_specs, check_vma=False
    )
```

```python
import functools

import jax
import jax.numpy as jnp
from jax import lax
from jax.experimental import pallas as pl
from jax.experimental.pallas import tpu as pltpu
from jax.sharding import PartitionSpec as P

F32 = jnp.float32
BF16 = jnp.bfloat16
VMEM_SPEC = pl.BlockSpec(memory_space=pltpu.VMEM)
SMEM_SPEC = pl.BlockSpec(memory_space=pltpu.SMEM)
PARAMS = pltpu.CompilerParams(vmem_limit_bytes=48 * 1024 * 1024)


def rows_by_rows(left, right):
    return lax.dot_general(left, right, (((1,), (1,)), ((), ())), preferred_element_type=F32)


def offsets_of(widths_ref, supernodes):
    offsets = [0]
    for k in range(supernodes):
        offsets.append(offsets[-1] + widths_ref[k])
    return offsets


def pack_kernel(supernodes, slot, pattern_ref, widths_ref, panel_ref, packed_ref):
    packed_width = packed_ref.shape[0] // 2
    offsets = offsets_of(widths_ref, supernodes)
    lane = lax.broadcasted_iota(jnp.int32, (1, slot), 1)
    place = []
    for k in range(supernodes):
        valid = (lane < widths_ref[k]) & (pattern_ref[0, k] == 1)
        place.append(jnp.where(valid, offsets[k] + lane, -1))
    place = jnp.concatenate(place, axis=1)
    target = lax.broadcasted_iota(jnp.int32, (packed_width, supernodes * slot), 0)
    select = jnp.where(target == place, 1.0, 0.0).astype(BF16)
    for part in range(2):
        packed_ref[part * packed_width:(part + 1) * packed_width, :] = rows_by_rows(
            select, panel_ref[part]
        ).astype(BF16)


def prepare_kernel(
    counts, widths_ref, weights_ref, place_ref, inverse_ref, diag_ref, *refs
):
    row_count, col_count = counts
    own_refs, (straight_ref, own_wide_ref, term_ref) = refs[:col_count], refs[col_count:]
    packed_width = own_refs[0].shape[0] // 2
    col_index = place_ref[1]
    block = inverse_ref.shape[1]
    local_rows = straight_ref.shape[1]
    row_index = place_ref[0]
    group = max(8, 256 // row_count)
    span = group * row_count
    row_id = lax.broadcasted_iota(jnp.int32, (span, span), 0)
    col_id = lax.broadcasted_iota(jnp.int32, (span, span), 1)
    source = (row_id % group) * row_count + (row_id // group + row_index) % row_count
    order = jnp.where(col_id == source, 1.0, 0.0).astype(BF16)
    for part in range(2):
        for chunk in range(local_rows // group):
            base = (part * local_rows + chunk * group) * row_count
            mixed = inverse_ref[base:base + span, :]
            sorted_rows = jnp.dot(order, mixed, preferred_element_type=F32).astype(BF16)
            for owner in range(row_count):
                straight_ref[
                    part, chunk * group:(chunk + 1) * group, owner * block:(owner + 1) * block
                ] = sorted_rows[owner * group:(owner + 1) * group]
    own = []
    for c in range(col_count):
        block_of = own_refs[0][...]
        for other in range(1, col_count):
            block_of = jnp.where((col_index ^ c) == other, own_refs[other][...], block_of)
        own.append(block_of)
    own = jnp.concatenate(own, axis=1)
    total_cols = own_wide_ref.shape[0]
    slot = diag_ref.shape[2]
    offsets = offsets_of(widths_ref, total_cols // slot)
    row_in_slot = lax.broadcasted_iota(jnp.int32, (slot, packed_width), 0)
    column = lax.broadcasted_iota(jnp.int32, (slot, packed_width), 1)
    for k in range(total_cols // slot):
        chosen = (column == row_in_slot + offsets[k]) & (row_in_slot < widths_ref[k])
        chosen = jnp.where(chosen, 1.0, 0.0).astype(BF16)
        for part, sign in enumerate((1.0, -1.0)):
            rows = own[part * packed_width:(part + 1) * packed_width]
            own_wide_ref[k * slot:(k + 1) * slot, part * local_rows:(part + 1) * local_rows] = (
                sign * jnp.dot(chosen, rows, preferred_element_type=F32)
            ).astype(BF16)
    per_col = term_ref.shape[0]
    first = pl.multiple_of(col_index * per_col, per_col)
    term_ref[...] = weights_ref[0, 0] * diag_ref[0, pl.ds(first, per_col), :].astype(
        F32
    ) - weights_ref[0, 1] * diag_ref[1, pl.ds(first, per_col), :].astype(F32)


def compute_kernel(
    shifts, col_count, supernodes, slot, widths_ref, weights_ref, place_ref, straight_ref,
    own_wide_ref, *refs
):
    block_refs, refs = refs[:-7], refs[-7:]
    block_refs = [block_refs[shifts.index(shift)] for shift in range(len(shifts))]
    keep_d_ref, send_d_ref, keep_t_ref, send_t_ref, x_ref, y_ref, t_ref = refs
    packed_width = block_refs[0].shape[0] // 2
    local_rows = straight_ref.shape[1]
    strips = local_rows // slot
    w_real = weights_ref[0, 0]
    w_imag = weights_ref[0, 1]
    col_index = place_ref[1]

    panel = jnp.concatenate([ref[...] for ref in block_refs], axis=1)
    with_real = rows_by_rows(panel, straight_ref[0])
    with_imag = rows_by_rows(panel, straight_ref[1])
    u_real = with_imag[packed_width:] - with_real[:packed_width]
    u_imag = -(with_real[packed_width:] + with_imag[:packed_width])
    weighted = w_real * u_real - w_imag * u_imag
    turned = w_real * u_imag + w_imag * u_real

    half = packed_width // 2
    upper = (col_index & (col_count // 2)) != 0
    keep_d_ref[...] = jnp.where(upper, weighted[half:], weighted[:half])
    send_d_ref[...] = jnp.where(upper, weighted[:half], weighted[half:])

    for ref, value in ((x_ref, weighted), (y_ref, turned)):
        for s in range(strips):
            ref[s, :packed_width] = value[:, s * slot:(s + 1) * slot]
            ref[s, packed_width:] = jnp.zeros((slot, slot), F32)

    offsets = offsets_of(widths_ref, supernodes)
    for k in range(supernodes):
        right = jnp.concatenate(
            [ref[s, pl.ds(offsets[k], slot), :] for ref in (x_ref, y_ref) for s in range(strips)],
            axis=1,
        )
        high = right.astype(BF16)
        low = (right - high.astype(F32)).astype(BF16)
        product = rows_by_rows(
            own_wide_ref[k * slot:(k + 1) * slot, :], jnp.concatenate([high, low], axis=0)
        )
        t_ref[pl.ds(offsets[k], slot), :] = product[:, :slot] + product[:, slot:]
    keep_t_ref[...] = jnp.where(upper, t_ref[half:2 * half], t_ref[:half])
    send_t_ref[...] = jnp.where(upper, t_ref[:half], t_ref[half:2 * half])


def expand_kernel(
    col_count, slot, widths_ref, place_ref, mine_d_ref, other_d_ref, mine_t_ref, other_t_ref,
    mine_term_ref, other_term_ref, density_ref, diagonal_ref, strip_ref,
):
    supernodes = diagonal_ref.shape[0] // slot
    per_col, local_rows = density_ref.shape
    strips = local_rows // slot
    share = col_count // 2
    part = mine_d_ref.shape[0] // share
    col_index = place_ref[1]
    upper = (col_index & share) != 0
    for side in range(2):
        own_side = upper if side else jnp.logical_not(upper)
        d_value = jnp.where(own_side, mine_d_ref[...], other_d_ref[...])
        t_value = jnp.where(own_side, mine_t_ref[...], other_t_ref[...])
        rows = mine_term_ref.shape[0]
        diagonal_ref[side * rows:(side + 1) * rows] = jnp.where(
            own_side, mine_term_ref[...], other_term_ref[...]
        )
        for q in range(share):
            owner = side * share + q
            base = owner * part
            for s in range(strips):
                lanes = slice(s * slot, (s + 1) * slot)
                strip_ref[s, base:base + part] = d_value[q * part:(q + 1) * part, lanes]
            strip_ref[strips, base:base + part] = t_value[q * part:(q + 1) * part]
    for s in range(strips + 1):
        strip_ref[s, col_count * part:] = jnp.zeros((slot, slot), F32)
    offsets = offsets_of(widths_ref, supernodes)
    lane = lax.broadcasted_iota(jnp.int32, (1, slot), 1)
    row_in_slot = lax.broadcasted_iota(jnp.int32, (slot, 1), 0)
    for k in range(supernodes):
        product = strip_ref[strips, pl.ds(offsets[k], slot), :]
        valid = (row_in_slot < widths_ref[k]) & (lane < widths_ref[k])
        product = jnp.where(valid, product, 0.0)
        diagonal_ref[k * slot:(k + 1) * slot] -= product
    size = min(per_col, slot)
    row_in_part = lax.broadcasted_iota(jnp.int32, (size, 1), 0)
    for part in range(per_col // size):
        first = col_index * per_col + part * size
        owner = first // slot
        within = first % slot
        start, count = 0, 0
        for k in range(supernodes):
            start = start + jnp.where(k < owner, widths_ref[k], 0)
            count = count + jnp.where(k == owner, widths_ref[k], 0)
        for s in range(strips):
            piece = strip_ref[s, pl.ds(start + within, size), :]
            density_ref[part * size:(part + 1) * size, s * slot:(s + 1) * slot] = jnp.where(
                row_in_part < count - within, piece, 0.0
            )


def bits_of(count):
    return [1 << k for k in range(count.bit_length() - 1)]


def swap(value, axis, bit):
    return lax.ppermute(value, axis, [(i, i ^ bit) for i in range(lax.axis_size(axis))])


def tree_sum(terms):
    while len(terms) > 1:
        terms = [terms[j] + terms[j + 1] for j in range(0, len(terms), 2)]
    return terms[0]


def sum_direct(value, axis):
    return tree_sum([value] + [swap(value, axis, j) for j in range(1, lax.axis_size(axis))])


def scatter_rest(value, axis):
    index = lax.axis_index(axis)
    for bit in bits_of(lax.axis_size(axis))[:-1][::-1]:
        half = value.shape[0] // 2
        upper = (index & bit) != 0
        keep = jnp.where(upper, value[half:], value[:half])
        value = keep + swap(jnp.where(upper, value[:half], value[half:]), axis, bit)
    return value


def gather_but_last(value, axis):
    index = lax.axis_index(axis)
    for bit in bits_of(lax.axis_size(axis))[:-1]:
        other = swap(value, axis, bit)
        upper = (index & bit) != 0
        value = jnp.concatenate(
            [jnp.where(upper, other, value), jnp.where(upper, value, other)], axis=0
        )
    return value


def per_device(found_inverse, l_panel, block_pattern, sup_widths, diag_inverse, pole_weights):
    slot = diag_inverse.shape[-1]
    total_cols = l_panel.shape[-1]
    supernodes = total_cols // slot
    packed_width = slot + (supernodes - 1) * (slot // 2)
    half = packed_width // 2
    local_rows = found_inverse.shape[2]
    block = l_panel.shape[2]
    row_count = lax.axis_size("row")
    col_count = lax.axis_size("col")
    top = col_count // 2
    place = jnp.stack([lax.axis_index("row"), lax.axis_index("col")]).astype(jnp.int32)

    packed = pl.pallas_call(
        functools.partial(pack_kernel, supernodes, slot),
        in_specs=[SMEM_SPEC, SMEM_SPEC, VMEM_SPEC],
        out_specs=VMEM_SPEC,
        out_shape=jax.ShapeDtypeStruct((2 * packed_width, block), BF16),
        name="pack",
    )(block_pattern, sup_widths, l_panel[0])

    blocks = {0: packed}
    shifts = sorted(range(row_count), key=lambda shift: min(shift, row_count - shift))
    for shift in shifts[1:]:
        pairs = [((i + shift) % row_count, i) for i in range(row_count)]
        blocks[shift] = lax.ppermute(packed, "row", pairs)
    own = [packed] + [swap(packed, "col", other) for other in range(1, col_count)]

    straight, own_wide, term = pl.pallas_call(
        functools.partial(prepare_kernel, (row_count, col_count)),
        in_specs=[SMEM_SPEC] * 3 + [VMEM_SPEC] * (2 + col_count),
        out_specs=[VMEM_SPEC] * 3,
        out_shape=[
            jax.ShapeDtypeStruct((2, local_rows, row_count * block), BF16),
            jax.ShapeDtypeStruct((total_cols, 2 * local_rows), BF16),
            jax.ShapeDtypeStruct((total_cols // col_count, slot), F32),
        ],
        compiler_params=PARAMS,
        cost_estimate=pl.CostEstimate(
            flops=4 * 256 * local_rows * row_count * block,
            bytes_accessed=8 * local_rows * row_count * block,
            transcendentals=0,
        ),
        name="prepare",
    )(
        sup_widths, pole_weights, place,
        found_inverse.reshape(2 * local_rows * row_count, block), diag_inverse[0], *own,
    )
    term = sum_direct(term, "pole")

    keep_d, send_d, keep_t, send_t = pl.pallas_call(
        functools.partial(compute_kernel, shifts, col_count, supernodes, slot),
        in_specs=[SMEM_SPEC] * 3 + [VMEM_SPEC] * (2 + row_count),
        out_specs=[VMEM_SPEC] * 4,
        out_shape=[jax.ShapeDtypeStruct((half, local_rows), F32)] * 2
        + [jax.ShapeDtypeStruct((half, slot), F32)] * 2,
        scratch_shapes=[
            pltpu.VMEM((local_rows // slot, packed_width + slot, slot), F32),
            pltpu.VMEM((local_rows // slot, packed_width + slot, slot), F32),
            pltpu.VMEM((packed_width + slot, slot), F32),
        ],
        compiler_params=PARAMS,
        name="compute",
    )(
        sup_widths, pole_weights, place, straight, own_wide,
        *[blocks[shift] for shift in shifts],
    )

    tie = lax.optimization_barrier
    products, send_d, term = tie((keep_t + swap(send_t, "col", top), send_d, term))
    term = gather_but_last(term, "col")
    products = scatter_rest(products, "col")
    for bit in bits_of(row_count):
        products = products + swap(products, "row", bit)
    density = scatter_rest(keep_d + swap(send_d, "col", top), "col")
    density = sum_direct(density, "pole")
    products = sum_direct(products, "pole")
    density = gather_but_last(density, "col")
    products = gather_but_last(products, "col")

    return pl.pallas_call(
        functools.partial(expand_kernel, col_count, slot),
        in_specs=[SMEM_SPEC] * 2 + [VMEM_SPEC] * 6,
        out_specs=[VMEM_SPEC] * 2,
        out_shape=[
            jax.ShapeDtypeStruct((total_cols // col_count, local_rows), F32),
            jax.ShapeDtypeStruct((total_cols, slot), F32),
        ],
        scratch_shapes=[pltpu.VMEM((local_rows // slot + 1, packed_width + slot, slot), F32)],
        compiler_params=PARAMS,
        name="expand",
    )(
        sup_widths, place, density, swap(density, "col", top),
        products, swap(products, "col", top), term, swap(term, "col", top),
    )


def solution(mesh):
    in_specs = (
        P("pole", None, "row", None, "col", None),
        P("pole", None, ("row", "col"), None),
        P(("row", "col"), None),
        P(),
        P("pole", None, None, None),
        P("pole", None),
    )
    out_specs = (P("col", "row"), P())
    return jax.shard_map(
        per_device, mesh=mesh, in_specs=in_specs, out_specs=out_specs, check_vma=False
    )
```

```python
import functools

import jax
import jax.numpy as jnp
from jax import lax
from jax.experimental import pallas as pl
from jax.experimental.pallas import tpu as pltpu
from jax.sharding import PartitionSpec as P

F32 = jnp.float32
BF16 = jnp.bfloat16
VMEM_SPEC = pl.BlockSpec(memory_space=pltpu.VMEM)
SMEM_SPEC = pl.BlockSpec(memory_space=pltpu.SMEM)
PARAMS = pltpu.CompilerParams(vmem_limit_bytes=48 * 1024 * 1024)


def rows_by_rows(left, right):
    return lax.dot_general(left, right, (((1,), (1,)), ((), ())), preferred_element_type=F32)


def offsets_of(widths_ref, supernodes):
    offsets = [0]
    for k in range(supernodes):
        offsets.append(offsets[-1] + widths_ref[k])
    return offsets


def pack_kernel(supernodes, slot, pattern_ref, widths_ref, panel_ref, packed_ref):
    packed_width = packed_ref.shape[0] // 2
    offsets = offsets_of(widths_ref, supernodes)
    lane = lax.broadcasted_iota(jnp.int32, (1, slot), 1)
    place = []
    for k in range(supernodes):
        valid = (lane < widths_ref[k]) & (pattern_ref[0, k] == 1)
        place.append(jnp.where(valid, offsets[k] + lane, -1))
    place = jnp.concatenate(place, axis=1)
    target = lax.broadcasted_iota(jnp.int32, (packed_width, supernodes * slot), 0)
    select = jnp.where(target == place, 1.0, 0.0).astype(BF16)
    for part in range(2):
        packed_ref[part * packed_width:(part + 1) * packed_width, :] = rows_by_rows(
            select, panel_ref[part]
        ).astype(BF16)


def prepare_kernel(
    counts, widths_ref, weights_ref, place_ref, inverse_ref, diag_ref, *refs
):
    row_count, col_count = counts
    own_refs, refs = refs[:col_count], refs[col_count:]
    straight_ref, own_wide_ref, term_ref, pick_d_ref, pick_t_ref, keep_ref, upper_ref = refs
    packed_width = own_refs[0].shape[0] // 2
    col_index = place_ref[1]
    block = inverse_ref.shape[1]
    local_rows = straight_ref.shape[1]
    row_index = place_ref[0]
    group = max(8, 256 // row_count)
    span = group * row_count
    row_id = lax.broadcasted_iota(jnp.int32, (span, span), 0)
    col_id = lax.broadcasted_iota(jnp.int32, (span, span), 1)
    source = (row_id % group) * row_count + (row_id // group + row_index) % row_count
    order = jnp.where(col_id == source, 1.0, 0.0).astype(BF16)
    for part in range(2):
        for chunk in range(local_rows // group):
            base = (part * local_rows + chunk * group) * row_count
            mixed = inverse_ref[base:base + span, :]
            sorted_rows = jnp.dot(order, mixed, preferred_element_type=F32).astype(BF16)
            for owner in range(row_count):
                straight_ref[
                    part, chunk * group:(chunk + 1) * group, owner * block:(owner + 1) * block
                ] = sorted_rows[owner * group:(owner + 1) * group]
    own = []
    for c in range(col_count):
        block_of = own_refs[0][...]
        for other in range(1, col_count):
            block_of = jnp.where((col_index ^ c) == other, own_refs[other][...], block_of)
        own.append(block_of)
    own = jnp.concatenate(own, axis=1)
    total_cols = own_wide_ref.shape[0]
    slot = diag_ref.shape[2]
    offsets = offsets_of(widths_ref, total_cols // slot)
    row_in_slot = lax.broadcasted_iota(jnp.int32, (slot, packed_width), 0)
    column = lax.broadcasted_iota(jnp.int32, (slot, packed_width), 1)
    for k in range(total_cols // slot):
        chosen = (column == row_in_slot + offsets[k]) & (row_in_slot < widths_ref[k])
        chosen = jnp.where(chosen, 1.0, 0.0).astype(BF16)
        for part, sign in enumerate((1.0, -1.0)):
            rows = own[part * packed_width:(part + 1) * packed_width]
            own_wide_ref[k * slot:(k + 1) * slot, part * local_rows:(part + 1) * local_rows] = (
                sign * jnp.dot(chosen, rows, preferred_element_type=F32)
            ).astype(BF16)
    per_col = term_ref.shape[0]
    first = pl.multiple_of(col_index * per_col, per_col)
    term_ref[...] = weights_ref[0, 0] * diag_ref[0, pl.ds(first, per_col), :].astype(
        F32
    ) - weights_ref[0, 1] * diag_ref[1, pl.ds(first, per_col), :].astype(F32)
    side = jnp.where((col_index & (col_count // 2)) != 0, 1, 0)
    half = packed_width // 2
    position = jnp.where(column < half, column + side * half, column - side * half)
    lane = lax.broadcasted_iota(jnp.int32, (slot, slot), 1)
    for k in range(total_cols // slot):
        chosen = (position == row_in_slot + offsets[k]) & (row_in_slot < widths_ref[k])
        rows = slice(k * slot, (k + 1) * slot)
        pick_t_ref[rows, :] = jnp.where(chosen, 1.0, 0.0).astype(BF16)
        keep_ref[rows, :] = jnp.where(
            (lane < widths_ref[k]) & (row_in_slot[:, :slot] < widths_ref[k]), 1.0, 0.0
        )
    size = min(per_col, slot)
    for part in range(per_col // size):
        begin = col_index * per_col + part * size
        start, count = 0, 0
        for k in range(total_cols // slot):
            start = start + jnp.where(k < begin // slot, widths_ref[k], 0)
            count = count + jnp.where(k == begin // slot, widths_ref[k], 0)
        within = row_in_slot[:size] + begin % slot
        chosen = (position[:size] == within + start) & (within < count)
        pick_d_ref[part * size:(part + 1) * size, :] = jnp.where(chosen, 1.0, 0.0).astype(BF16)
    upper_ref[...] = jnp.full(upper_ref.shape, side, jnp.int32).astype(F32)


def compute_kernel(
    shifts, col_count, supernodes, slot, widths_ref, weights_ref, place_ref, straight_ref,
    own_wide_ref, *refs
):
    block_refs, refs = refs[:-7], refs[-7:]
    block_refs = [block_refs[shifts.index(shift)] for shift in range(len(shifts))]
    keep_d_ref, send_d_ref, keep_t_ref, send_t_ref, x_ref, y_ref, t_ref = refs
    packed_width = block_refs[0].shape[0] // 2
    local_rows = straight_ref.shape[1]
    strips = local_rows // slot
    w_real = weights_ref[0, 0]
    w_imag = weights_ref[0, 1]
    col_index = place_ref[1]

    panel = jnp.concatenate([ref[...] for ref in block_refs], axis=1)
    with_real = rows_by_rows(panel, straight_ref[0])
    with_imag = rows_by_rows(panel, straight_ref[1])
    u_real = with_imag[packed_width:] - with_real[:packed_width]
    u_imag = -(with_real[packed_width:] + with_imag[:packed_width])
    weighted = w_real * u_real - w_imag * u_imag
    turned = w_real * u_imag + w_imag * u_real

    half = packed_width // 2
    upper = (col_index & (col_count // 2)) != 0
    keep_d_ref[...] = jnp.where(upper, weighted[half:], weighted[:half])
    send_d_ref[...] = jnp.where(upper, weighted[:half], weighted[half:])

    for ref, value in ((x_ref, weighted), (y_ref, turned)):
        for s in range(strips):
            ref[s, :packed_width] = value[:, s * slot:(s + 1) * slot]
            ref[s, packed_width:] = jnp.zeros((slot, slot), F32)

    offsets = offsets_of(widths_ref, supernodes)
    for k in range(supernodes):
        right = jnp.concatenate(
            [ref[s, pl.ds(offsets[k], slot), :] for ref in (x_ref, y_ref) for s in range(strips)],
            axis=1,
        )
        high = right.astype(BF16)
        low = (right - high.astype(F32)).astype(BF16)
        product = rows_by_rows(
            own_wide_ref[k * slot:(k + 1) * slot, :], jnp.concatenate([high, low], axis=0)
        )
        t_ref[pl.ds(offsets[k], slot), :] = product[:, :slot] + product[:, slot:]
    keep_t_ref[...] = jnp.where(upper, t_ref[half:2 * half], t_ref[:half])
    send_t_ref[...] = jnp.where(upper, t_ref[:half], t_ref[half:2 * half])


def picked(pick_ref, value):
    high = value.astype(BF16)
    low = (value - high.astype(F32)).astype(BF16)
    return jnp.dot(pick_ref[...], high, preferred_element_type=F32) + jnp.dot(
        pick_ref[...], low, preferred_element_type=F32
    )


def expand_kernel(
    pick_d_ref, pick_t_ref, keep_ref, upper_ref, mine_d_ref, other_d_ref, mine_t_ref, other_t_ref,
    mine_term_ref, other_term_ref, density_ref, diagonal_ref,
):
    density_ref[...] = picked(pick_d_ref, jnp.concatenate([mine_d_ref[...], other_d_ref[...]], axis=0))
    product = picked(pick_t_ref, jnp.concatenate([mine_t_ref[...], other_t_ref[...]], axis=0))
    rows = mine_term_ref.shape[0]
    upper = upper_ref[:1, :] > 0.5
    terms = (
        jnp.where(upper, other_term_ref[...], mine_term_ref[...]),
        jnp.where(upper, mine_term_ref[...], other_term_ref[...]),
    )
    for side in range(2):
        part = slice(side * rows, (side + 1) * rows)
        diagonal_ref[part] = terms[side] - jnp.where(keep_ref[part] > 0.5, product[part], 0.0)


def bits_of(count):
    return [1 << k for k in range(count.bit_length() - 1)]


def swap(value, axis, bit):
    return lax.ppermute(value, axis, [(i, i ^ bit) for i in range(lax.axis_size(axis))])


def tree_sum(terms):
    while len(terms) > 1:
        terms = [terms[j] + terms[j + 1] for j in range(0, len(terms), 2)]
    return terms[0]


def sum_direct(value, axis):
    return tree_sum([value] + [swap(value, axis, j) for j in range(1, lax.axis_size(axis))])


def scatter_rest(value, axis):
    index = lax.axis_index(axis)
    for bit in bits_of(lax.axis_size(axis))[:-1][::-1]:
        half = value.shape[0] // 2
        upper = (index & bit) != 0
        keep = jnp.where(upper, value[half:], value[:half])
        value = keep + swap(jnp.where(upper, value[:half], value[half:]), axis, bit)
    return value


def gather_but_last(value, axis):
    index = lax.axis_index(axis)
    for bit in bits_of(lax.axis_size(axis))[:-1]:
        other = swap(value, axis, bit)
        upper = (index & bit) != 0
        value = jnp.concatenate(
            [jnp.where(upper, other, value), jnp.where(upper, value, other)], axis=0
        )
    return value


def per_device(found_inverse, l_panel, block_pattern, sup_widths, diag_inverse, pole_weights):
    slot = diag_inverse.shape[-1]
    total_cols = l_panel.shape[-1]
    supernodes = total_cols // slot
    packed_width = slot + (supernodes - 1) * (slot // 2)
    half = packed_width // 2
    local_rows = found_inverse.shape[2]
    block = l_panel.shape[2]
    row_count = lax.axis_size("row")
    col_count = lax.axis_size("col")
    top = col_count // 2
    place = jnp.stack([lax.axis_index("row"), lax.axis_index("col")]).astype(jnp.int32)

    packed = pl.pallas_call(
        functools.partial(pack_kernel, supernodes, slot),
        in_specs=[SMEM_SPEC, SMEM_SPEC, VMEM_SPEC],
        out_specs=VMEM_SPEC,
        out_shape=jax.ShapeDtypeStruct((2 * packed_width, block), BF16),
        name="pack",
    )(block_pattern, sup_widths, l_panel[0])

    blocks = {0: packed}
    shifts = sorted(range(row_count), key=lambda shift: min(shift, row_count - shift))
    for shift in shifts[1:]:
        pairs = [((i + shift) % row_count, i) for i in range(row_count)]
        blocks[shift] = lax.ppermute(packed, "row", pairs)
    own = [packed] + [swap(packed, "col", other) for other in range(1, col_count)]

    straight, own_wide, term, *picks = pl.pallas_call(
        functools.partial(prepare_kernel, (row_count, col_count)),
        in_specs=[SMEM_SPEC] * 3 + [VMEM_SPEC] * (2 + col_count),
        out_specs=[VMEM_SPEC] * 7,
        out_shape=[
            jax.ShapeDtypeStruct((2, local_rows, row_count * block), BF16),
            jax.ShapeDtypeStruct((total_cols, 2 * local_rows), BF16),
            jax.ShapeDtypeStruct((total_cols // col_count, slot), F32),
            jax.ShapeDtypeStruct((total_cols // col_count, packed_width), BF16),
            jax.ShapeDtypeStruct((total_cols, packed_width), BF16),
            jax.ShapeDtypeStruct((total_cols, slot), F32),
            jax.ShapeDtypeStruct((8, slot), F32),
        ],
        compiler_params=PARAMS,
        cost_estimate=pl.CostEstimate(
            flops=4 * 256 * local_rows * row_count * block,
            bytes_accessed=8 * local_rows * row_count * block,
            transcendentals=0,
        ),
        name="prepare",
    )(
        sup_widths, pole_weights, place,
        found_inverse.reshape(2 * local_rows * row_count, block), diag_inverse[0], *own,
    )
    term = sum_direct(term, "pole")

    keep_d, send_d, keep_t, send_t = pl.pallas_call(
        functools.partial(compute_kernel, shifts, col_count, supernodes, slot),
        in_specs=[SMEM_SPEC] * 3 + [VMEM_SPEC] * (2 + row_count),
        out_specs=[VMEM_SPEC] * 4,
        out_shape=[jax.ShapeDtypeStruct((half, local_rows), F32)] * 2
        + [jax.ShapeDtypeStruct((half, slot), F32)] * 2,
        scratch_shapes=[
            pltpu.VMEM((local_rows // slot, packed_width + slot, slot), F32),
            pltpu.VMEM((local_rows // slot, packed_width + slot, slot), F32),
            pltpu.VMEM((packed_width + slot, slot), F32),
        ],
        compiler_params=PARAMS,
        name="compute",
    )(
        sup_widths, pole_weights, place, straight, own_wide,
        *[blocks[shift] for shift in shifts],
    )

    tie = lax.optimization_barrier
    products, send_d, term = tie((keep_t + swap(send_t, "col", top), send_d, term))
    term = gather_but_last(term, "col")
    products = scatter_rest(products, "col")
    for bit in bits_of(row_count):
        products = products + swap(products, "row", bit)
    density = scatter_rest(keep_d + swap(send_d, "col", top), "col")
    density = sum_direct(density, "pole")
    products = sum_direct(products, "pole")
    density = gather_but_last(density, "col")
    products = gather_but_last(products, "col")

    return pl.pallas_call(
        expand_kernel,
        in_specs=[VMEM_SPEC] * 10,
        out_specs=[VMEM_SPEC] * 2,
        out_shape=[
            jax.ShapeDtypeStruct((total_cols // col_count, local_rows), F32),
            jax.ShapeDtypeStruct((total_cols, slot), F32),
        ],
        compiler_params=PARAMS,
        name="expand",
    )(
        *picks, density, swap(density, "col", top), products, swap(products, "col", top),
        term, swap(term, "col", top),
    )


def solution(mesh):
    in_specs = (
        P("pole", None, "row", None, "col", None),
        P("pole", None, ("row", "col"), None),
        P(("row", "col"), None),
        P(),
        P("pole", None, None, None),
        P("pole", None),
    )
    out_specs = (P("col", "row"), P())
    return jax.shard_map(
        per_device, mesh=mesh, in_specs=in_specs, out_specs=out_specs, check_vma=False
    )
```

```python
import functools

import jax
import jax.numpy as jnp
from jax import lax
from jax.experimental import pallas as pl
from jax.experimental.pallas import tpu as pltpu
from jax.sharding import PartitionSpec as P

F32 = jnp.float32
BF16 = jnp.bfloat16
VMEM_SPEC = pl.BlockSpec(memory_space=pltpu.VMEM)
SMEM_SPEC = pl.BlockSpec(memory_space=pltpu.SMEM)
PARAMS = pltpu.CompilerParams(vmem_limit_bytes=48 * 1024 * 1024)


def rows_by_rows(left, right):
    return lax.dot_general(left, right, (((1,), (1,)), ((), ())), preferred_element_type=F32)


def offsets_of(widths_ref, supernodes):
    offsets = [0]
    for k in range(supernodes):
        offsets.append(offsets[-1] + widths_ref[k])
    return offsets


def pack_kernel(supernodes, slot, pattern_ref, widths_ref, panel_ref, packed_ref):
    packed_width = packed_ref.shape[0] // 2
    offsets = offsets_of(widths_ref, supernodes)
    lane = lax.broadcasted_iota(jnp.int32, (1, slot), 1)
    place = []
    for k in range(supernodes):
        valid = (lane < widths_ref[k]) & (pattern_ref[0, k] == 1)
        place.append(jnp.where(valid, offsets[k] + lane, -1))
    place = jnp.concatenate(place, axis=1)
    target = lax.broadcasted_iota(jnp.int32, (packed_width, supernodes * slot), 0)
    select = jnp.where(target == place, 1.0, 0.0).astype(BF16)
    for part in range(2):
        packed_ref[part * packed_width:(part + 1) * packed_width, :] = rows_by_rows(
            select, panel_ref[part]
        ).astype(BF16)


def prepare_kernel(
    counts, widths_ref, weights_ref, place_ref, inverse_ref, diag_ref, *refs
):
    row_count, col_count = counts
    own_refs, refs = refs[:col_count], refs[col_count:]
    straight_ref, own_wide_ref, term_ref, pick_d_ref, pick_t_ref, keep_ref, upper_ref = refs
    packed_width = own_refs[0].shape[0] // 2
    col_index = place_ref[1]
    block = inverse_ref.shape[1]
    local_rows = straight_ref.shape[1]
    row_index = place_ref[0]
    group = max(8, 256 // row_count)
    span = group * row_count
    row_id = lax.broadcasted_iota(jnp.int32, (span, span), 0)
    col_id = lax.broadcasted_iota(jnp.int32, (span, span), 1)
    source = (row_id % group) * row_count + ((row_id // group) ^ row_index)
    order = jnp.where(col_id == source, 1.0, 0.0).astype(BF16)
    for part in range(2):
        for chunk in range(local_rows // group):
            base = (part * local_rows + chunk * group) * row_count
            mixed = inverse_ref[base:base + span, :]
            sorted_rows = jnp.dot(order, mixed, preferred_element_type=F32).astype(BF16)
            for owner in range(row_count):
                straight_ref[
                    part, chunk * group:(chunk + 1) * group, owner * block:(owner + 1) * block
                ] = sorted_rows[owner * group:(owner + 1) * group]
    own = []
    for c in range(col_count):
        block_of = own_refs[0][...]
        for other in range(1, col_count):
            block_of = jnp.where((col_index ^ c) == other, own_refs[other][...], block_of)
        own.append(block_of)
    own = jnp.concatenate(own, axis=1)
    total_cols = own_wide_ref.shape[0]
    slot = diag_ref.shape[2]
    offsets = offsets_of(widths_ref, total_cols // slot)
    row_in_slot = lax.broadcasted_iota(jnp.int32, (slot, packed_width), 0)
    column = lax.broadcasted_iota(jnp.int32, (slot, packed_width), 1)
    for k in range(total_cols // slot):
        chosen = (column == row_in_slot + offsets[k]) & (row_in_slot < widths_ref[k])
        chosen = jnp.where(chosen, 1.0, 0.0).astype(BF16)
        for part, sign in enumerate((1.0, -1.0)):
            rows = own[part * packed_width:(part + 1) * packed_width]
            own_wide_ref[k * slot:(k + 1) * slot, part * local_rows:(part + 1) * local_rows] = (
                sign * jnp.dot(chosen, rows, preferred_element_type=F32)
            ).astype(BF16)
    per_col = term_ref.shape[0]
    first = pl.multiple_of(col_index * per_col, per_col)
    term_ref[...] = weights_ref[0, 0] * diag_ref[0, pl.ds(first, per_col), :].astype(
        F32
    ) - weights_ref[0, 1] * diag_ref[1, pl.ds(first, per_col), :].astype(F32)
    side = jnp.where((col_index & (col_count // 2)) != 0, 1, 0)
    half = packed_width // 2
    position = jnp.where(column < half, column + side * half, column - side * half)
    lane = lax.broadcasted_iota(jnp.int32, (slot, slot), 1)
    for k in range(total_cols // slot):
        chosen = (position == row_in_slot + offsets[k]) & (row_in_slot < widths_ref[k])
        rows = slice(k * slot, (k + 1) * slot)
        pick_t_ref[rows, :] = jnp.where(chosen, 1.0, 0.0).astype(BF16)
        keep_ref[rows, :] = jnp.where(
            (lane < widths_ref[k]) & (row_in_slot[:, :slot] < widths_ref[k]), 1.0, 0.0
        )
    size = min(per_col, slot)
    for part in range(per_col // size):
        begin = col_index * per_col + part * size
        start, count = 0, 0
        for k in range(total_cols // slot):
            start = start + jnp.where(k < begin // slot, widths_ref[k], 0)
            count = count + jnp.where(k == begin // slot, widths_ref[k], 0)
        within = row_in_slot[:size] + begin % slot
        chosen = (position[:size] == within + start) & (within < count)
        pick_d_ref[part * size:(part + 1) * size, :] = jnp.where(chosen, 1.0, 0.0).astype(BF16)
    upper_ref[...] = jnp.full(upper_ref.shape, side, jnp.int32).astype(F32)


def compute_kernel(
    col_count, supernodes, slot, widths_ref, weights_ref, place_ref, straight_ref,
    own_wide_ref, *refs
):
    block_refs, refs = refs[:-7], refs[-7:]
    keep_d_ref, send_d_ref, keep_t_ref, send_t_ref, x_ref, y_ref, t_ref = refs
    packed_width = block_refs[0].shape[0] // 2
    local_rows = straight_ref.shape[1]
    strips = local_rows // slot
    w_real = weights_ref[0, 0]
    w_imag = weights_ref[0, 1]
    col_index = place_ref[1]

    panel = jnp.concatenate([ref[...] for ref in block_refs], axis=1)
    with_real = rows_by_rows(panel, straight_ref[0])
    with_imag = rows_by_rows(panel, straight_ref[1])
    u_real = with_imag[packed_width:] - with_real[:packed_width]
    u_imag = -(with_real[packed_width:] + with_imag[:packed_width])
    weighted = w_real * u_real - w_imag * u_imag
    turned = w_real * u_imag + w_imag * u_real

    half = packed_width // 2
    upper = (col_index & (col_count // 2)) != 0
    keep_d_ref[...] = jnp.where(upper, weighted[half:], weighted[:half])
    send_d_ref[...] = jnp.where(upper, weighted[:half], weighted[half:])

    for ref, value in ((x_ref, weighted), (y_ref, turned)):
        for s in range(strips):
            ref[s, :packed_width] = value[:, s * slot:(s + 1) * slot]
            ref[s, packed_width:] = jnp.zeros((slot, slot), F32)

    offsets = offsets_of(widths_ref, supernodes)
    for k in range(supernodes):
        right = jnp.concatenate(
            [ref[s, pl.ds(offsets[k], slot), :] for ref in (x_ref, y_ref) for s in range(strips)],
            axis=1,
        )
        high = right.astype(BF16)
        low = (right - high.astype(F32)).astype(BF16)
        product = rows_by_rows(
            own_wide_ref[k * slot:(k + 1) * slot, :], jnp.concatenate([high, low], axis=0)
        )
        t_ref[pl.ds(offsets[k], slot), :] = product[:, :slot] + product[:, slot:]
    keep_t_ref[...] = jnp.where(upper, t_ref[half:2 * half], t_ref[:half])
    send_t_ref[...] = jnp.where(upper, t_ref[:half], t_ref[half:2 * half])


def picked(pick_ref, value):
    high = value.astype(BF16)
    low = (value - high.astype(F32)).astype(BF16)
    return jnp.dot(pick_ref[...], high, preferred_element_type=F32) + jnp.dot(
        pick_ref[...], low, preferred_element_type=F32
    )


def expand_kernel(
    pick_d_ref, pick_t_ref, keep_ref, upper_ref, mine_d_ref, other_d_ref, mine_t_ref, other_t_ref,
    mine_term_ref, other_term_ref, density_ref, diagonal_ref,
):
    density_ref[...] = picked(pick_d_ref, jnp.concatenate([mine_d_ref[...], other_d_ref[...]], axis=0))
    product = picked(pick_t_ref, jnp.concatenate([mine_t_ref[...], other_t_ref[...]], axis=0))
    rows = mine_term_ref.shape[0]
    upper = upper_ref[:1, :] > 0.5
    terms = (
        jnp.where(upper, other_term_ref[...], mine_term_ref[...]),
        jnp.where(upper, mine_term_ref[...], other_term_ref[...]),
    )
    for side in range(2):
        part = slice(side * rows, (side + 1) * rows)
        diagonal_ref[part] = terms[side] - jnp.where(keep_ref[part] > 0.5, product[part], 0.0)


def bits_of(count):
    return [1 << k for k in range(count.bit_length() - 1)]


def swap(value, axis, bit):
    return lax.ppermute(value, axis, [(i, i ^ bit) for i in range(lax.axis_size(axis))])


def tree_sum(terms):
    while len(terms) > 1:
        terms = [terms[j] + terms[j + 1] for j in range(0, len(terms), 2)]
    return terms[0]


def sum_direct(value, axis):
    return tree_sum([value] + [swap(value, axis, j) for j in range(1, lax.axis_size(axis))])


def scatter_rest(value, axis):
    index = lax.axis_index(axis)
    for bit in bits_of(lax.axis_size(axis))[:-1][::-1]:
        half = value.shape[0] // 2
        upper = (index & bit) != 0
        keep = jnp.where(upper, value[half:], value[:half])
        value = keep + swap(jnp.where(upper, value[:half], value[half:]), axis, bit)
    return value


def gather_but_last(value, axis):
    index = lax.axis_index(axis)
    for bit in bits_of(lax.axis_size(axis))[:-1]:
        other = swap(value, axis, bit)
        upper = (index & bit) != 0
        value = jnp.concatenate(
            [jnp.where(upper, other, value), jnp.where(upper, value, other)], axis=0
        )
    return value


def per_device(found_inverse, l_panel, block_pattern, sup_widths, diag_inverse, pole_weights):
    slot = diag_inverse.shape[-1]
    total_cols = l_panel.shape[-1]
    supernodes = total_cols // slot
    packed_width = slot + (supernodes - 1) * (slot // 2)
    half = packed_width // 2
    local_rows = found_inverse.shape[2]
    block = l_panel.shape[2]
    row_count = lax.axis_size("row")
    col_count = lax.axis_size("col")
    top = col_count // 2
    place = jnp.stack([lax.axis_index("row"), lax.axis_index("col")]).astype(jnp.int32)

    packed = pl.pallas_call(
        functools.partial(pack_kernel, supernodes, slot),
        in_specs=[SMEM_SPEC, SMEM_SPEC, VMEM_SPEC],
        out_specs=VMEM_SPEC,
        out_shape=jax.ShapeDtypeStruct((2 * packed_width, block), BF16),
        name="pack",
    )(block_pattern, sup_widths, l_panel[0])

    blocks = {0: packed}
    for other in range(1, row_count):
        blocks[other] = swap(packed, "row", other)
    own = [packed] + [swap(packed, "col", other) for other in range(1, col_count)]

    straight, own_wide, term, *picks = pl.pallas_call(
        functools.partial(prepare_kernel, (row_count, col_count)),
        in_specs=[SMEM_SPEC] * 3 + [VMEM_SPEC] * (2 + col_count),
        out_specs=[VMEM_SPEC] * 7,
        out_shape=[
            jax.ShapeDtypeStruct((2, local_rows, row_count * block), BF16),
            jax.ShapeDtypeStruct((total_cols, 2 * local_rows), BF16),
            jax.ShapeDtypeStruct((total_cols // col_count, slot), F32),
            jax.ShapeDtypeStruct((total_cols // col_count, packed_width), BF16),
            jax.ShapeDtypeStruct((total_cols, packed_width), BF16),
            jax.ShapeDtypeStruct((total_cols, slot), F32),
            jax.ShapeDtypeStruct((8, slot), F32),
        ],
        compiler_params=PARAMS,
        cost_estimate=pl.CostEstimate(
            flops=4 * 256 * local_rows * row_count * block,
            bytes_accessed=8 * local_rows * row_count * block,
            transcendentals=0,
        ),
        name="prepare",
    )(
        sup_widths, pole_weights, place,
        found_inverse.reshape(2 * local_rows * row_count, block), diag_inverse[0], *own,
    )
    term = sum_direct(term, "pole")

    keep_d, send_d, keep_t, send_t = pl.pallas_call(
        functools.partial(compute_kernel, col_count, supernodes, slot),
        in_specs=[SMEM_SPEC] * 3 + [VMEM_SPEC] * (2 + row_count),
        out_specs=[VMEM_SPEC] * 4,
        out_shape=[jax.ShapeDtypeStruct((half, local_rows), F32)] * 2
        + [jax.ShapeDtypeStruct((half, slot), F32)] * 2,
        scratch_shapes=[
            pltpu.VMEM((local_rows // slot, packed_width + slot, slot), F32),
            pltpu.VMEM((local_rows // slot, packed_width + slot, slot), F32),
            pltpu.VMEM((packed_width + slot, slot), F32),
        ],
        compiler_params=PARAMS,
        name="compute",
    )(
        sup_widths, pole_weights, place, straight, own_wide,
        *[blocks[other] for other in range(row_count)],
    )

    tie = lax.optimization_barrier
    products, send_d, term = tie((keep_t + swap(send_t, "col", top), send_d, term))
    term = gather_but_last(term, "col")
    products = scatter_rest(products, "col")
    for bit in bits_of(row_count)[::-1]:
        products = products + swap(products, "row", 2 * bit - 1)
    density = scatter_rest(keep_d + swap(send_d, "col", top), "col")
    density = sum_direct(density, "pole")
    products = sum_direct(products, "pole")
    density = gather_but_last(density, "col")
    products = gather_but_last(products, "col")

    return pl.pallas_call(
        expand_kernel,
        in_specs=[VMEM_SPEC] * 10,
        out_specs=[VMEM_SPEC] * 2,
        out_shape=[
            jax.ShapeDtypeStruct((total_cols // col_count, local_rows), F32),
            jax.ShapeDtypeStruct((total_cols, slot), F32),
        ],
        compiler_params=PARAMS,
        name="expand",
    )(
        *picks, density, swap(density, "col", top), products, swap(products, "col", top),
        term, swap(term, "col", top),
    )


def solution(mesh):
    in_specs = (
        P("pole", None, "row", None, "col", None),
        P("pole", None, ("row", "col"), None),
        P(("row", "col"), None),
        P(),
        P("pole", None, None, None),
        P("pole", None),
    )
    out_specs = (P("col", "row"), P())
    return jax.shard_map(
        per_device, mesh=mesh, in_specs=in_specs, out_specs=out_specs, check_vma=False
    )
```

```python
import functools

import jax
import jax.numpy as jnp
from jax import lax
from jax.experimental import pallas as pl
from jax.experimental.pallas import tpu as pltpu
from jax.sharding import PartitionSpec as P

F32 = jnp.float32
BF16 = jnp.bfloat16
VMEM_SPEC = pl.BlockSpec(memory_space=pltpu.VMEM)
SMEM_SPEC = pl.BlockSpec(memory_space=pltpu.SMEM)
PARAMS = pltpu.CompilerParams(vmem_limit_bytes=48 * 1024 * 1024)


def rows_by_rows(left, right):
    return lax.dot_general(left, right, (((1,), (1,)), ((), ())), preferred_element_type=F32)


def offsets_of(widths_ref, supernodes):
    offsets = [0]
    for k in range(supernodes):
        offsets.append(offsets[-1] + widths_ref[k])
    return offsets


def pack_kernel(supernodes, slot, pattern_ref, widths_ref, panel_ref, packed_ref):
    packed_width = packed_ref.shape[0] // 2
    offsets = offsets_of(widths_ref, supernodes)
    lane = lax.broadcasted_iota(jnp.int32, (1, slot), 1)
    place = []
    for k in range(supernodes):
        valid = (lane < widths_ref[k]) & (pattern_ref[0, k] == 1)
        place.append(jnp.where(valid, offsets[k] + lane, -1))
    place = jnp.concatenate(place, axis=1)
    target = lax.broadcasted_iota(jnp.int32, (packed_width, supernodes * slot), 0)
    select = jnp.where(target == place, 1.0, 0.0).astype(BF16)
    block = packed_ref.shape[1]
    both = rows_by_rows(select, panel_ref[...]).astype(BF16)
    for part in range(2):
        packed_ref[part * packed_width:(part + 1) * packed_width, :] = both[
            :, part * block:(part + 1) * block
        ]


def prepare_kernel(
    counts, widths_ref, weights_ref, place_ref, inverse_ref, diag_ref, *refs
):
    row_count, col_count = counts
    own_refs, refs = refs[:col_count], refs[col_count:]
    straight_ref, own_wide_ref, term_ref, pick_d_ref, pick_t_ref, keep_ref, upper_ref = refs
    packed_width = own_refs[0].shape[0] // 2
    col_index = place_ref[1]
    block = inverse_ref.shape[1]
    local_rows = straight_ref.shape[1]
    row_index = place_ref[0]
    group = max(8, 256 // row_count)
    span = group * row_count
    row_id = lax.broadcasted_iota(jnp.int32, (span, span), 0)
    col_id = lax.broadcasted_iota(jnp.int32, (span, span), 1)
    source = (row_id % group) * row_count + ((row_id // group) ^ row_index)
    order = jnp.where(col_id == source, 1.0, 0.0).astype(BF16)
    for part in range(2):
        for chunk in range(local_rows // group):
            base = (part * local_rows + chunk * group) * row_count
            mixed = inverse_ref[base:base + span, :]
            sorted_rows = jnp.dot(order, mixed, preferred_element_type=F32).astype(BF16)
            for owner in range(row_count):
                straight_ref[
                    part, chunk * group:(chunk + 1) * group, owner * block:(owner + 1) * block
                ] = sorted_rows[owner * group:(owner + 1) * group]
    own = []
    for c in range(col_count):
        block_of = own_refs[0][...]
        for other in range(1, col_count):
            block_of = jnp.where((col_index ^ c) == other, own_refs[other][...], block_of)
        own.append(block_of)
    own = jnp.concatenate(own, axis=1)
    total_cols = own_wide_ref.shape[0]
    slot = diag_ref.shape[2]
    offsets = offsets_of(widths_ref, total_cols // slot)
    row_in_slot = lax.broadcasted_iota(jnp.int32, (slot, packed_width), 0)
    column = lax.broadcasted_iota(jnp.int32, (slot, packed_width), 1)
    for k in range(total_cols // slot):
        chosen = (column == row_in_slot + offsets[k]) & (row_in_slot < widths_ref[k])
        chosen = jnp.where(chosen, 1.0, 0.0).astype(BF16)
        for part, sign in enumerate((1.0, -1.0)):
            rows = own[part * packed_width:(part + 1) * packed_width]
            own_wide_ref[k * slot:(k + 1) * slot, part * local_rows:(part + 1) * local_rows] = (
                sign * jnp.dot(chosen, rows, preferred_element_type=F32)
            ).astype(BF16)
    per_col = term_ref.shape[0]
    first = pl.multiple_of(col_index * per_col, per_col)
    term_ref[...] = weights_ref[0, 0] * diag_ref[0, pl.ds(first, per_col), :].astype(
        F32
    ) - weights_ref[0, 1] * diag_ref[1, pl.ds(first, per_col), :].astype(F32)
    side = jnp.where((col_index & (col_count // 2)) != 0, 1, 0)
    half = packed_width // 2
    position = jnp.where(column < half, column + side * half, column - side * half)
    lane = lax.broadcasted_iota(jnp.int32, (slot, slot), 1)
    for k in range(total_cols // slot):
        chosen = (position == row_in_slot + offsets[k]) & (row_in_slot < widths_ref[k])
        rows = slice(k * slot, (k + 1) * slot)
        pick_t_ref[rows, :] = jnp.where(chosen, 1.0, 0.0).astype(BF16)
        keep_ref[rows, :] = jnp.where(
            (lane < widths_ref[k]) & (row_in_slot[:, :slot] < widths_ref[k]), 1.0, 0.0
        )
    size = min(per_col, slot)
    for part in range(per_col // size):
        begin = col_index * per_col + part * size
        start, count = 0, 0
        for k in range(total_cols // slot):
            start = start + jnp.where(k < begin // slot, widths_ref[k], 0)
            count = count + jnp.where(k == begin // slot, widths_ref[k], 0)
        within = row_in_slot[:size] + begin % slot
        chosen = (position[:size] == within + start) & (within < count)
        pick_d_ref[part * size:(part + 1) * size, :] = jnp.where(chosen, 1.0, 0.0).astype(BF16)
    upper_ref[...] = jnp.full(upper_ref.shape, side, jnp.int32).astype(F32)


def compute_kernel(
    col_count, supernodes, slot, widths_ref, weights_ref, place_ref, straight_ref,
    own_wide_ref, *refs
):
    block_refs, refs = refs[:-7], refs[-7:]
    keep_d_ref, send_d_ref, keep_t_ref, send_t_ref, x_ref, y_ref, t_ref = refs
    packed_width = block_refs[0].shape[0] // 2
    local_rows = straight_ref.shape[1]
    strips = local_rows // slot
    w_real = weights_ref[0, 0]
    w_imag = weights_ref[0, 1]
    col_index = place_ref[1]

    panel = jnp.concatenate([ref[...] for ref in block_refs], axis=1)
    with_real = rows_by_rows(panel, straight_ref[0])
    with_imag = rows_by_rows(panel, straight_ref[1])
    u_real = with_imag[packed_width:] - with_real[:packed_width]
    u_imag = -(with_real[packed_width:] + with_imag[:packed_width])
    weighted = w_real * u_real - w_imag * u_imag
    turned = w_real * u_imag + w_imag * u_real

    half = packed_width // 2
    upper = (col_index & (col_count // 2)) != 0
    keep_d_ref[...] = jnp.where(upper, weighted[half:], weighted[:half])
    send_d_ref[...] = jnp.where(upper, weighted[:half], weighted[half:])

    for ref, value in ((x_ref, weighted), (y_ref, turned)):
        for s in range(strips):
            ref[s, :packed_width] = value[:, s * slot:(s + 1) * slot]
            ref[s, packed_width:] = jnp.zeros((slot, slot), F32)

    offsets = offsets_of(widths_ref, supernodes)
    for k in range(supernodes):
        right = jnp.concatenate(
            [ref[s, pl.ds(offsets[k], slot), :] for ref in (x_ref, y_ref) for s in range(strips)],
            axis=1,
        )
        high = right.astype(BF16)
        low = (right - high.astype(F32)).astype(BF16)
        product = rows_by_rows(
            own_wide_ref[k * slot:(k + 1) * slot, :], jnp.concatenate([high, low], axis=0)
        )
        t_ref[pl.ds(offsets[k], slot), :] = product[:, :slot] + product[:, slot:]
    keep_t_ref[...] = jnp.where(upper, t_ref[half:2 * half], t_ref[:half])
    send_t_ref[...] = jnp.where(upper, t_ref[:half], t_ref[half:2 * half])


def picked(pick_ref, value):
    high = value.astype(BF16)
    low = (value - high.astype(F32)).astype(BF16)
    return jnp.dot(pick_ref[...], high, preferred_element_type=F32) + jnp.dot(
        pick_ref[...], low, preferred_element_type=F32
    )


def expand_kernel(
    pick_d_ref, pick_t_ref, keep_ref, upper_ref, mine_d_ref, other_d_ref, mine_t_ref, other_t_ref,
    mine_term_ref, other_term_ref, density_ref, diagonal_ref,
):
    density_ref[...] = picked(pick_d_ref, jnp.concatenate([mine_d_ref[...], other_d_ref[...]], axis=0))
    product = picked(pick_t_ref, jnp.concatenate([mine_t_ref[...], other_t_ref[...]], axis=0))
    rows = mine_term_ref.shape[0]
    upper = upper_ref[:1, :] > 0.5
    terms = (
        jnp.where(upper, other_term_ref[...], mine_term_ref[...]),
        jnp.where(upper, mine_term_ref[...], other_term_ref[...]),
    )
    for side in range(2):
        part = slice(side * rows, (side + 1) * rows)
        diagonal_ref[part] = terms[side] - jnp.where(keep_ref[part] > 0.5, product[part], 0.0)


def bits_of(count):
    return [1 << k for k in range(count.bit_length() - 1)]


def swap(value, axis, bit):
    return lax.ppermute(value, axis, [(i, i ^ bit) for i in range(lax.axis_size(axis))])


def tree_sum(terms):
    while len(terms) > 1:
        terms = [terms[j] + terms[j + 1] for j in range(0, len(terms), 2)]
    return terms[0]


def sum_direct(value, axis):
    return tree_sum([value] + [swap(value, axis, j) for j in range(1, lax.axis_size(axis))])


def scatter_rest(value, axis):
    index = lax.axis_index(axis)
    for bit in bits_of(lax.axis_size(axis))[:-1][::-1]:
        half = value.shape[0] // 2
        upper = (index & bit) != 0
        keep = jnp.where(upper, value[half:], value[:half])
        value = keep + swap(jnp.where(upper, value[:half], value[half:]), axis, bit)
    return value


def gather_but_last(value, axis):
    index = lax.axis_index(axis)
    for bit in bits_of(lax.axis_size(axis))[:-1]:
        other = swap(value, axis, bit)
        upper = (index & bit) != 0
        value = jnp.concatenate(
            [jnp.where(upper, other, value), jnp.where(upper, value, other)], axis=0
        )
    return value


def per_device(found_inverse, l_panel, block_pattern, sup_widths, diag_inverse, pole_weights):
    slot = diag_inverse.shape[-1]
    total_cols = l_panel.shape[-1]
    supernodes = total_cols // slot
    packed_width = slot + (supernodes - 1) * (slot // 2)
    half = packed_width // 2
    local_rows = found_inverse.shape[2]
    block = l_panel.shape[2]
    row_count = lax.axis_size("row")
    col_count = lax.axis_size("col")
    top = col_count // 2
    place = jnp.stack([lax.axis_index("row"), lax.axis_index("col")]).astype(jnp.int32)

    packed = pl.pallas_call(
        functools.partial(pack_kernel, supernodes, slot),
        in_specs=[SMEM_SPEC, SMEM_SPEC, VMEM_SPEC],
        out_specs=VMEM_SPEC,
        out_shape=jax.ShapeDtypeStruct((2 * packed_width, block), BF16),
        name="pack",
    )(block_pattern, sup_widths, l_panel[0].reshape(2 * block, total_cols))

    blocks = {0: packed}
    for other in range(1, row_count):
        blocks[other] = swap(packed, "row", other)
    own = [packed] + [swap(packed, "col", other) for other in range(1, col_count)]

    straight, own_wide, term, *picks = pl.pallas_call(
        functools.partial(prepare_kernel, (row_count, col_count)),
        in_specs=[SMEM_SPEC] * 3 + [VMEM_SPEC] * (2 + col_count),
        out_specs=[VMEM_SPEC] * 7,
        out_shape=[
            jax.ShapeDtypeStruct((2, local_rows, row_count * block), BF16),
            jax.ShapeDtypeStruct((total_cols, 2 * local_rows), BF16),
            jax.ShapeDtypeStruct((total_cols // col_count, slot), F32),
            jax.ShapeDtypeStruct((total_cols // col_count, packed_width), BF16),
            jax.ShapeDtypeStruct((total_cols, packed_width), BF16),
            jax.ShapeDtypeStruct((total_cols, slot), F32),
            jax.ShapeDtypeStruct((8, slot), F32),
        ],
        compiler_params=PARAMS,
        cost_estimate=pl.CostEstimate(
            flops=4 * 256 * local_rows * row_count * block,
            bytes_accessed=8 * local_rows * row_count * block,
            transcendentals=0,
        ),
        name="prepare",
    )(
        sup_widths, pole_weights, place,
        found_inverse.reshape(2 * local_rows * row_count, block), diag_inverse[0], *own,
    )
    term = sum_direct(term, "pole")

    keep_d, send_d, keep_t, send_t = pl.pallas_call(
        functools.partial(compute_kernel, col_count, supernodes, slot),
        in_specs=[SMEM_SPEC] * 3 + [VMEM_SPEC] * (2 + row_count),
        out_specs=[VMEM_SPEC] * 4,
        out_shape=[jax.ShapeDtypeStruct((half, local_rows), F32)] * 2
        + [jax.ShapeDtypeStruct((half, slot), F32)] * 2,
        scratch_shapes=[
            pltpu.VMEM((local_rows // slot, packed_width + slot, slot), F32),
            pltpu.VMEM((local_rows // slot, packed_width + slot, slot), F32),
            pltpu.VMEM((packed_width + slot, slot), F32),
        ],
        compiler_params=PARAMS,
        name="compute",
    )(
        sup_widths, pole_weights, place, straight, own_wide,
        *[blocks[other] for other in range(row_count)],
    )

    tie = lax.optimization_barrier
    products, send_d, term = tie((keep_t + swap(send_t, "col", top), send_d, term))
    term = gather_but_last(term, "col")
    products = scatter_rest(products, "col")
    for bit in bits_of(row_count):
        products = products + swap(products, "row", bit)
    density = scatter_rest(keep_d + swap(send_d, "col", top), "col")
    density = sum_direct(density, "pole")
    products = sum_direct(products, "pole")
    density = gather_but_last(density, "col")
    products = gather_but_last(products, "col")

    return pl.pallas_call(
        expand_kernel,
        in_specs=[VMEM_SPEC] * 10,
        out_specs=[VMEM_SPEC] * 2,
        out_shape=[
            jax.ShapeDtypeStruct((total_cols // col_count, local_rows), F32),
            jax.ShapeDtypeStruct((total_cols, slot), F32),
        ],
        compiler_params=PARAMS,
        name="expand",
    )(
        *picks, density, swap(density, "col", top), products, swap(products, "col", top),
        term, swap(term, "col", top),
    )


def solution(mesh):
    in_specs = (
        P("pole", None, "row", None, "col", None),
        P("pole", None, ("row", "col"), None),
        P(("row", "col"), None),
        P(),
        P("pole", None, None, None),
        P("pole", None),
    )
    out_specs = (P("col", "row"), P())
    return jax.shard_map(
        per_device, mesh=mesh, in_specs=in_specs, out_specs=out_specs, check_vma=False
    )
```

```python
import functools

import jax
import jax.numpy as jnp
from jax import lax
from jax.experimental import pallas as pl
from jax.experimental.pallas import tpu as pltpu
from jax.sharding import PartitionSpec as P

F32 = jnp.float32
BF16 = jnp.bfloat16
VMEM_SPEC = pl.BlockSpec(memory_space=pltpu.VMEM)
SMEM_SPEC = pl.BlockSpec(memory_space=pltpu.SMEM)
PARAMS = pltpu.CompilerParams(vmem_limit_bytes=48 * 1024 * 1024)


def rows_by_rows(left, right):
    return lax.dot_general(left, right, (((1,), (1,)), ((), ())), preferred_element_type=F32)


def offsets_of(widths_ref, supernodes):
    offsets = [0]
    for k in range(supernodes):
        offsets.append(offsets[-1] + widths_ref[k])
    return offsets


def pack_kernel(supernodes, slot, pattern_ref, widths_ref, panel_ref, packed_ref):
    packed_width = packed_ref.shape[0] // 2
    offsets = offsets_of(widths_ref, supernodes)
    lane = lax.broadcasted_iota(jnp.int32, (1, slot), 1)
    place = []
    for k in range(supernodes):
        valid = (lane < widths_ref[k]) & (pattern_ref[0, k] == 1)
        place.append(jnp.where(valid, offsets[k] + lane, -1))
    place = jnp.concatenate(place, axis=1)
    target = lax.broadcasted_iota(jnp.int32, (packed_width, supernodes * slot), 0)
    select = jnp.where(target == place, 1.0, 0.0).astype(BF16)
    for part in range(2):
        packed_ref[part * packed_width:(part + 1) * packed_width, :] = rows_by_rows(
            select, panel_ref[part]
        ).astype(BF16)


def prepare_kernel(
    counts, widths_ref, weights_ref, place_ref, inverse_ref, diag_ref, *refs
):
    row_count, col_count = counts
    own_refs, refs = refs[:col_count], refs[col_count:]
    straight_ref, own_wide_ref, term_ref, pick_d_ref, mine_ref, other_ref, keep_ref, upper_ref = refs
    packed_width = own_refs[0].shape[0] // 2
    col_index = place_ref[1]
    block = inverse_ref.shape[1]
    local_rows = straight_ref.shape[1]
    row_index = place_ref[0]
    group = max(8, 256 // row_count)
    span = group * row_count
    row_id = lax.broadcasted_iota(jnp.int32, (span, span), 0)
    col_id = lax.broadcasted_iota(jnp.int32, (span, span), 1)
    source = (row_id % group) * row_count + ((row_id // group) ^ row_index)
    order = jnp.where(col_id == source, 1.0, 0.0).astype(BF16)
    for part in range(2):
        for chunk in range(local_rows // group):
            base = (part * local_rows + chunk * group) * row_count
            mixed = inverse_ref[base:base + span, :]
            sorted_rows = jnp.dot(order, mixed, preferred_element_type=F32).astype(BF16)
            for owner in range(row_count):
                straight_ref[
                    part, chunk * group:(chunk + 1) * group, owner * block:(owner + 1) * block
                ] = sorted_rows[owner * group:(owner + 1) * group]
    own = []
    for c in range(col_count):
        block_of = own_refs[0][...]
        for other in range(1, col_count):
            block_of = jnp.where((col_index ^ c) == other, own_refs[other][...], block_of)
        own.append(block_of)
    own = jnp.concatenate(own, axis=1)
    total_cols = own_wide_ref.shape[0]
    slot = diag_ref.shape[2]
    offsets = offsets_of(widths_ref, total_cols // slot)
    row_in_slot = lax.broadcasted_iota(jnp.int32, (slot, packed_width), 0)
    column = lax.broadcasted_iota(jnp.int32, (slot, packed_width), 1)
    for k in range(total_cols // slot):
        chosen = (column == row_in_slot + offsets[k]) & (row_in_slot < widths_ref[k])
        chosen = jnp.where(chosen, 1.0, 0.0).astype(BF16)
        for part, sign in enumerate((1.0, -1.0)):
            rows = own[part * packed_width:(part + 1) * packed_width]
            own_wide_ref[k * slot:(k + 1) * slot, part * local_rows:(part + 1) * local_rows] = (
                sign * jnp.dot(chosen, rows, preferred_element_type=F32)
            ).astype(BF16)
    per_col = term_ref.shape[0]
    first = pl.multiple_of(col_index * per_col, per_col)
    term_ref[...] = weights_ref[0, 0] * diag_ref[0, pl.ds(first, per_col), :].astype(
        F32
    ) - weights_ref[0, 1] * diag_ref[1, pl.ds(first, per_col), :].astype(F32)
    side = jnp.where((col_index & (col_count // 2)) != 0, 1, 0)
    half = packed_width // 2
    position = jnp.where(column < half, column + side * half, column - side * half)
    lane = lax.broadcasted_iota(jnp.int32, (slot, slot), 1)
    for k in range(total_cols // slot):
        rows = slice(k * slot, (k + 1) * slot)
        for ref, at in ((mine_ref, side), (other_ref, 1 - side)):
            inside = row_in_slot[:, :half]
            chosen = (column[:, :half] + at * half == inside + offsets[k]) & (inside < widths_ref[k])
            ref[rows, :] = jnp.where(chosen, 1.0, 0.0).astype(BF16)
        keep_ref[rows, :] = jnp.where(
            (lane < widths_ref[k]) & (row_in_slot[:, :slot] < widths_ref[k]), 1.0, 0.0
        )
    size = min(per_col, slot)
    for part in range(per_col // size):
        begin = col_index * per_col + part * size
        start, count = 0, 0
        for k in range(total_cols // slot):
            start = start + jnp.where(k < begin // slot, widths_ref[k], 0)
            count = count + jnp.where(k == begin // slot, widths_ref[k], 0)
        within = row_in_slot[:size] + begin % slot
        chosen = (position[:size] == within + start) & (within < count)
        pick_d_ref[part * size:(part + 1) * size, :] = jnp.where(chosen, 1.0, 0.0).astype(BF16)
    upper_ref[...] = jnp.full(upper_ref.shape, side, jnp.int32).astype(F32)


def compute_kernel(
    col_count, supernodes, slot, widths_ref, weights_ref, place_ref, straight_ref,
    own_wide_ref, *refs
):
    block_refs, refs = refs[:-7], refs[-7:]
    keep_d_ref, send_d_ref, keep_t_ref, send_t_ref, x_ref, y_ref, t_ref = refs
    packed_width = block_refs[0].shape[0] // 2
    local_rows = straight_ref.shape[1]
    strips = local_rows // slot
    w_real = weights_ref[0, 0]
    w_imag = weights_ref[0, 1]
    col_index = place_ref[1]

    panel = jnp.concatenate([ref[...] for ref in block_refs], axis=1)
    with_real = rows_by_rows(panel, straight_ref[0])
    with_imag = rows_by_rows(panel, straight_ref[1])
    u_real = with_imag[packed_width:] - with_real[:packed_width]
    u_imag = -(with_real[packed_width:] + with_imag[:packed_width])
    weighted = w_real * u_real - w_imag * u_imag
    turned = w_real * u_imag + w_imag * u_real

    half = packed_width // 2
    upper = (col_index & (col_count // 2)) != 0
    keep_d_ref[...] = jnp.where(upper, weighted[half:], weighted[:half])
    send_d_ref[...] = jnp.where(upper, weighted[:half], weighted[half:])

    for ref, value in ((x_ref, weighted), (y_ref, turned)):
        for s in range(strips):
            ref[s, :packed_width] = value[:, s * slot:(s + 1) * slot]
            ref[s, packed_width:] = jnp.zeros((slot, slot), F32)

    offsets = offsets_of(widths_ref, supernodes)
    for k in range(supernodes):
        right = jnp.concatenate(
            [ref[s, pl.ds(offsets[k], slot), :] for ref in (x_ref, y_ref) for s in range(strips)],
            axis=1,
        )
        high = right.astype(BF16)
        low = (right - high.astype(F32)).astype(BF16)
        product = rows_by_rows(
            own_wide_ref[k * slot:(k + 1) * slot, :], jnp.concatenate([high, low], axis=0)
        )
        t_ref[pl.ds(offsets[k], slot), :] = product[:, :slot] + product[:, slot:]
    keep_t_ref[...] = jnp.where(upper, t_ref[half:2 * half], t_ref[:half])
    send_t_ref[...] = jnp.where(upper, t_ref[:half], t_ref[half:2 * half])


def picked(pick_ref, value):
    high = value.astype(BF16)
    low = (value - high.astype(F32)).astype(BF16)
    return jnp.dot(pick_ref[...], high, preferred_element_type=F32) + jnp.dot(
        pick_ref[...], low, preferred_element_type=F32
    )


def expand_kernel(
    pick_d_ref, pick_ref, keep_ref, upper_ref, mine_d_ref, other_d_ref, mine_t_ref,
    mine_term_ref, other_term_ref, density_ref, diagonal_ref,
):
    density_ref[...] = picked(pick_d_ref, jnp.concatenate([mine_d_ref[...], other_d_ref[...]], axis=0))
    product = picked(pick_ref, mine_t_ref[...])
    rows = mine_term_ref.shape[0]
    upper = upper_ref[:1, :] > 0.5
    terms = (
        jnp.where(upper, other_term_ref[...], mine_term_ref[...]),
        jnp.where(upper, mine_term_ref[...], other_term_ref[...]),
    )
    for side in range(2):
        part = slice(side * rows, (side + 1) * rows)
        diagonal_ref[part] = terms[side] - jnp.where(keep_ref[part] > 0.5, product[part], 0.0)


def finish_kernel(pick_ref, keep_ref, other_t_ref, partial_ref, diagonal_ref):
    product = picked(pick_ref, other_t_ref[...])
    diagonal_ref[...] = partial_ref[...] - jnp.where(keep_ref[...] > 0.5, product, 0.0)


def bits_of(count):
    return [1 << k for k in range(count.bit_length() - 1)]


def swap(value, axis, bit):
    return lax.ppermute(value, axis, [(i, i ^ bit) for i in range(lax.axis_size(axis))])


def tree_sum(terms):
    while len(terms) > 1:
        terms = [terms[j] + terms[j + 1] for j in range(0, len(terms), 2)]
    return terms[0]


def sum_direct(value, axis):
    return tree_sum([value] + [swap(value, axis, j) for j in range(1, lax.axis_size(axis))])


def scatter_rest(value, axis):
    index = lax.axis_index(axis)
    for bit in bits_of(lax.axis_size(axis))[:-1][::-1]:
        half = value.shape[0] // 2
        upper = (index & bit) != 0
        keep = jnp.where(upper, value[half:], value[:half])
        value = keep + swap(jnp.where(upper, value[:half], value[half:]), axis, bit)
    return value


def gather_but_last(value, axis):
    index = lax.axis_index(axis)
    for bit in bits_of(lax.axis_size(axis))[:-1]:
        other = swap(value, axis, bit)
        upper = (index & bit) != 0
        value = jnp.concatenate(
            [jnp.where(upper, other, value), jnp.where(upper, value, other)], axis=0
        )
    return value


def per_device(found_inverse, l_panel, block_pattern, sup_widths, diag_inverse, pole_weights):
    slot = diag_inverse.shape[-1]
    total_cols = l_panel.shape[-1]
    supernodes = total_cols // slot
    packed_width = slot + (supernodes - 1) * (slot // 2)
    half = packed_width // 2
    local_rows = found_inverse.shape[2]
    block = l_panel.shape[2]
    row_count = lax.axis_size("row")
    col_count = lax.axis_size("col")
    top = col_count // 2
    place = jnp.stack([lax.axis_index("row"), lax.axis_index("col")]).astype(jnp.int32)

    packed = pl.pallas_call(
        functools.partial(pack_kernel, supernodes, slot),
        in_specs=[SMEM_SPEC, SMEM_SPEC, VMEM_SPEC],
        out_specs=VMEM_SPEC,
        out_shape=jax.ShapeDtypeStruct((2 * packed_width, block), BF16),
        name="pack",
    )(block_pattern, sup_widths, l_panel[0])

    blocks = {0: packed}
    for other in range(1, row_count):
        blocks[other] = swap(packed, "row", other)
    own = [packed] + [swap(packed, "col", other) for other in range(1, col_count)]

    straight, own_wide, term, pick_d, pick_mine, pick_other, keep, upper = pl.pallas_call(
        functools.partial(prepare_kernel, (row_count, col_count)),
        in_specs=[SMEM_SPEC] * 3 + [VMEM_SPEC] * (2 + col_count),
        out_specs=[VMEM_SPEC] * 8,
        out_shape=[
            jax.ShapeDtypeStruct((2, local_rows, row_count * block), BF16),
            jax.ShapeDtypeStruct((total_cols, 2 * local_rows), BF16),
            jax.ShapeDtypeStruct((total_cols // col_count, slot), F32),
            jax.ShapeDtypeStruct((total_cols // col_count, packed_width), BF16),
            jax.ShapeDtypeStruct((total_cols, packed_width // 2), BF16),
            jax.ShapeDtypeStruct((total_cols, packed_width // 2), BF16),
            jax.ShapeDtypeStruct((total_cols, slot), F32),
            jax.ShapeDtypeStruct((8, slot), F32),
        ],
        compiler_params=PARAMS,
        cost_estimate=pl.CostEstimate(
            flops=4 * 256 * local_rows * row_count * block,
            bytes_accessed=8 * local_rows * row_count * block,
            transcendentals=0,
        ),
        name="prepare",
    )(
        sup_widths, pole_weights, place,
        found_inverse.reshape(2 * local_rows * row_count, block), diag_inverse[0], *own,
    )
    term = sum_direct(term, "pole")

    keep_d, send_d, keep_t, send_t = pl.pallas_call(
        functools.partial(compute_kernel, col_count, supernodes, slot),
        in_specs=[SMEM_SPEC] * 3 + [VMEM_SPEC] * (2 + row_count),
        out_specs=[VMEM_SPEC] * 4,
        out_shape=[jax.ShapeDtypeStruct((half, local_rows), F32)] * 2
        + [jax.ShapeDtypeStruct((half, slot), F32)] * 2,
        scratch_shapes=[
            pltpu.VMEM((local_rows // slot, packed_width + slot, slot), F32),
            pltpu.VMEM((local_rows // slot, packed_width + slot, slot), F32),
            pltpu.VMEM((packed_width + slot, slot), F32),
        ],
        compiler_params=PARAMS,
        name="compute",
    )(
        sup_widths, pole_weights, place, straight, own_wide,
        *[blocks[other] for other in range(row_count)],
    )

    tie = lax.optimization_barrier
    products, send_d, term = tie((keep_t + swap(send_t, "col", top), send_d, term))
    term = gather_but_last(term, "col")
    products = scatter_rest(products, "col")
    for bit in bits_of(row_count)[::-1]:
        products = products + swap(products, "row", 2 * bit - 1)
    density = scatter_rest(keep_d + swap(send_d, "col", top), "col")
    density = sum_direct(density, "pole")
    products = sum_direct(products, "pole")
    density = gather_but_last(density, "col")
    products = gather_but_last(products, "col")

    density, partial = pl.pallas_call(
        expand_kernel,
        in_specs=[VMEM_SPEC] * 9,
        out_specs=[VMEM_SPEC] * 2,
        out_shape=[
            jax.ShapeDtypeStruct((total_cols // col_count, local_rows), F32),
            jax.ShapeDtypeStruct((total_cols, slot), F32),
        ],
        compiler_params=PARAMS,
        cost_estimate=pl.CostEstimate(
            flops=8 * total_cols * packed_width * (local_rows + slot),
            bytes_accessed=16 * total_cols * local_rows,
            transcendentals=0,
        ),
        name="expand",
    )(
        pick_d, pick_mine, keep, upper, density, swap(density, "col", top), products,
        term, swap(term, "col", top),
    )
    diagonal = pl.pallas_call(
        finish_kernel,
        in_specs=[VMEM_SPEC] * 4,
        out_specs=VMEM_SPEC,
        out_shape=jax.ShapeDtypeStruct((total_cols, slot), F32),
        compiler_params=PARAMS,
        name="finish",
    )(pick_other, keep, swap(products, "col", top), partial)
    return (density, diagonal)


def solution(mesh):
    in_specs = (
        P("pole", None, "row", None, "col", None),
        P("pole", None, ("row", "col"), None),
        P(("row", "col"), None),
        P(),
        P("pole", None, None, None),
        P("pole", None),
    )
    out_specs = (P("col", "row"), P())
    return jax.shard_map(
        per_device, mesh=mesh, in_specs=in_specs, out_specs=out_specs, check_vma=False
    )
```

```python
import functools

import jax
import jax.numpy as jnp
from jax import lax
from jax.experimental import pallas as pl
from jax.experimental.pallas import tpu as pltpu
from jax.sharding import PartitionSpec as P

F32 = jnp.float32
BF16 = jnp.bfloat16
VMEM_SPEC = pl.BlockSpec(memory_space=pltpu.VMEM)
SMEM_SPEC = pl.BlockSpec(memory_space=pltpu.SMEM)
PARAMS = pltpu.CompilerParams(vmem_limit_bytes=48 * 1024 * 1024)


def rows_by_rows(left, right):
    return lax.dot_general(left, right, (((1,), (1,)), ((), ())), preferred_element_type=F32)


def offsets_of(widths_ref, supernodes):
    offsets = [0]
    for k in range(supernodes):
        offsets.append(offsets[-1] + widths_ref[k])
    return offsets


def pack_kernel(supernodes, slot, pattern_ref, widths_ref, panel_ref, packed_ref):
    packed_width = packed_ref.shape[0] // 2
    offsets = offsets_of(widths_ref, supernodes)
    lane = lax.broadcasted_iota(jnp.int32, (1, slot), 1)
    place = []
    for k in range(supernodes):
        valid = (lane < widths_ref[k]) & (pattern_ref[0, k] == 1)
        place.append(jnp.where(valid, offsets[k] + lane, -1))
    place = jnp.concatenate(place, axis=1)
    target = lax.broadcasted_iota(jnp.int32, (packed_width, supernodes * slot), 0)
    select = jnp.where(target == place, 1.0, 0.0).astype(BF16)
    for part in range(2):
        packed_ref[part * packed_width:(part + 1) * packed_width, :] = rows_by_rows(
            select, panel_ref[part]
        ).astype(BF16)


def prepare_kernel(
    counts, widths_ref, weights_ref, place_ref, inverse_ref, diag_ref, *refs
):
    row_count, col_count = counts
    own_refs, refs = refs[:col_count], refs[col_count:]
    straight_ref, own_wide_ref, term_ref, pick_d_ref, mine_ref, other_ref, keep_ref, upper_ref = refs
    packed_width = own_refs[0].shape[0] // 2
    col_index = place_ref[1]
    block = inverse_ref.shape[1]
    local_rows = straight_ref.shape[1]
    row_index = place_ref[0]
    group = max(8, 256 // row_count)
    span = group * row_count
    row_id = lax.broadcasted_iota(jnp.int32, (span, span), 0)
    col_id = lax.broadcasted_iota(jnp.int32, (span, span), 1)
    source = (row_id % group) * row_count + ((row_id // group) ^ row_index)
    order = jnp.where(col_id == source, 1.0, 0.0).astype(BF16)
    for part in range(2):
        for chunk in range(local_rows // group):
            base = (part * local_rows + chunk * group) * row_count
            mixed = inverse_ref[base:base + span, :]
            sorted_rows = jnp.dot(order, mixed, preferred_element_type=F32).astype(BF16)
            for owner in range(row_count):
                straight_ref[
                    part, chunk * group:(chunk + 1) * group, owner * block:(owner + 1) * block
                ] = sorted_rows[owner * group:(owner + 1) * group]
    own = []
    for c in range(col_count):
        block_of = own_refs[0][...]
        for other in range(1, col_count):
            block_of = jnp.where((col_index ^ c) == other, own_refs[other][...], block_of)
        own.append(block_of)
    own = jnp.concatenate(own, axis=1)
    total_cols = own_wide_ref.shape[0]
    slot = diag_ref.shape[2]
    offsets = offsets_of(widths_ref, total_cols // slot)
    row_in_slot = lax.broadcasted_iota(jnp.int32, (slot, packed_width), 0)
    column = lax.broadcasted_iota(jnp.int32, (slot, packed_width), 1)
    for k in range(total_cols // slot):
        chosen = (column == row_in_slot + offsets[k]) & (row_in_slot < widths_ref[k])
        chosen = jnp.where(chosen, 1.0, 0.0).astype(BF16)
        for part, sign in enumerate((1.0, -1.0)):
            rows = own[part * packed_width:(part + 1) * packed_width]
            own_wide_ref[k * slot:(k + 1) * slot, part * local_rows:(part + 1) * local_rows] = (
                sign * jnp.dot(chosen, rows, preferred_element_type=F32)
            ).astype(BF16)
    per_col = term_ref.shape[0]
    first = pl.multiple_of(col_index * per_col, per_col)
    term_ref[...] = weights_ref[0, 0] * diag_ref[0, pl.ds(first, per_col), :].astype(
        F32
    ) - weights_ref[0, 1] * diag_ref[1, pl.ds(first, per_col), :].astype(F32)
    side = jnp.where((col_index & (col_count // 2)) != 0, 1, 0)
    half = packed_width // 2
    position = jnp.where(column < half, column + side * half, column - side * half)
    lane = lax.broadcasted_iota(jnp.int32, (slot, slot), 1)
    for k in range(total_cols // slot):
        rows = slice(k * slot, (k + 1) * slot)
        for ref, at in ((mine_ref, side), (other_ref, 1 - side)):
            inside = row_in_slot[:, :half]
            chosen = (column[:, :half] + at * half == inside + offsets[k]) & (inside < widths_ref[k])
            ref[rows, :] = jnp.where(chosen, 1.0, 0.0).astype(BF16)
        keep_ref[rows, :] = jnp.where(
            (lane < widths_ref[k]) & (row_in_slot[:, :slot] < widths_ref[k]), 1.0, 0.0
        )
    size = min(per_col, slot)
    for part in range(per_col // size):
        begin = col_index * per_col + part * size
        start, count = 0, 0
        for k in range(total_cols // slot):
            start = start + jnp.where(k < begin // slot, widths_ref[k], 0)
            count = count + jnp.where(k == begin // slot, widths_ref[k], 0)
        within = row_in_slot[:size] + begin % slot
        chosen = (position[:size] == within + start) & (within < count)
        pick_d_ref[part * size:(part + 1) * size, :] = jnp.where(chosen, 1.0, 0.0).astype(BF16)
    upper_ref[...] = jnp.full(upper_ref.shape, side, jnp.int32).astype(F32)


def compute_kernel(
    col_count, supernodes, slot, widths_ref, weights_ref, place_ref, straight_ref,
    own_wide_ref, *refs
):
    block_refs, refs = refs[:-7], refs[-7:]
    keep_d_ref, send_d_ref, keep_t_ref, send_t_ref, x_ref, y_ref, t_ref = refs
    packed_width = block_refs[0].shape[0] // 2
    local_rows = straight_ref.shape[1]
    strips = local_rows // slot
    w_real = weights_ref[0, 0]
    w_imag = weights_ref[0, 1]
    col_index = place_ref[1]

    panel = jnp.concatenate([ref[...] for ref in block_refs], axis=1)
    with_real = rows_by_rows(panel, straight_ref[0])
    with_imag = rows_by_rows(panel, straight_ref[1])
    u_real = with_imag[packed_width:] - with_real[:packed_width]
    u_imag = -(with_real[packed_width:] + with_imag[:packed_width])
    weighted = w_real * u_real - w_imag * u_imag
    turned = w_real * u_imag + w_imag * u_real

    half = packed_width // 2
    upper = (col_index & (col_count // 2)) != 0
    keep_d_ref[...] = jnp.where(upper, weighted[half:], weighted[:half])
    send_d_ref[...] = jnp.where(upper, weighted[:half], weighted[half:])

    for ref, value in ((x_ref, weighted), (y_ref, turned)):
        for s in range(strips):
            ref[s, :packed_width] = value[:, s * slot:(s + 1) * slot]
            ref[s, packed_width:] = jnp.zeros((slot, slot), F32)

    offsets = offsets_of(widths_ref, supernodes)
    for k in range(supernodes):
        right = jnp.concatenate(
            [ref[s, pl.ds(offsets[k], slot), :] for ref in (x_ref, y_ref) for s in range(strips)],
            axis=1,
        )
        high = right.astype(BF16)
        low = (right - high.astype(F32)).astype(BF16)
        product = rows_by_rows(
            own_wide_ref[k * slot:(k + 1) * slot, :], jnp.concatenate([high, low], axis=0)
        )
        t_ref[pl.ds(offsets[k], slot), :] = product[:, :slot] + product[:, slot:]
    keep_t_ref[...] = jnp.where(upper, t_ref[half:2 * half], t_ref[:half])
    send_t_ref[...] = jnp.where(upper, t_ref[:half], t_ref[half:2 * half])


def picked(pick_ref, value):
    high = value.astype(BF16)
    low = (value - high.astype(F32)).astype(BF16)
    return jnp.dot(pick_ref[...], high, preferred_element_type=F32) + jnp.dot(
        pick_ref[...], low, preferred_element_type=F32
    )


def expand_kernel(
    pick_d_ref, pick_ref, keep_ref, upper_ref, mine_d_ref, other_d_ref, mine_t_ref,
    mine_term_ref, other_term_ref, density_ref, diagonal_ref,
):
    density_ref[...] = picked(pick_d_ref, jnp.concatenate([mine_d_ref[...], other_d_ref[...]], axis=0))
    product = picked(pick_ref, mine_t_ref[...])
    rows = mine_term_ref.shape[0]
    upper = upper_ref[:1, :] > 0.5
    terms = (
        jnp.where(upper, other_term_ref[...], mine_term_ref[...]),
        jnp.where(upper, mine_term_ref[...], other_term_ref[...]),
    )
    for side in range(2):
        part = slice(side * rows, (side + 1) * rows)
        diagonal_ref[part] = terms[side] - jnp.where(keep_ref[part] > 0.5, product[part], 0.0)


def finish_kernel(pick_ref, keep_ref, other_t_ref, partial_ref, diagonal_ref):
    product = picked(pick_ref, other_t_ref[...])
    diagonal_ref[...] = partial_ref[...] - jnp.where(keep_ref[...] > 0.5, product, 0.0)


def bits_of(count):
    return [1 << k for k in range(count.bit_length() - 1)]


def swap(value, axis, bit):
    return lax.ppermute(value, axis, [(i, i ^ bit) for i in range(lax.axis_size(axis))])


def tree_sum(terms):
    while len(terms) > 1:
        terms = [terms[j] + terms[j + 1] for j in range(0, len(terms), 2)]
    return terms[0]


def sum_direct(value, axis):
    return tree_sum([swap(value, axis, j) for j in range(1, lax.axis_size(axis))][::-1] + [value])


def scatter_rest(value, axis):
    index = lax.axis_index(axis)
    for bit in bits_of(lax.axis_size(axis))[:-1][::-1]:
        half = value.shape[0] // 2
        upper = (index & bit) != 0
        keep = jnp.where(upper, value[half:], value[:half])
        value = keep + swap(jnp.where(upper, value[:half], value[half:]), axis, bit)
    return value


def gather_but_last(value, axis):
    index = lax.axis_index(axis)
    for bit in bits_of(lax.axis_size(axis))[:-1]:
        other = swap(value, axis, bit)
        upper = (index & bit) != 0
        value = jnp.concatenate(
            [jnp.where(upper, other, value), jnp.where(upper, value, other)], axis=0
        )
    return value


def per_device(found_inverse, l_panel, block_pattern, sup_widths, diag_inverse, pole_weights):
    slot = diag_inverse.shape[-1]
    total_cols = l_panel.shape[-1]
    supernodes = total_cols // slot
    packed_width = slot + (supernodes - 1) * (slot // 2)
    half = packed_width // 2
    local_rows = found_inverse.shape[2]
    block = l_panel.shape[2]
    row_count = lax.axis_size("row")
    col_count = lax.axis_size("col")
    top = col_count // 2
    place = jnp.stack([lax.axis_index("row"), lax.axis_index("col")]).astype(jnp.int32)

    packed = pl.pallas_call(
        functools.partial(pack_kernel, supernodes, slot),
        in_specs=[SMEM_SPEC, SMEM_SPEC, VMEM_SPEC],
        out_specs=VMEM_SPEC,
        out_shape=jax.ShapeDtypeStruct((2 * packed_width, block), BF16),
        name="pack",
    )(block_pattern, sup_widths, l_panel[0])

    blocks = {0: packed}
    for other in range(1, row_count):
        blocks[other] = swap(packed, "row", other)
    own = [packed] + [swap(packed, "col", other) for other in range(1, col_count)]

    straight, own_wide, term, pick_d, pick_mine, pick_other, keep, upper = pl.pallas_call(
        functools.partial(prepare_kernel, (row_count, col_count)),
        in_specs=[SMEM_SPEC] * 3 + [VMEM_SPEC] * (2 + col_count),
        out_specs=[VMEM_SPEC] * 8,
        out_shape=[
            jax.ShapeDtypeStruct((2, local_rows, row_count * block), BF16),
            jax.ShapeDtypeStruct((total_cols, 2 * local_rows), BF16),
            jax.ShapeDtypeStruct((total_cols // col_count, slot), F32),
            jax.ShapeDtypeStruct((total_cols // col_count, packed_width), BF16),
            jax.ShapeDtypeStruct((total_cols, packed_width // 2), BF16),
            jax.ShapeDtypeStruct((total_cols, packed_width // 2), BF16),
            jax.ShapeDtypeStruct((total_cols, slot), F32),
            jax.ShapeDtypeStruct((8, slot), F32),
        ],
        compiler_params=PARAMS,
        cost_estimate=pl.CostEstimate(
            flops=4 * 256 * local_rows * row_count * block,
            bytes_accessed=8 * local_rows * row_count * block,
            transcendentals=0,
        ),
        name="prepare",
    )(
        sup_widths, pole_weights, place,
        found_inverse.reshape(2 * local_rows * row_count, block), diag_inverse[0], *own,
    )
    term = sum_direct(term, "pole")

    keep_d, send_d, keep_t, send_t = pl.pallas_call(
        functools.partial(compute_kernel, col_count, supernodes, slot),
        in_specs=[SMEM_SPEC] * 3 + [VMEM_SPEC] * (2 + row_count),
        out_specs=[VMEM_SPEC] * 4,
        out_shape=[jax.ShapeDtypeStruct((half, local_rows), F32)] * 2
        + [jax.ShapeDtypeStruct((half, slot), F32)] * 2,
        scratch_shapes=[
            pltpu.VMEM((local_rows // slot, packed_width + slot, slot), F32),
            pltpu.VMEM((local_rows // slot, packed_width + slot, slot), F32),
            pltpu.VMEM((packed_width + slot, slot), F32),
        ],
        compiler_params=PARAMS,
        name="compute",
    )(
        sup_widths, pole_weights, place, straight, own_wide,
        *[blocks[other] for other in range(row_count)],
    )

    tie = lax.optimization_barrier
    products, send_d, term = tie((keep_t + swap(send_t, "col", top), send_d, term))
    term = gather_but_last(term, "col")
    products = scatter_rest(products, "col")
    for bit in bits_of(row_count)[::-1]:
        products = products + swap(products, "row", 2 * bit - 1)
    density = scatter_rest(keep_d + swap(send_d, "col", top), "col")
    density = sum_direct(density, "pole")
    products = sum_direct(products, "pole")
    density = gather_but_last(density, "col")
    products = gather_but_last(products, "col")

    density, partial = pl.pallas_call(
        expand_kernel,
        in_specs=[VMEM_SPEC] * 9,
        out_specs=[VMEM_SPEC] * 2,
        out_shape=[
            jax.ShapeDtypeStruct((total_cols // col_count, local_rows), F32),
            jax.ShapeDtypeStruct((total_cols, slot), F32),
        ],
        compiler_params=PARAMS,
        cost_estimate=pl.CostEstimate(
            flops=8 * total_cols * packed_width * (local_rows + slot),
            bytes_accessed=16 * total_cols * local_rows,
            transcendentals=0,
        ),
        name="expand",
    )(
        pick_d, pick_mine, keep, upper, density, swap(density, "col", top), products,
        term, swap(term, "col", top),
    )
    diagonal = pl.pallas_call(
        finish_kernel,
        in_specs=[VMEM_SPEC] * 4,
        out_specs=VMEM_SPEC,
        out_shape=jax.ShapeDtypeStruct((total_cols, slot), F32),
        compiler_params=PARAMS,
        name="finish",
    )(pick_other, keep, swap(products, "col", top), partial)
    return (density, diagonal)


def solution(mesh):
    in_specs = (
        P("pole", None, "row", None, "col", None),
        P("pole", None, ("row", "col"), None),
        P(("row", "col"), None),
        P(),
        P("pole", None, None, None),
        P("pole", None),
    )
    out_specs = (P("col", "row"), P())
    return jax.shard_map(
        per_device, mesh=mesh, in_specs=in_specs, out_specs=out_specs, check_vma=False
    )
```

```python
import functools

import jax
import jax.numpy as jnp
from jax import lax
from jax.experimental import pallas as pl
from jax.experimental.pallas import tpu as pltpu
from jax.sharding import PartitionSpec as P

F32 = jnp.float32
BF16 = jnp.bfloat16
VMEM_SPEC = pl.BlockSpec(memory_space=pltpu.VMEM)
SMEM_SPEC = pl.BlockSpec(memory_space=pltpu.SMEM)
PARAMS = pltpu.CompilerParams(vmem_limit_bytes=48 * 1024 * 1024)


def rows_by_rows(left, right):
    return lax.dot_general(left, right, (((1,), (1,)), ((), ())), preferred_element_type=F32)


def offsets_of(widths_ref, supernodes):
    offsets = [0]
    for k in range(supernodes):
        offsets.append(offsets[-1] + widths_ref[k])
    return offsets


def pack_kernel(supernodes, slot, pattern_ref, widths_ref, panel_ref, packed_ref):
    packed_width = packed_ref.shape[0] // 2
    offsets = offsets_of(widths_ref, supernodes)
    lane = lax.broadcasted_iota(jnp.int32, (1, slot), 1)
    place = []
    for k in range(supernodes):
        valid = (lane < widths_ref[k]) & (pattern_ref[0, k] == 1)
        place.append(jnp.where(valid, offsets[k] + lane, -1))
    place = jnp.concatenate(place, axis=1)
    target = lax.broadcasted_iota(jnp.int32, (packed_width, supernodes * slot), 0)
    select = jnp.where(target == place, 1.0, 0.0).astype(BF16)
    for part in range(2):
        packed_ref[part * packed_width:(part + 1) * packed_width, :] = rows_by_rows(
            select, panel_ref[part]
        ).astype(BF16)


def prepare_kernel(
    counts, widths_ref, weights_ref, place_ref, inverse_ref, diag_ref, *refs
):
    row_count, col_count = counts
    own_refs, refs = refs[:col_count], refs[col_count:]
    straight_ref, own_wide_ref, term_ref, pick_d_ref, mine_ref, other_ref, keep_ref, upper_ref = refs
    packed_width = own_refs[0].shape[0] // 2
    col_index = place_ref[1]
    block = inverse_ref.shape[1]
    local_rows = straight_ref.shape[1]
    row_index = place_ref[0]
    group = max(8, 256 // row_count)
    span = group * row_count
    row_id = lax.broadcasted_iota(jnp.int32, (span, span), 0)
    col_id = lax.broadcasted_iota(jnp.int32, (span, span), 1)
    source = (row_id % group) * row_count + ((row_id // group) ^ row_index)
    order = jnp.where(col_id == source, 1.0, 0.0).astype(BF16)
    for part in range(2):
        for chunk in range(local_rows // group):
            base = (part * local_rows + chunk * group) * row_count
            mixed = inverse_ref[base:base + span, :]
            sorted_rows = jnp.dot(order, mixed, preferred_element_type=F32).astype(BF16)
            for owner in range(row_count):
                straight_ref[
                    part, chunk * group:(chunk + 1) * group, owner * block:(owner + 1) * block
                ] = sorted_rows[owner * group:(owner + 1) * group]
    own = []
    for c in range(col_count):
        block_of = own_refs[0][...]
        for other in range(1, col_count):
            block_of = jnp.where((col_index ^ c) == other, own_refs[other][...], block_of)
        own.append(block_of)
    own = jnp.concatenate(own, axis=1)
    total_cols = own_wide_ref.shape[0]
    slot = diag_ref.shape[2]
    offsets = offsets_of(widths_ref, total_cols // slot)
    row_in_slot = lax.broadcasted_iota(jnp.int32, (slot, packed_width), 0)
    column = lax.broadcasted_iota(jnp.int32, (slot, packed_width), 1)
    for k in range(total_cols // slot):
        chosen = (column == row_in_slot + offsets[k]) & (row_in_slot < widths_ref[k])
        chosen = jnp.where(chosen, 1.0, 0.0).astype(BF16)
        for part, sign in enumerate((1.0, -1.0)):
            rows = own[part * packed_width:(part + 1) * packed_width]
            own_wide_ref[k * slot:(k + 1) * slot, part * local_rows:(part + 1) * local_rows] = (
                sign * jnp.dot(chosen, rows, preferred_element_type=F32)
            ).astype(BF16)
    per_col = term_ref.shape[0]
    first = pl.multiple_of(col_index * per_col, per_col)
    term_ref[...] = weights_ref[0, 0] * diag_ref[0, pl.ds(first, per_col), :].astype(
        F32
    ) - weights_ref[0, 1] * diag_ref[1, pl.ds(first, per_col), :].astype(F32)
    side = jnp.where((col_index & (col_count // 2)) != 0, 1, 0)
    half = packed_width // 2
    position = jnp.where(column < half, column + side * half, column - side * half)
    lane = lax.broadcasted_iota(jnp.int32, (slot, slot), 1)
    for k in range(total_cols // slot):
        rows = slice(k * slot, (k + 1) * slot)
        for ref, at in ((mine_ref, side), (other_ref, 1 - side)):
            inside = row_in_slot[:, :half]
            chosen = (column[:, :half] + at * half == inside + offsets[k]) & (inside < widths_ref[k])
            ref[rows, :] = jnp.where(chosen, 1.0, 0.0).astype(BF16)
        keep_ref[rows, :] = jnp.where(
            (lane < widths_ref[k]) & (row_in_slot[:, :slot] < widths_ref[k]), 1.0, 0.0
        )
    size = min(per_col, slot)
    for part in range(per_col // size):
        begin = col_index * per_col + part * size
        start, count = 0, 0
        for k in range(total_cols // slot):
            start = start + jnp.where(k < begin // slot, widths_ref[k], 0)
            count = count + jnp.where(k == begin // slot, widths_ref[k], 0)
        within = row_in_slot[:size] + begin % slot
        chosen = (position[:size] == within + start) & (within < count)
        pick_d_ref[part * size:(part + 1) * size, :] = jnp.where(chosen, 1.0, 0.0).astype(BF16)
    upper_ref[...] = jnp.full(upper_ref.shape, side, jnp.int32).astype(F32)


def compute_kernel(
    others, col_count, supernodes, slot, widths_ref, weights_ref, place_ref, straight_ref,
    own_wide_ref, *refs
):
    block_refs, refs = refs[:-7], refs[-7:]
    block_refs = [block_refs[others.index(other)] for other in range(len(others))]
    keep_d_ref, send_d_ref, keep_t_ref, send_t_ref, x_ref, y_ref, t_ref = refs
    packed_width = block_refs[0].shape[0] // 2
    local_rows = straight_ref.shape[1]
    strips = local_rows // slot
    w_real = weights_ref[0, 0]
    w_imag = weights_ref[0, 1]
    col_index = place_ref[1]

    panel = jnp.concatenate([ref[...] for ref in block_refs], axis=1)
    with_real = rows_by_rows(panel, straight_ref[0])
    with_imag = rows_by_rows(panel, straight_ref[1])
    u_real = with_imag[packed_width:] - with_real[:packed_width]
    u_imag = -(with_real[packed_width:] + with_imag[:packed_width])
    weighted = w_real * u_real - w_imag * u_imag
    turned = w_real * u_imag + w_imag * u_real

    half = packed_width // 2
    upper = (col_index & (col_count // 2)) != 0
    keep_d_ref[...] = jnp.where(upper, weighted[half:], weighted[:half])
    send_d_ref[...] = jnp.where(upper, weighted[:half], weighted[half:])

    for ref, value in ((x_ref, weighted), (y_ref, turned)):
        for s in range(strips):
            ref[s, :packed_width] = value[:, s * slot:(s + 1) * slot]
            ref[s, packed_width:] = jnp.zeros((slot, slot), F32)

    offsets = offsets_of(widths_ref, supernodes)
    for k in range(supernodes):
        right = jnp.concatenate(
            [ref[s, pl.ds(offsets[k], slot), :] for ref in (x_ref, y_ref) for s in range(strips)],
            axis=1,
        )
        high = right.astype(BF16)
        low = (right - high.astype(F32)).astype(BF16)
        product = rows_by_rows(
            own_wide_ref[k * slot:(k + 1) * slot, :], jnp.concatenate([high, low], axis=0)
        )
        t_ref[pl.ds(offsets[k], slot), :] = product[:, :slot] + product[:, slot:]
    keep_t_ref[...] = jnp.where(upper, t_ref[half:2 * half], t_ref[:half])
    send_t_ref[...] = jnp.where(upper, t_ref[:half], t_ref[half:2 * half])


def picked(pick_ref, value):
    high = value.astype(BF16)
    low = (value - high.astype(F32)).astype(BF16)
    return jnp.dot(pick_ref[...], high, preferred_element_type=F32) + jnp.dot(
        pick_ref[...], low, preferred_element_type=F32
    )


def expand_kernel(
    pick_d_ref, pick_ref, keep_ref, upper_ref, mine_d_ref, other_d_ref, mine_t_ref,
    mine_term_ref, other_term_ref, density_ref, diagonal_ref,
):
    density_ref[...] = picked(pick_d_ref, jnp.concatenate([mine_d_ref[...], other_d_ref[...]], axis=0))
    product = picked(pick_ref, mine_t_ref[...])
    rows = mine_term_ref.shape[0]
    upper = upper_ref[:1, :] > 0.5
    terms = (
        jnp.where(upper, other_term_ref[...], mine_term_ref[...]),
        jnp.where(upper, mine_term_ref[...], other_term_ref[...]),
    )
    for side in range(2):
        part = slice(side * rows, (side + 1) * rows)
        diagonal_ref[part] = terms[side] - jnp.where(keep_ref[part] > 0.5, product[part], 0.0)


def finish_kernel(pick_ref, keep_ref, other_t_ref, partial_ref, diagonal_ref):
    product = picked(pick_ref, other_t_ref[...])
    diagonal_ref[...] = partial_ref[...] - jnp.where(keep_ref[...] > 0.5, product, 0.0)


def bits_of(count):
    return [1 << k for k in range(count.bit_length() - 1)]


def swap(value, axis, bit):
    return lax.ppermute(value, axis, [(i, i ^ bit) for i in range(lax.axis_size(axis))])


def tree_sum(terms):
    while len(terms) > 1:
        terms = [terms[j] + terms[j + 1] for j in range(0, len(terms), 2)]
    return terms[0]


def sum_direct(value, axis):
    return tree_sum([value] + [swap(value, axis, j) for j in range(1, lax.axis_size(axis))])


def scatter_rest(value, axis):
    index = lax.axis_index(axis)
    for bit in bits_of(lax.axis_size(axis))[:-1][::-1]:
        half = value.shape[0] // 2
        upper = (index & bit) != 0
        keep = jnp.where(upper, value[half:], value[:half])
        value = keep + swap(jnp.where(upper, value[:half], value[half:]), axis, bit)
    return value


def gather_but_last(value, axis):
    index = lax.axis_index(axis)
    for bit in bits_of(lax.axis_size(axis))[:-1]:
        other = swap(value, axis, bit)
        upper = (index & bit) != 0
        value = jnp.concatenate(
            [jnp.where(upper, other, value), jnp.where(upper, value, other)], axis=0
        )
    return value


def per_device(found_inverse, l_panel, block_pattern, sup_widths, diag_inverse, pole_weights):
    slot = diag_inverse.shape[-1]
    total_cols = l_panel.shape[-1]
    supernodes = total_cols // slot
    packed_width = slot + (supernodes - 1) * (slot // 2)
    half = packed_width // 2
    local_rows = found_inverse.shape[2]
    block = l_panel.shape[2]
    row_count = lax.axis_size("row")
    col_count = lax.axis_size("col")
    top = col_count // 2
    place = jnp.stack([lax.axis_index("row"), lax.axis_index("col")]).astype(jnp.int32)

    packed = pl.pallas_call(
        functools.partial(pack_kernel, supernodes, slot),
        in_specs=[SMEM_SPEC, SMEM_SPEC, VMEM_SPEC],
        out_specs=VMEM_SPEC,
        out_shape=jax.ShapeDtypeStruct((2 * packed_width, block), BF16),
        name="pack",
    )(block_pattern, sup_widths, l_panel[0])

    blocks = {0: packed}
    others = sorted(range(row_count), key=lambda other: other > 0 and other % 2 == 0)
    for other in range(1, row_count):
        blocks[other] = swap(packed, "row", other)
    own = [packed] + [swap(packed, "col", other) for other in range(1, col_count)]

    straight, own_wide, term, pick_d, pick_mine, pick_other, keep, upper = pl.pallas_call(
        functools.partial(prepare_kernel, (row_count, col_count)),
        in_specs=[SMEM_SPEC] * 3 + [VMEM_SPEC] * (2 + col_count),
        out_specs=[VMEM_SPEC] * 8,
        out_shape=[
            jax.ShapeDtypeStruct((2, local_rows, row_count * block), BF16),
            jax.ShapeDtypeStruct((total_cols, 2 * local_rows), BF16),
            jax.ShapeDtypeStruct((total_cols // col_count, slot), F32),
            jax.ShapeDtypeStruct((total_cols // col_count, packed_width), BF16),
            jax.ShapeDtypeStruct((total_cols, packed_width // 2), BF16),
            jax.ShapeDtypeStruct((total_cols, packed_width // 2), BF16),
            jax.ShapeDtypeStruct((total_cols, slot), F32),
            jax.ShapeDtypeStruct((8, slot), F32),
        ],
        compiler_params=PARAMS,
        cost_estimate=pl.CostEstimate(
            flops=4 * 256 * local_rows * row_count * block,
            bytes_accessed=8 * local_rows * row_count * block,
            transcendentals=0,
        ),
        name="prepare",
    )(
        sup_widths, pole_weights, place,
        found_inverse.reshape(2 * local_rows * row_count, block), diag_inverse[0], *own,
    )
    term = sum_direct(term, "pole")

    keep_d, send_d, keep_t, send_t = pl.pallas_call(
        functools.partial(compute_kernel, others, col_count, supernodes, slot),
        in_specs=[SMEM_SPEC] * 3 + [VMEM_SPEC] * (2 + row_count),
        out_specs=[VMEM_SPEC] * 4,
        out_shape=[jax.ShapeDtypeStruct((half, local_rows), F32)] * 2
        + [jax.ShapeDtypeStruct((half, slot), F32)] * 2,
        scratch_shapes=[
            pltpu.VMEM((local_rows // slot, packed_width + slot, slot), F32),
            pltpu.VMEM((local_rows // slot, packed_width + slot, slot), F32),
            pltpu.VMEM((packed_width + slot, slot), F32),
        ],
        compiler_params=PARAMS,
        name="compute",
    )(
        sup_widths, pole_weights, place, straight, own_wide,
        *[blocks[other] for other in others],
    )

    tie = lax.optimization_barrier
    products, send_d, term = tie((keep_t + swap(send_t, "col", top), send_d, term))
    term = gather_but_last(term, "col")
    products = scatter_rest(products, "col")
    for bit in bits_of(row_count)[::-1]:
        products = products + swap(products, "row", 2 * bit - 1)
    density = scatter_rest(keep_d + swap(send_d, "col", top), "col")
    density = sum_direct(density, "pole")
    products = sum_direct(products, "pole")
    density = gather_but_last(density, "col")
    products = gather_but_last(products, "col")

    density, partial = pl.pallas_call(
        expand_kernel,
        in_specs=[VMEM_SPEC] * 9,
        out_specs=[VMEM_SPEC] * 2,
        out_shape=[
            jax.ShapeDtypeStruct((total_cols // col_count, local_rows), F32),
            jax.ShapeDtypeStruct((total_cols, slot), F32),
        ],
        compiler_params=PARAMS,
        cost_estimate=pl.CostEstimate(
            flops=8 * total_cols * packed_width * (local_rows + slot),
            bytes_accessed=16 * total_cols * local_rows,
            transcendentals=0,
        ),
        name="expand",
    )(
        pick_d, pick_mine, keep, upper, density, swap(density, "col", top), products,
        term, swap(term, "col", top),
    )
    diagonal = pl.pallas_call(
        finish_kernel,
        in_specs=[VMEM_SPEC] * 4,
        out_specs=VMEM_SPEC,
        out_shape=jax.ShapeDtypeStruct((total_cols, slot), F32),
        compiler_params=PARAMS,
        name="finish",
    )(pick_other, keep, swap(products, "col", top), partial)
    return (density, diagonal)


def solution(mesh):
    in_specs = (
        P("pole", None, "row", None, "col", None),
        P("pole", None, ("row", "col"), None),
        P(("row", "col"), None),
        P(),
        P("pole", None, None, None),
        P("pole", None),
    )
    out_specs = (P("col", "row"), P())
    return jax.shard_map(
        per_device, mesh=mesh, in_specs=in_specs, out_specs=out_specs, check_vma=False
    )
```

```python
import functools

import jax
import jax.numpy as jnp
from jax import lax
from jax.experimental import pallas as pl
from jax.experimental.pallas import tpu as pltpu
from jax.sharding import PartitionSpec as P

F32 = jnp.float32
BF16 = jnp.bfloat16
VMEM_SPEC = pl.BlockSpec(memory_space=pltpu.VMEM)
SMEM_SPEC = pl.BlockSpec(memory_space=pltpu.SMEM)
PARAMS = pltpu.CompilerParams(vmem_limit_bytes=48 * 1024 * 1024)


def rows_by_rows(left, right):
    return lax.dot_general(left, right, (((1,), (1,)), ((), ())), preferred_element_type=F32)


def offsets_of(widths_ref, supernodes):
    offsets = [0]
    for k in range(supernodes):
        offsets.append(offsets[-1] + widths_ref[k])
    return offsets


def pack_kernel(supernodes, slot, pattern_ref, widths_ref, panel_ref, packed_ref):
    packed_width = packed_ref.shape[0] // 2
    offsets = offsets_of(widths_ref, supernodes)
    lane = lax.broadcasted_iota(jnp.int32, (1, slot), 1)
    place = []
    for k in range(supernodes):
        valid = (lane < widths_ref[k]) & (pattern_ref[0, k] == 1)
        place.append(jnp.where(valid, offsets[k] + lane, -1))
    place = jnp.concatenate(place, axis=1)
    target = lax.broadcasted_iota(jnp.int32, (packed_width, supernodes * slot), 0)
    select = jnp.where(target == place, 1.0, 0.0).astype(BF16)
    for part in range(2):
        packed_ref[part * packed_width:(part + 1) * packed_width, :] = rows_by_rows(
            select, panel_ref[part]
        ).astype(BF16)


def prepare_kernel(
    counts, widths_ref, weights_ref, place_ref, inverse_ref, diag_ref, *refs
):
    row_count, col_count = counts
    own_refs, refs = refs[:col_count], refs[col_count:]
    straight_ref, own_wide_ref, term_ref, pick_d_ref, mine_ref, other_ref, keep_ref, upper_ref = refs
    packed_width = own_refs[0].shape[0] // 2
    col_index = place_ref[1]
    block = inverse_ref.shape[1]
    local_rows = straight_ref.shape[1]
    row_index = place_ref[0]
    group = max(8, 256 // row_count)
    span = group * row_count
    row_id = lax.broadcasted_iota(jnp.int32, (span, span), 0)
    col_id = lax.broadcasted_iota(jnp.int32, (span, span), 1)
    source = (row_id % group) * row_count + ((row_id // group) ^ row_index)
    order = jnp.where(col_id == source, 1.0, 0.0).astype(BF16)
    for part in range(2):
        for chunk in range(local_rows // group):
            base = (part * local_rows + chunk * group) * row_count
            mixed = inverse_ref[base:base + span, :]
            sorted_rows = jnp.dot(order, mixed, preferred_element_type=F32).astype(BF16)
            for owner in range(row_count):
                straight_ref[
                    part, chunk * group:(chunk + 1) * group, owner * block:(owner + 1) * block
                ] = sorted_rows[owner * group:(owner + 1) * group]
    own = []
    for c in range(col_count):
        block_of = own_refs[0][...]
        for other in range(1, col_count):
            block_of = jnp.where((col_index ^ c) == other, own_refs[other][...], block_of)
        own.append(block_of)
    own = jnp.concatenate(own, axis=1)
    total_cols = own_wide_ref.shape[0]
    slot = diag_ref.shape[2]
    offsets = offsets_of(widths_ref, total_cols // slot)
    row_in_slot = lax.broadcasted_iota(jnp.int32, (slot, packed_width), 0)
    column = lax.broadcasted_iota(jnp.int32, (slot, packed_width), 1)
    for k in range(total_cols // slot):
        chosen = (column == row_in_slot + offsets[k]) & (row_in_slot < widths_ref[k])
        chosen = jnp.where(chosen, 1.0, 0.0).astype(BF16)
        for part, sign in enumerate((1.0, -1.0)):
            rows = own[part * packed_width:(part + 1) * packed_width]
            own_wide_ref[k * slot:(k + 1) * slot, part * local_rows:(part + 1) * local_rows] = (
                sign * jnp.dot(chosen, rows, preferred_element_type=F32)
            ).astype(BF16)
    per_col = term_ref.shape[0]
    first = pl.multiple_of(col_index * per_col, per_col)
    term_ref[...] = weights_ref[0, 0] * diag_ref[0, pl.ds(first, per_col), :].astype(
        F32
    ) - weights_ref[0, 1] * diag_ref[1, pl.ds(first, per_col), :].astype(F32)
    side = jnp.where((col_index & (col_count // 2)) != 0, 1, 0)
    half = packed_width // 2
    position = jnp.where(column < half, column + side * half, column - side * half)
    lane = lax.broadcasted_iota(jnp.int32, (slot, slot), 1)
    for k in range(total_cols // slot):
        rows = slice(k * slot, (k + 1) * slot)
        for ref, at in ((mine_ref, side), (other_ref, 1 - side)):
            inside = row_in_slot[:, :half]
            chosen = (column[:, :half] + at * half == inside + offsets[k]) & (inside < widths_ref[k])
            ref[rows, :] = jnp.where(chosen, 1.0, 0.0).astype(BF16)
        keep_ref[rows, :] = jnp.where(
            (lane < widths_ref[k]) & (row_in_slot[:, :slot] < widths_ref[k]), 1.0, 0.0
        )
    size = min(per_col, slot)
    for part in range(per_col // size):
        begin = col_index * per_col + part * size
        start, count = 0, 0
        for k in range(total_cols // slot):
            start = start + jnp.where(k < begin // slot, widths_ref[k], 0)
            count = count + jnp.where(k == begin // slot, widths_ref[k], 0)
        within = row_in_slot[:size] + begin % slot
        chosen = (position[:size] == within + start) & (within < count)
        pick_d_ref[part * size:(part + 1) * size, :] = jnp.where(chosen, 1.0, 0.0).astype(BF16)
    upper_ref[...] = jnp.full(upper_ref.shape, side, jnp.int32).astype(F32)


def compute_kernel(
    others, col_count, supernodes, slot, widths_ref, weights_ref, place_ref, straight_ref,
    own_wide_ref, *refs
):
    block_refs, refs = refs[:-7], refs[-7:]
    block_refs = [block_refs[others.index(other)] for other in range(len(others))]
    keep_d_ref, send_d_ref, keep_t_ref, send_t_ref, x_ref, y_ref, t_ref = refs
    packed_width = block_refs[0].shape[0] // 2
    local_rows = straight_ref.shape[1]
    strips = local_rows // slot
    w_real = weights_ref[0, 0]
    w_imag = weights_ref[0, 1]
    col_index = place_ref[1]

    panel = jnp.concatenate([ref[...] for ref in block_refs], axis=1)
    with_real = rows_by_rows(panel, straight_ref[0])
    with_imag = rows_by_rows(panel, straight_ref[1])
    u_real = with_imag[packed_width:] - with_real[:packed_width]
    u_imag = -(with_real[packed_width:] + with_imag[:packed_width])
    weighted = w_real * u_real - w_imag * u_imag
    turned = w_real * u_imag + w_imag * u_real

    half = packed_width // 2
    upper = (col_index & (col_count // 2)) != 0
    keep_d_ref[...] = jnp.where(upper, weighted[half:], weighted[:half])
    send_d_ref[...] = jnp.where(upper, weighted[:half], weighted[half:])

    for ref, value in ((x_ref, weighted), (y_ref, turned)):
        for s in range(strips):
            ref[s, :packed_width] = value[:, s * slot:(s + 1) * slot]
            ref[s, packed_width:] = jnp.zeros((slot, slot), F32)

    offsets = offsets_of(widths_ref, supernodes)
    for k in range(supernodes):
        right = jnp.concatenate(
            [ref[s, pl.ds(offsets[k], slot), :] for ref in (x_ref, y_ref) for s in range(strips)],
            axis=1,
        )
        high = right.astype(BF16)
        low = (right - high.astype(F32)).astype(BF16)
        product = rows_by_rows(
            own_wide_ref[k * slot:(k + 1) * slot, :], jnp.concatenate([high, low], axis=0)
        )
        t_ref[pl.ds(offsets[k], slot), :] = product[:, :slot] + product[:, slot:]
    keep_t_ref[...] = jnp.where(upper, t_ref[half:2 * half], t_ref[:half])
    send_t_ref[...] = jnp.where(upper, t_ref[:half], t_ref[half:2 * half])


def picked(pick_ref, value):
    high = value.astype(BF16)
    low = (value - high.astype(F32)).astype(BF16)
    return jnp.dot(pick_ref[...], high, preferred_element_type=F32) + jnp.dot(
        pick_ref[...], low, preferred_element_type=F32
    )


def expand_kernel(
    pick_d_ref, pick_ref, keep_ref, upper_ref, mine_d_ref, other_d_ref, mine_t_ref,
    mine_term_ref, other_term_ref, density_ref, diagonal_ref,
):
    density_ref[...] = picked(pick_d_ref, jnp.concatenate([mine_d_ref[...], other_d_ref[...]], axis=0))
    product = picked(pick_ref, mine_t_ref[...])
    rows = mine_term_ref.shape[0]
    upper = upper_ref[:1, :] > 0.5
    terms = (
        jnp.where(upper, other_term_ref[...], mine_term_ref[...]),
        jnp.where(upper, mine_term_ref[...], other_term_ref[...]),
    )
    for side in range(2):
        part = slice(side * rows, (side + 1) * rows)
        diagonal_ref[part] = terms[side] - jnp.where(keep_ref[part] > 0.5, product[part], 0.0)


def finish_kernel(pick_ref, keep_ref, other_t_ref, partial_ref, diagonal_ref):
    product = picked(pick_ref, other_t_ref[...])
    diagonal_ref[...] = partial_ref[...] - jnp.where(keep_ref[...] > 0.5, product, 0.0)


def bits_of(count):
    return [1 << k for k in range(count.bit_length() - 1)]


def swap(value, axis, bit):
    return lax.ppermute(value, axis, [(i, i ^ bit) for i in range(lax.axis_size(axis))])


def tree_sum(terms):
    while len(terms) > 1:
        terms = [terms[j] + terms[j + 1] for j in range(0, len(terms), 2)]
    return terms[0]


def sum_direct(value, axis):
    return tree_sum([value] + [swap(value, axis, j) for j in range(1, lax.axis_size(axis))])


def scatter_rest(value, axis):
    index = lax.axis_index(axis)
    for bit in bits_of(lax.axis_size(axis))[:-1][::-1]:
        half = value.shape[0] // 2
        upper = (index & bit) != 0
        keep = jnp.where(upper, value[half:], value[:half])
        value = keep + swap(jnp.where(upper, value[:half], value[half:]), axis, bit)
    return value


def gather_but_last(value, axis):
    index = lax.axis_index(axis)
    for bit in bits_of(lax.axis_size(axis))[:-1]:
        other = swap(value, axis, bit)
        upper = (index & bit) != 0
        value = jnp.concatenate(
            [jnp.where(upper, other, value), jnp.where(upper, value, other)], axis=0
        )
    return value


def per_device(found_inverse, l_panel, block_pattern, sup_widths, diag_inverse, pole_weights):
    slot = diag_inverse.shape[-1]
    total_cols = l_panel.shape[-1]
    supernodes = total_cols // slot
    packed_width = slot + (supernodes - 1) * (slot // 2)
    half = packed_width // 2
    local_rows = found_inverse.shape[2]
    block = l_panel.shape[2]
    row_count = lax.axis_size("row")
    col_count = lax.axis_size("col")
    top = col_count // 2
    place = jnp.stack([lax.axis_index("row"), lax.axis_index("col")]).astype(jnp.int32)

    packed = pl.pallas_call(
        functools.partial(pack_kernel, supernodes, slot),
        in_specs=[SMEM_SPEC, SMEM_SPEC, VMEM_SPEC],
        out_specs=VMEM_SPEC,
        out_shape=jax.ShapeDtypeStruct((2 * packed_width, block), BF16),
        name="pack",
    )(block_pattern, sup_widths, l_panel[0])

    blocks = {0: packed}
    others = sorted(range(row_count), key=lambda other: other > 0 and other % 2 == 0)
    for other in range(1, row_count):
        blocks[other] = swap(packed, "row", other)
    own = [packed] + [swap(packed, "col", other) for other in range(1, col_count)]

    straight, own_wide, term, pick_d, pick_mine, pick_other, keep, upper = pl.pallas_call(
        functools.partial(prepare_kernel, (row_count, col_count)),
        in_specs=[SMEM_SPEC] * 3 + [VMEM_SPEC] * (2 + col_count),
        out_specs=[VMEM_SPEC] * 8,
        out_shape=[
            jax.ShapeDtypeStruct((2, local_rows, row_count * block), BF16),
            jax.ShapeDtypeStruct((total_cols, 2 * local_rows), BF16),
            jax.ShapeDtypeStruct((total_cols // col_count, slot), F32),
            jax.ShapeDtypeStruct((total_cols // col_count, packed_width), BF16),
            jax.ShapeDtypeStruct((total_cols, packed_width // 2), BF16),
            jax.ShapeDtypeStruct((total_cols, packed_width // 2), BF16),
            jax.ShapeDtypeStruct((total_cols, slot), F32),
            jax.ShapeDtypeStruct((8, slot), F32),
        ],
        compiler_params=PARAMS,
        cost_estimate=pl.CostEstimate(
            flops=4 * 256 * local_rows * row_count * block,
            bytes_accessed=8 * local_rows * row_count * block,
            transcendentals=0,
        ),
        name="prepare",
    )(
        sup_widths, pole_weights, place,
        found_inverse.reshape(2 * local_rows * row_count, block), diag_inverse[0], *own,
    )
    term = sum_direct(term, "pole")

    keep_d, send_d, keep_t, send_t = pl.pallas_call(
        functools.partial(compute_kernel, others, col_count, supernodes, slot),
        in_specs=[SMEM_SPEC] * 3 + [VMEM_SPEC] * (2 + row_count),
        out_specs=[VMEM_SPEC] * 4,
        out_shape=[jax.ShapeDtypeStruct((half, local_rows), F32)] * 2
        + [jax.ShapeDtypeStruct((half, slot), F32)] * 2,
        scratch_shapes=[
            pltpu.VMEM((local_rows // slot, packed_width + slot, slot), F32),
            pltpu.VMEM((local_rows // slot, packed_width + slot, slot), F32),
            pltpu.VMEM((packed_width + slot, slot), F32),
        ],
        compiler_params=PARAMS,
        name="compute",
    )(
        sup_widths, pole_weights, place, straight, own_wide,
        *[blocks[other] for other in others],
    )

    tie = lax.optimization_barrier
    products, send_d, term = tie((keep_t + swap(send_t, "col", top), send_d, term))
    term = gather_but_last(term, "col")
    products = scatter_rest(products, "col")
    for bit in bits_of(row_count)[::-1]:
        products = products + swap(products, "row", bit)
    density = scatter_rest(keep_d + swap(send_d, "col", top), "col")
    density = sum_direct(density, "pole")
    products = sum_direct(products, "pole")
    density = gather_but_last(density, "col")
    products = gather_but_last(products, "col")

    density, partial = pl.pallas_call(
        expand_kernel,
        in_specs=[VMEM_SPEC] * 9,
        out_specs=[VMEM_SPEC] * 2,
        out_shape=[
            jax.ShapeDtypeStruct((total_cols // col_count, local_rows), F32),
            jax.ShapeDtypeStruct((total_cols, slot), F32),
        ],
        compiler_params=PARAMS,
        cost_estimate=pl.CostEstimate(
            flops=8 * total_cols * packed_width * (local_rows + slot),
            bytes_accessed=16 * total_cols * local_rows,
            transcendentals=0,
        ),
        name="expand",
    )(
        pick_d, pick_mine, keep, upper, density, swap(density, "col", top), products,
        term, swap(term, "col", top),
    )
    diagonal = pl.pallas_call(
        finish_kernel,
        in_specs=[VMEM_SPEC] * 4,
        out_specs=VMEM_SPEC,
        out_shape=jax.ShapeDtypeStruct((total_cols, slot), F32),
        compiler_params=PARAMS,
        name="finish",
    )(pick_other, keep, swap(products, "col", top), partial)
    return (density, diagonal)


def solution(mesh):
    in_specs = (
        P("pole", None, "row", None, "col", None),
        P("pole", None, ("row", "col"), None),
        P(("row", "col"), None),
        P(),
        P("pole", None, None, None),
        P("pole", None),
    )
    out_specs = (P("col", "row"), P())
    return jax.shard_map(
        per_device, mesh=mesh, in_specs=in_specs, out_specs=out_specs, check_vma=False
    )
```

```python
import functools

import jax
import jax.numpy as jnp
from jax import lax
from jax.experimental import pallas as pl
from jax.experimental.pallas import tpu as pltpu
from jax.sharding import PartitionSpec as P

F32 = jnp.float32
BF16 = jnp.bfloat16
VMEM_SPEC = pl.BlockSpec(memory_space=pltpu.VMEM)
SMEM_SPEC = pl.BlockSpec(memory_space=pltpu.SMEM)
PARAMS = pltpu.CompilerParams(vmem_limit_bytes=48 * 1024 * 1024)


def rows_by_rows(left, right):
    return lax.dot_general(left, right, (((1,), (1,)), ((), ())), preferred_element_type=F32)


def offsets_of(widths_ref, supernodes):
    offsets = [0]
    for k in range(supernodes):
        offsets.append(offsets[-1] + widths_ref[k])
    return offsets


def pack_kernel(supernodes, slot, pattern_ref, widths_ref, panel_ref, packed_ref):
    packed_width = packed_ref.shape[0] // 2
    offsets = offsets_of(widths_ref, supernodes)
    lane = lax.broadcasted_iota(jnp.int32, (1, slot), 1)
    place = []
    for k in range(supernodes):
        valid = (lane < widths_ref[k]) & (pattern_ref[0, k] == 1)
        place.append(jnp.where(valid, offsets[k] + lane, -1))
    place = jnp.concatenate(place, axis=1)
    target = lax.broadcasted_iota(jnp.int32, (packed_width, supernodes * slot), 0)
    select = jnp.where(target == place, 1.0, 0.0).astype(BF16)
    for part in range(2):
        packed_ref[part * packed_width:(part + 1) * packed_width, :] = rows_by_rows(
            select, panel_ref[part]
        ).astype(BF16)


def prepare_kernel(
    counts, widths_ref, weights_ref, place_ref, inverse_ref, diag_ref, *refs
):
    row_count, col_count = counts
    own_refs, refs = refs[:col_count], refs[col_count:]
    straight_ref, own_wide_ref, term_ref, pick_d_ref, mine_ref, other_ref, keep_ref, upper_ref = refs
    packed_width = own_refs[0].shape[0] // 2
    col_index = place_ref[1]
    block = inverse_ref.shape[1]
    local_rows = straight_ref.shape[1]
    row_index = place_ref[0]
    group = max(8, 256 // row_count)
    span = group * row_count
    row_id = lax.broadcasted_iota(jnp.int32, (span, span), 0)
    col_id = lax.broadcasted_iota(jnp.int32, (span, span), 1)
    source = (row_id % group) * row_count + ((row_id // group) ^ row_index)
    order = jnp.where(col_id == source, 1.0, 0.0).astype(BF16)
    for part in range(2):
        for chunk in range(local_rows // group):
            base = (part * local_rows + chunk * group) * row_count
            mixed = inverse_ref[base:base + span, :]
            sorted_rows = jnp.dot(order, mixed, preferred_element_type=F32).astype(BF16)
            for owner in range(row_count):
                straight_ref[
                    part, chunk * group:(chunk + 1) * group, owner * block:(owner + 1) * block
                ] = sorted_rows[owner * group:(owner + 1) * group]
    own = []
    for c in range(col_count):
        block_of = own_refs[0][...]
        for other in range(1, col_count):
            block_of = jnp.where((col_index ^ c) == other, own_refs[other][...], block_of)
        own.append(block_of)
    own = jnp.concatenate(own, axis=1)
    total_cols = own_wide_ref.shape[0]
    slot = diag_ref.shape[2]
    offsets = offsets_of(widths_ref, total_cols // slot)
    row_in_slot = lax.broadcasted_iota(jnp.int32, (slot, packed_width), 0)
    column = lax.broadcasted_iota(jnp.int32, (slot, packed_width), 1)
    for k in range(total_cols // slot):
        chosen = (column == row_in_slot + offsets[k]) & (row_in_slot < widths_ref[k])
        chosen = jnp.where(chosen, 1.0, 0.0).astype(BF16)
        for part, sign in enumerate((1.0, -1.0)):
            rows = own[part * packed_width:(part + 1) * packed_width]
            own_wide_ref[k * slot:(k + 1) * slot, part * local_rows:(part + 1) * local_rows] = (
                sign * jnp.dot(chosen, rows, preferred_element_type=F32)
            ).astype(BF16)
    per_col = term_ref.shape[0]
    first = pl.multiple_of(col_index * per_col, per_col)
    term_ref[...] = weights_ref[0, 0] * diag_ref[0, pl.ds(first, per_col), :].astype(
        F32
    ) - weights_ref[0, 1] * diag_ref[1, pl.ds(first, per_col), :].astype(F32)
    side = jnp.where((col_index & (col_count // 2)) != 0, 1, 0)
    half = packed_width // 2
    position = jnp.where(column < half, column + side * half, column - side * half)
    lane = lax.broadcasted_iota(jnp.int32, (slot, slot), 1)
    for k in range(total_cols // slot):
        rows = slice(k * slot, (k + 1) * slot)
        for ref, at in ((mine_ref, side), (other_ref, 1 - side)):
            inside = row_in_slot[:, :half]
            chosen = (column[:, :half] + at * half == inside + offsets[k]) & (inside < widths_ref[k])
            ref[rows, :] = jnp.where(chosen, 1.0, 0.0).astype(BF16)
        keep_ref[rows, :] = jnp.where(
            (lane < widths_ref[k]) & (row_in_slot[:, :slot] < widths_ref[k]), 1.0, 0.0
        )
    size = min(per_col, slot)
    for part in range(per_col // size):
        begin = col_index * per_col + part * size
        start, count = 0, 0
        for k in range(total_cols // slot):
            start = start + jnp.where(k < begin // slot, widths_ref[k], 0)
            count = count + jnp.where(k == begin // slot, widths_ref[k], 0)
        within = row_in_slot[:size] + begin % slot
        chosen = (position[:size] == within + start) & (within < count)
        pick_d_ref[part * size:(part + 1) * size, :] = jnp.where(chosen, 1.0, 0.0).astype(BF16)
    upper_ref[...] = jnp.full(upper_ref.shape, side, jnp.int32).astype(F32)


def compute_kernel(
    others, col_count, supernodes, slot, widths_ref, weights_ref, place_ref, straight_ref,
    own_wide_ref, *refs
):
    block_refs, refs = refs[:-7], refs[-7:]
    block_refs = [block_refs[others.index(other)] for other in range(len(others))]
    keep_d_ref, send_d_ref, keep_t_ref, send_t_ref, x_ref, y_ref, t_ref = refs
    packed_width = block_refs[0].shape[0] // 2
    local_rows = straight_ref.shape[1]
    strips = local_rows // slot
    w_real = weights_ref[0, 0]
    w_imag = weights_ref[0, 1]
    col_index = place_ref[1]

    panel = jnp.concatenate([ref[...] for ref in block_refs], axis=1)
    with_real = rows_by_rows(panel, straight_ref[0])
    with_imag = rows_by_rows(panel, straight_ref[1])
    u_real = with_imag[packed_width:] - with_real[:packed_width]
    u_imag = -(with_real[packed_width:] + with_imag[:packed_width])
    weighted = w_real * u_real - w_imag * u_imag
    turned = w_real * u_imag + w_imag * u_real

    half = packed_width // 2
    upper = (col_index & (col_count // 2)) != 0
    keep_d_ref[...] = jnp.where(upper, weighted[half:], weighted[:half])
    send_d_ref[...] = jnp.where(upper, weighted[:half], weighted[half:])

    for ref, value in ((x_ref, weighted), (y_ref, turned)):
        for s in range(strips):
            ref[s, :packed_width] = value[:, s * slot:(s + 1) * slot]
            ref[s, packed_width:] = jnp.zeros((slot, slot), F32)

    offsets = offsets_of(widths_ref, supernodes)
    for k in range(supernodes):
        right = jnp.concatenate(
            [ref[s, pl.ds(offsets[k], slot), :] for ref in (x_ref, y_ref) for s in range(strips)],
            axis=1,
        )
        high = right.astype(BF16)
        low = (right - high.astype(F32)).astype(BF16)
        product = rows_by_rows(
            own_wide_ref[k * slot:(k + 1) * slot, :], jnp.concatenate([high, low], axis=0)
        )
        t_ref[pl.ds(offsets[k], slot), :] = product[:, :slot] + product[:, slot:]
    keep_t_ref[...] = jnp.where(upper, t_ref[half:2 * half], t_ref[:half])
    send_t_ref[...] = jnp.where(upper, t_ref[:half], t_ref[half:2 * half])


def picked(pick_ref, value):
    high = value.astype(BF16)
    low = (value - high.astype(F32)).astype(BF16)
    return jnp.dot(pick_ref[...], high, preferred_element_type=F32) + jnp.dot(
        pick_ref[...], low, preferred_element_type=F32
    )


def expand_kernel(
    pick_d_ref, pick_ref, keep_ref, upper_ref, mine_d_ref, other_d_ref, mine_t_ref,
    mine_term_ref, other_term_ref, density_ref, diagonal_ref,
):
    density_ref[...] = picked(pick_d_ref, jnp.concatenate([mine_d_ref[...], other_d_ref[...]], axis=0))
    product = picked(pick_ref, mine_t_ref[...])
    rows = mine_term_ref.shape[0]
    upper = upper_ref[:1, :] > 0.5
    terms = (
        jnp.where(upper, other_term_ref[...], mine_term_ref[...]),
        jnp.where(upper, mine_term_ref[...], other_term_ref[...]),
    )
    for side in range(2):
        part = slice(side * rows, (side + 1) * rows)
        diagonal_ref[part] = terms[side] - jnp.where(keep_ref[part] > 0.5, product[part], 0.0)


def finish_kernel(pick_ref, keep_ref, other_t_ref, partial_ref, diagonal_ref):
    product = picked(pick_ref, other_t_ref[...])
    diagonal_ref[...] = partial_ref[...] - jnp.where(keep_ref[...] > 0.5, product, 0.0)


def bits_of(count):
    return [1 << k for k in range(count.bit_length() - 1)]


def swap(value, axis, bit):
    return lax.ppermute(value, axis, [(i, i ^ bit) for i in range(lax.axis_size(axis))])


def tree_sum(terms):
    while len(terms) > 1:
        terms = [terms[j] + terms[j + 1] for j in range(0, len(terms), 2)]
    return terms[0]


def sum_direct(value, axis):
    return tree_sum([value] + [swap(value, axis, j) for j in range(1, lax.axis_size(axis))])


def scatter_rest(value, axis):
    index = lax.axis_index(axis)
    for bit in bits_of(lax.axis_size(axis))[:-1][::-1]:
        half = value.shape[0] // 2
        upper = (index & bit) != 0
        keep = jnp.where(upper, value[half:], value[:half])
        value = keep + swap(jnp.where(upper, value[:half], value[half:]), axis, bit)
    return value


def gather_but_last(value, axis):
    index = lax.axis_index(axis)
    for bit in bits_of(lax.axis_size(axis))[:-1]:
        other = swap(value, axis, bit)
        upper = (index & bit) != 0
        value = jnp.concatenate(
            [jnp.where(upper, other, value), jnp.where(upper, value, other)], axis=0
        )
    return value


def per_device(found_inverse, l_panel, block_pattern, sup_widths, diag_inverse, pole_weights):
    slot = diag_inverse.shape[-1]
    total_cols = l_panel.shape[-1]
    supernodes = total_cols // slot
    packed_width = slot + (supernodes - 1) * (slot // 2)
    half = packed_width // 2
    local_rows = found_inverse.shape[2]
    block = l_panel.shape[2]
    row_count = lax.axis_size("row")
    col_count = lax.axis_size("col")
    top = col_count // 2
    place = jnp.stack([lax.axis_index("row"), lax.axis_index("col")]).astype(jnp.int32)

    packed = pl.pallas_call(
        functools.partial(pack_kernel, supernodes, slot),
        in_specs=[SMEM_SPEC, SMEM_SPEC, VMEM_SPEC],
        out_specs=VMEM_SPEC,
        out_shape=jax.ShapeDtypeStruct((2 * packed_width, block), BF16),
        name="pack",
    )(block_pattern, sup_widths, l_panel[0])

    blocks = {0: packed}
    others = sorted(range(row_count), key=lambda other: other > 0 and other % 2 == 0)
    for other in range(1, row_count):
        blocks[other] = swap(packed, "row", other)
    own = [packed] + [swap(packed, "col", other) for other in range(1, col_count)]

    straight, own_wide, term, pick_d, pick_mine, pick_other, keep, upper = pl.pallas_call(
        functools.partial(prepare_kernel, (row_count, col_count)),
        in_specs=[SMEM_SPEC] * 3 + [VMEM_SPEC] * (2 + col_count),
        out_specs=[VMEM_SPEC] * 8,
        out_shape=[
            jax.ShapeDtypeStruct((2, local_rows, row_count * block), BF16),
            jax.ShapeDtypeStruct((total_cols, 2 * local_rows), BF16),
            jax.ShapeDtypeStruct((total_cols // col_count, slot), F32),
            jax.ShapeDtypeStruct((total_cols // col_count, packed_width), BF16),
            jax.ShapeDtypeStruct((total_cols, packed_width // 2), BF16),
            jax.ShapeDtypeStruct((total_cols, packed_width // 2), BF16),
            jax.ShapeDtypeStruct((total_cols, slot), F32),
            jax.ShapeDtypeStruct((8, slot), F32),
        ],
        compiler_params=PARAMS,
        cost_estimate=pl.CostEstimate(
            flops=4 * 256 * local_rows * row_count * block,
            bytes_accessed=8 * local_rows * row_count * block,
            transcendentals=0,
        ),
        name="prepare",
    )(
        sup_widths, pole_weights, place,
        found_inverse.reshape(2 * local_rows * row_count, block), diag_inverse[0], *own,
    )
    later, blocks[1] = lax.optimization_barrier((term, blocks[1]))
    term = tree_sum(
        [term]
        + [swap(later if j == 1 else term, "pole", j) for j in range(1, lax.axis_size("pole"))]
    )

    keep_d, send_d, keep_t, send_t = pl.pallas_call(
        functools.partial(compute_kernel, others, col_count, supernodes, slot),
        in_specs=[SMEM_SPEC] * 3 + [VMEM_SPEC] * (2 + row_count),
        out_specs=[VMEM_SPEC] * 4,
        out_shape=[jax.ShapeDtypeStruct((half, local_rows), F32)] * 2
        + [jax.ShapeDtypeStruct((half, slot), F32)] * 2,
        scratch_shapes=[
            pltpu.VMEM((local_rows // slot, packed_width + slot, slot), F32),
            pltpu.VMEM((local_rows // slot, packed_width + slot, slot), F32),
            pltpu.VMEM((packed_width + slot, slot), F32),
        ],
        compiler_params=PARAMS,
        name="compute",
    )(
        sup_widths, pole_weights, place, straight, own_wide,
        *[blocks[other] for other in others],
    )

    tie = lax.optimization_barrier
    products, send_d, term = tie((keep_t + swap(send_t, "col", top), send_d, term))
    term = gather_but_last(term, "col")
    products = scatter_rest(products, "col")
    for bit in bits_of(row_count)[::-1]:
        products = products + swap(products, "row", 2 * bit - 1)
    density = scatter_rest(keep_d + swap(send_d, "col", top), "col")
    density = sum_direct(density, "pole")
    products = sum_direct(products, "pole")
    density = gather_but_last(density, "col")
    products = gather_but_last(products, "col")

    density, partial = pl.pallas_call(
        expand_kernel,
        in_specs=[VMEM_SPEC] * 9,
        out_specs=[VMEM_SPEC] * 2,
        out_shape=[
            jax.ShapeDtypeStruct((total_cols // col_count, local_rows), F32),
            jax.ShapeDtypeStruct((total_cols, slot), F32),
        ],
        compiler_params=PARAMS,
        cost_estimate=pl.CostEstimate(
            flops=8 * total_cols * packed_width * (local_rows + slot),
            bytes_accessed=16 * total_cols * local_rows,
            transcendentals=0,
        ),
        name="expand",
    )(
        pick_d, pick_mine, keep, upper, density, swap(density, "col", top), products,
        term, swap(term, "col", top),
    )
    diagonal = pl.pallas_call(
        finish_kernel,
        in_specs=[VMEM_SPEC] * 4,
        out_specs=VMEM_SPEC,
        out_shape=jax.ShapeDtypeStruct((total_cols, slot), F32),
        compiler_params=PARAMS,
        name="finish",
    )(pick_other, keep, swap(products, "col", top), partial)
    return (density, diagonal)


def solution(mesh):
    in_specs = (
        P("pole", None, "row", None, "col", None),
        P("pole", None, ("row", "col"), None),
        P(("row", "col"), None),
        P(),
        P("pole", None, None, None),
        P("pole", None),
    )
    out_specs = (P("col", "row"), P())
    return jax.shard_map(
        per_device, mesh=mesh, in_specs=in_specs, out_specs=out_specs, check_vma=False
    )
```

```python
import functools

import jax
import jax.numpy as jnp
from jax import lax
from jax.experimental import pallas as pl
from jax.experimental.pallas import tpu as pltpu
from jax.sharding import PartitionSpec as P

F32 = jnp.float32
BF16 = jnp.bfloat16
VMEM_SPEC = pl.BlockSpec(memory_space=pltpu.VMEM)
SMEM_SPEC = pl.BlockSpec(memory_space=pltpu.SMEM)
PARAMS = pltpu.CompilerParams(vmem_limit_bytes=48 * 1024 * 1024)


def rows_by_rows(left, right):
    return lax.dot_general(left, right, (((1,), (1,)), ((), ())), preferred_element_type=F32)


def offsets_of(widths_ref, supernodes):
    offsets = [0]
    for k in range(supernodes):
        offsets.append(offsets[-1] + widths_ref[k])
    return offsets


def pack_kernel(
    supernodes, slot, pattern_ref, widths_ref, panel_ref, packed_ref, *half_refs
):
    packed_width = packed_ref.shape[0] // 2
    offsets = offsets_of(widths_ref, supernodes)
    lane = lax.broadcasted_iota(jnp.int32, (1, slot), 1)
    place = []
    for k in range(supernodes):
        valid = (lane < widths_ref[k]) & (pattern_ref[0, k] == 1)
        place.append(jnp.where(valid, offsets[k] + lane, -1))
    place = jnp.concatenate(place, axis=1)
    target = lax.broadcasted_iota(jnp.int32, (packed_width, supernodes * slot), 0)
    select = jnp.where(target == place, 1.0, 0.0).astype(BF16)
    for part in range(2):
        packed = rows_by_rows(select, panel_ref[part]).astype(BF16)
        packed_ref[part * packed_width:(part + 1) * packed_width, :] = packed
        half_refs[part][...] = packed


def prepare_kernel(
    counts, widths_ref, weights_ref, place_ref, inverse_ref, diag_ref, *refs
):
    row_count, col_count = counts
    own_refs, refs = refs[:col_count], refs[col_count:]
    straight_ref, own_wide_ref, term_ref, pick_d_ref, mine_ref, other_ref, keep_ref, upper_ref = refs
    packed_width = own_refs[0].shape[0] // 2
    col_index = place_ref[1]
    block = inverse_ref.shape[1]
    local_rows = straight_ref.shape[1]
    row_index = place_ref[0]
    group = max(8, 256 // row_count)
    span = group * row_count
    row_id = lax.broadcasted_iota(jnp.int32, (span, span), 0)
    col_id = lax.broadcasted_iota(jnp.int32, (span, span), 1)
    source = (row_id % group) * row_count + ((row_id // group) ^ row_index)
    order = jnp.where(col_id == source, 1.0, 0.0).astype(BF16)
    for part in range(2):
        for chunk in range(local_rows // group):
            base = (part * local_rows + chunk * group) * row_count
            mixed = inverse_ref[base:base + span, :]
            sorted_rows = jnp.dot(order, mixed, preferred_element_type=F32).astype(BF16)
            for owner in range(row_count):
                straight_ref[
                    part, chunk * group:(chunk + 1) * group, owner * block:(owner + 1) * block
                ] = sorted_rows[owner * group:(owner + 1) * group]
    own = []
    for c in range(col_count):
        block_of = own_refs[0][...]
        for other in range(1, col_count):
            block_of = jnp.where((col_index ^ c) == other, own_refs[other][...], block_of)
        own.append(block_of)
    own = jnp.concatenate(own, axis=1)
    total_cols = own_wide_ref.shape[0]
    slot = diag_ref.shape[2]
    offsets = offsets_of(widths_ref, total_cols // slot)
    row_in_slot = lax.broadcasted_iota(jnp.int32, (slot, packed_width), 0)
    column = lax.broadcasted_iota(jnp.int32, (slot, packed_width), 1)
    for k in range(total_cols // slot):
        chosen = (column == row_in_slot + offsets[k]) & (row_in_slot < widths_ref[k])
        chosen = jnp.where(chosen, 1.0, 0.0).astype(BF16)
        for part, sign in enumerate((1.0, -1.0)):
            rows = own[part * packed_width:(part + 1) * packed_width]
            own_wide_ref[k * slot:(k + 1) * slot, part * local_rows:(part + 1) * local_rows] = (
                sign * jnp.dot(chosen, rows, preferred_element_type=F32)
            ).astype(BF16)
    per_col = term_ref.shape[0]
    first = pl.multiple_of(col_index * per_col, per_col)
    term_ref[...] = weights_ref[0, 0] * diag_ref[0, pl.ds(first, per_col), :].astype(
        F32
    ) - weights_ref[0, 1] * diag_ref[1, pl.ds(first, per_col), :].astype(F32)
    side = jnp.where((col_index & (col_count // 2)) != 0, 1, 0)
    half = packed_width // 2
    position = jnp.where(column < half, column + side * half, column - side * half)
    lane = lax.broadcasted_iota(jnp.int32, (slot, slot), 1)
    for k in range(total_cols // slot):
        rows = slice(k * slot, (k + 1) * slot)
        for ref, at in ((mine_ref, side), (other_ref, 1 - side)):
            inside = row_in_slot[:, :half]
            chosen = (column[:, :half] + at * half == inside + offsets[k]) & (inside < widths_ref[k])
            ref[rows, :] = jnp.where(chosen, 1.0, 0.0).astype(BF16)
        keep_ref[rows, :] = jnp.where(
            (lane < widths_ref[k]) & (row_in_slot[:, :slot] < widths_ref[k]), 1.0, 0.0
        )
    size = min(per_col, slot)
    for part in range(per_col // size):
        begin = col_index * per_col + part * size
        start, count = 0, 0
        for k in range(total_cols // slot):
            start = start + jnp.where(k < begin // slot, widths_ref[k], 0)
            count = count + jnp.where(k == begin // slot, widths_ref[k], 0)
        within = row_in_slot[:size] + begin % slot
        chosen = (position[:size] == within + start) & (within < count)
        pick_d_ref[part * size:(part + 1) * size, :] = jnp.where(chosen, 1.0, 0.0).astype(BF16)
    upper_ref[...] = jnp.full(upper_ref.shape, side, jnp.int32).astype(F32)


def compute_kernel(
    others, col_count, supernodes, slot, widths_ref, weights_ref, place_ref, straight_ref,
    own_wide_ref, *refs
):
    block_refs, refs = refs[:-7], refs[-7:]
    keep_d_ref, send_d_ref, keep_t_ref, send_t_ref, x_ref, y_ref, t_ref = refs
    packed_width = block_refs[0].shape[0] // 2
    local_rows = straight_ref.shape[1]
    strips = local_rows // slot
    w_real = weights_ref[0, 0]
    w_imag = weights_ref[0, 1]
    col_index = place_ref[1]

    pieces = iter(block_refs)
    panels = {other: [next(pieces)[...] for _ in range(2 if other == 1 else 1)] for other in others}
    panel = jnp.concatenate(
        [jnp.concatenate(panels[other], axis=0) for other in range(len(others))], axis=1
    )
    with_real = rows_by_rows(panel, straight_ref[0])
    with_imag = rows_by_rows(panel, straight_ref[1])
    u_real = with_imag[packed_width:] - with_real[:packed_width]
    u_imag = -(with_real[packed_width:] + with_imag[:packed_width])
    weighted = w_real * u_real - w_imag * u_imag
    turned = w_real * u_imag + w_imag * u_real

    half = packed_width // 2
    upper = (col_index & (col_count // 2)) != 0
    keep_d_ref[...] = jnp.where(upper, weighted[half:], weighted[:half])
    send_d_ref[...] = jnp.where(upper, weighted[:half], weighted[half:])

    for ref, value in ((x_ref, weighted), (y_ref, turned)):
        for s in range(strips):
            ref[s, :packed_width] = value[:, s * slot:(s + 1) * slot]
            ref[s, packed_width:] = jnp.zeros((slot, slot), F32)

    offsets = offsets_of(widths_ref, supernodes)
    for k in range(supernodes):
        right = jnp.concatenate(
            [ref[s, pl.ds(offsets[k], slot), :] for ref in (x_ref, y_ref) for s in range(strips)],
            axis=1,
        )
        high = right.astype(BF16)
        low = (right - high.astype(F32)).astype(BF16)
        product = rows_by_rows(
            own_wide_ref[k * slot:(k + 1) * slot, :], jnp.concatenate([high, low], axis=0)
        )
        t_ref[pl.ds(offsets[k], slot), :] = product[:, :slot] + product[:, slot:]
    keep_t_ref[...] = jnp.where(upper, t_ref[half:2 * half], t_ref[:half])
    send_t_ref[...] = jnp.where(upper, t_ref[:half], t_ref[half:2 * half])


def picked(pick_ref, value):
    high = value.astype(BF16)
    low = (value - high.astype(F32)).astype(BF16)
    return jnp.dot(pick_ref[...], high, preferred_element_type=F32) + jnp.dot(
        pick_ref[...], low, preferred_element_type=F32
    )


def expand_kernel(
    pick_d_ref, pick_ref, keep_ref, upper_ref, mine_d_ref, other_d_ref, mine_t_ref,
    mine_term_ref, other_term_ref, density_ref, diagonal_ref,
):
    density_ref[...] = picked(pick_d_ref, jnp.concatenate([mine_d_ref[...], other_d_ref[...]], axis=0))
    product = picked(pick_ref, mine_t_ref[...])
    rows = mine_term_ref.shape[0]
    upper = upper_ref[:1, :] > 0.5
    terms = (
        jnp.where(upper, other_term_ref[...], mine_term_ref[...]),
        jnp.where(upper, mine_term_ref[...], other_term_ref[...]),
    )
    for side in range(2):
        part = slice(side * rows, (side + 1) * rows)
        diagonal_ref[part] = terms[side] - jnp.where(keep_ref[part] > 0.5, product[part], 0.0)


def finish_kernel(pick_ref, keep_ref, other_t_ref, partial_ref, diagonal_ref):
    product = picked(pick_ref, other_t_ref[...])
    diagonal_ref[...] = partial_ref[...] - jnp.where(keep_ref[...] > 0.5, product, 0.0)


def bits_of(count):
    return [1 << k for k in range(count.bit_length() - 1)]


def swap(value, axis, bit):
    return lax.ppermute(value, axis, [(i, i ^ bit) for i in range(lax.axis_size(axis))])


def tree_sum(terms):
    while len(terms) > 1:
        terms = [terms[j] + terms[j + 1] for j in range(0, len(terms), 2)]
    return terms[0]


def sum_direct(value, axis):
    return tree_sum([value] + [swap(value, axis, j) for j in range(1, lax.axis_size(axis))])


def scatter_rest(value, axis):
    index = lax.axis_index(axis)
    for bit in bits_of(lax.axis_size(axis))[:-1][::-1]:
        half = value.shape[0] // 2
        upper = (index & bit) != 0
        keep = jnp.where(upper, value[half:], value[:half])
        value = keep + swap(jnp.where(upper, value[:half], value[half:]), axis, bit)
    return value


def gather_but_last(value, axis):
    index = lax.axis_index(axis)
    for bit in bits_of(lax.axis_size(axis))[:-1]:
        other = swap(value, axis, bit)
        upper = (index & bit) != 0
        value = jnp.concatenate(
            [jnp.where(upper, other, value), jnp.where(upper, value, other)], axis=0
        )
    return value


def per_device(found_inverse, l_panel, block_pattern, sup_widths, diag_inverse, pole_weights):
    slot = diag_inverse.shape[-1]
    total_cols = l_panel.shape[-1]
    supernodes = total_cols // slot
    packed_width = slot + (supernodes - 1) * (slot // 2)
    half = packed_width // 2
    local_rows = found_inverse.shape[2]
    block = l_panel.shape[2]
    row_count = lax.axis_size("row")
    col_count = lax.axis_size("col")
    top = col_count // 2
    place = jnp.stack([lax.axis_index("row"), lax.axis_index("col")]).astype(jnp.int32)

    packed, *halves = pl.pallas_call(
        functools.partial(pack_kernel, supernodes, slot),
        in_specs=[SMEM_SPEC, SMEM_SPEC, VMEM_SPEC],
        out_specs=[VMEM_SPEC] * 3,
        out_shape=[
            jax.ShapeDtypeStruct((2 * packed_width, block), BF16),
            jax.ShapeDtypeStruct((packed_width, block), BF16),
            jax.ShapeDtypeStruct((packed_width, block), BF16),
        ],
        name="pack",
    )(block_pattern, sup_widths, l_panel[0])

    blocks = {0: packed}
    others = sorted(range(row_count), key=lambda other: other > 0 and other % 2 == 0)
    near = [swap(half, "row", 1) for half in halves]
    for other in range(2, row_count):
        blocks[other] = swap(packed, "row", other)
    own = [packed] + [swap(packed, "col", other) for other in range(1, col_count)]

    straight, own_wide, term, pick_d, pick_mine, pick_other, keep, upper = pl.pallas_call(
        functools.partial(prepare_kernel, (row_count, col_count)),
        in_specs=[SMEM_SPEC] * 3 + [VMEM_SPEC] * (2 + col_count),
        out_specs=[VMEM_SPEC] * 8,
        out_shape=[
            jax.ShapeDtypeStruct((2, local_rows, row_count * block), BF16),
            jax.ShapeDtypeStruct((total_cols, 2 * local_rows), BF16),
            jax.ShapeDtypeStruct((total_cols // col_count, slot), F32),
            jax.ShapeDtypeStruct((total_cols // col_count, packed_width), BF16),
            jax.ShapeDtypeStruct((total_cols, packed_width // 2), BF16),
            jax.ShapeDtypeStruct((total_cols, packed_width // 2), BF16),
            jax.ShapeDtypeStruct((total_cols, slot), F32),
            jax.ShapeDtypeStruct((8, slot), F32),
        ],
        compiler_params=PARAMS,
        cost_estimate=pl.CostEstimate(
            flops=4 * 256 * local_rows * row_count * block,
            bytes_accessed=8 * local_rows * row_count * block,
            transcendentals=0,
        ),
        name="prepare",
    )(
        sup_widths, pole_weights, place,
        found_inverse.reshape(2 * local_rows * row_count, block), diag_inverse[0], *own,
    )
    later, *near = lax.optimization_barrier((term, *near))
    term = tree_sum(
        [term]
        + [swap(later if j == 1 else term, "pole", j) for j in range(1, lax.axis_size("pole"))]
    )

    keep_d, send_d, keep_t, send_t = pl.pallas_call(
        functools.partial(compute_kernel, others, col_count, supernodes, slot),
        in_specs=[SMEM_SPEC] * 3 + [VMEM_SPEC] * (3 + row_count),
        out_specs=[VMEM_SPEC] * 4,
        out_shape=[jax.ShapeDtypeStruct((half, local_rows), F32)] * 2
        + [jax.ShapeDtypeStruct((half, slot), F32)] * 2,
        scratch_shapes=[
            pltpu.VMEM((local_rows // slot, packed_width + slot, slot), F32),
            pltpu.VMEM((local_rows // slot, packed_width + slot, slot), F32),
            pltpu.VMEM((packed_width + slot, slot), F32),
        ],
        compiler_params=PARAMS,
        name="compute",
    )(
        sup_widths, pole_weights, place, straight, own_wide,
        *[piece for other in others for piece in (near if other == 1 else [blocks[other]])],
    )

    tie = lax.optimization_barrier
    products, send_d, term = tie((keep_t + swap(send_t, "col", top), send_d, term))
    term = gather_but_last(term, "col")
    products = scatter_rest(products, "col")
    for bit in bits_of(row_count)[::-1]:
        products = products + swap(products, "row", 2 * bit - 1)
    density = scatter_rest(keep_d + swap(send_d, "col", top), "col")
    density = sum_direct(density, "pole")
    products = sum_direct(products, "pole")
    density = gather_but_last(density, "col")
    products = gather_but_last(products, "col")

    density, partial = pl.pallas_call(
        expand_kernel,
        in_specs=[VMEM_SPEC] * 9,
        out_specs=[VMEM_SPEC] * 2,
        out_shape=[
            jax.ShapeDtypeStruct((total_cols // col_count, local_rows), F32),
            jax.ShapeDtypeStruct((total_cols, slot), F32),
        ],
        compiler_params=PARAMS,
        cost_estimate=pl.CostEstimate(
            flops=8 * total_cols * packed_width * (local_rows + slot),
            bytes_accessed=16 * total_cols * local_rows,
            transcendentals=0,
        ),
        name="expand",
    )(
        pick_d, pick_mine, keep, upper, density, swap(density, "col", top), products,
        term, swap(term, "col", top),
    )
    diagonal = pl.pallas_call(
        finish_kernel,
        in_specs=[VMEM_SPEC] * 4,
        out_specs=VMEM_SPEC,
        out_shape=jax.ShapeDtypeStruct((total_cols, slot), F32),
        compiler_params=PARAMS,
        name="finish",
    )(pick_other, keep, swap(products, "col", top), partial)
    return (density, diagonal)


def solution(mesh):
    in_specs = (
        P("pole", None, "row", None, "col", None),
        P("pole", None, ("row", "col"), None),
        P(("row", "col"), None),
        P(),
        P("pole", None, None, None),
        P("pole", None),
    )
    out_specs = (P("col", "row"), P())
    return jax.shard_map(
        per_device, mesh=mesh, in_specs=in_specs, out_specs=out_specs, check_vma=False
    )
```

```python
import functools

import jax
import jax.numpy as jnp
from jax import lax
from jax.experimental import pallas as pl
from jax.experimental.pallas import tpu as pltpu
from jax.sharding import PartitionSpec as P

F32 = jnp.float32
BF16 = jnp.bfloat16
VMEM_SPEC = pl.BlockSpec(memory_space=pltpu.VMEM)
SMEM_SPEC = pl.BlockSpec(memory_space=pltpu.SMEM)
PARAMS = pltpu.CompilerParams(vmem_limit_bytes=48 * 1024 * 1024)


def rows_by_rows(left, right):
    return lax.dot_general(left, right, (((1,), (1,)), ((), ())), preferred_element_type=F32)


def offsets_of(widths_ref, supernodes):
    offsets = [0]
    for k in range(supernodes):
        offsets.append(offsets[-1] + widths_ref[k])
    return offsets


def pack_kernel(supernodes, slot, pattern_ref, widths_ref, panel_ref, packed_ref):
    packed_width = packed_ref.shape[0] // 2
    offsets = offsets_of(widths_ref, supernodes)
    lane = lax.broadcasted_iota(jnp.int32, (1, slot), 1)
    place = []
    for k in range(supernodes):
        valid = (lane < widths_ref[k]) & (pattern_ref[0, k] == 1)
        place.append(jnp.where(valid, offsets[k] + lane, -1))
    place = jnp.concatenate(place, axis=1)
    target = lax.broadcasted_iota(jnp.int32, (packed_width, supernodes * slot), 0)
    select = jnp.where(target == place, 1.0, 0.0).astype(BF16)
    for part in range(2):
        packed_ref[part * packed_width:(part + 1) * packed_width, :] = rows_by_rows(
            select, panel_ref[part]
        ).astype(BF16)


def prepare_kernel(
    counts, widths_ref, weights_ref, place_ref, inverse_ref, diag_ref, *refs
):
    row_count, col_count = counts
    own_refs, refs = refs[:col_count], refs[col_count:]
    straight_ref, own_wide_ref, term_ref, pick_d_ref, mine_ref, other_ref, keep_ref, upper_ref = refs
    packed_width = own_refs[0].shape[0] // 2
    col_index = place_ref[1]
    block = inverse_ref.shape[1]
    local_rows = straight_ref.shape[1]
    row_index = place_ref[0]
    group = max(8, 256 // row_count)
    span = group * row_count
    row_id = lax.broadcasted_iota(jnp.int32, (span, span), 0)
    col_id = lax.broadcasted_iota(jnp.int32, (span, span), 1)
    source = (row_id % group) * row_count + ((row_id // group) ^ row_index)
    order = jnp.where(col_id == source, 1.0, 0.0).astype(BF16)
    for part in range(2):
        for chunk in range(local_rows // group):
            base = (part * local_rows + chunk * group) * row_count
            mixed = inverse_ref[base:base + span, :]
            sorted_rows = jnp.dot(order, mixed, preferred_element_type=F32).astype(BF16)
            for owner in range(row_count):
                straight_ref[
                    part, chunk * group:(chunk + 1) * group, owner * block:(owner + 1) * block
                ] = sorted_rows[owner * group:(owner + 1) * group]
    own = []
    for c in range(col_count):
        block_of = own_refs[0][...]
        for other in range(1, col_count):
            block_of = jnp.where((col_index ^ c) == other, own_refs[other][...], block_of)
        own.append(block_of)
    own = jnp.concatenate(own, axis=1)
    total_cols = own_wide_ref.shape[0]
    slot = diag_ref.shape[2]
    offsets = offsets_of(widths_ref, total_cols // slot)
    row_in_slot = lax.broadcasted_iota(jnp.int32, (slot, packed_width), 0)
    column = lax.broadcasted_iota(jnp.int32, (slot, packed_width), 1)
    for k in range(total_cols // slot):
        chosen = (column == row_in_slot + offsets[k]) & (row_in_slot < widths_ref[k])
        chosen = jnp.where(chosen, 1.0, 0.0).astype(BF16)
        for part, sign in enumerate((1.0, -1.0)):
            rows = own[part * packed_width:(part + 1) * packed_width]
            own_wide_ref[k * slot:(k + 1) * slot, part * local_rows:(part + 1) * local_rows] = (
                sign * jnp.dot(chosen, rows, preferred_element_type=F32)
            ).astype(BF16)
    per_col = term_ref.shape[0]
    first = pl.multiple_of(col_index * per_col, per_col)
    term_ref[...] = weights_ref[0, 0] * diag_ref[0, pl.ds(first, per_col), :].astype(
        F32
    ) - weights_ref[0, 1] * diag_ref[1, pl.ds(first, per_col), :].astype(F32)
    side = jnp.where((col_index & (col_count // 2)) != 0, 1, 0)
    half = packed_width // 2
    position = jnp.where(column < half, column + side * half, column - side * half)
    lane = lax.broadcasted_iota(jnp.int32, (slot, slot), 1)
    for k in range(total_cols // slot):
        rows = slice(k * slot, (k + 1) * slot)
        for ref, at in ((mine_ref, side), (other_ref, 1 - side)):
            inside = row_in_slot[:, :half]
            chosen = (column[:, :half] + at * half == inside + offsets[k]) & (inside < widths_ref[k])
            ref[rows, :] = jnp.where(chosen, 1.0, 0.0).astype(BF16)
        keep_ref[rows, :] = jnp.where(
            (lane < widths_ref[k]) & (row_in_slot[:, :slot] < widths_ref[k]), 1.0, 0.0
        )
    size = min(per_col, slot)
    for part in range(per_col // size):
        begin = col_index * per_col + part * size
        start, count = 0, 0
        for k in range(total_cols // slot):
            start = start + jnp.where(k < begin // slot, widths_ref[k], 0)
            count = count + jnp.where(k == begin // slot, widths_ref[k], 0)
        within = row_in_slot[:size] + begin % slot
        chosen = (position[:size] == within + start) & (within < count)
        pick_d_ref[part * size:(part + 1) * size, :] = jnp.where(chosen, 1.0, 0.0).astype(BF16)
    upper_ref[...] = jnp.full(upper_ref.shape, side, jnp.int32).astype(F32)


def compute_kernel(
    others, col_count, supernodes, slot, widths_ref, weights_ref, place_ref, straight_ref,
    own_wide_ref, *refs
):
    block_refs, refs = refs[:-7], refs[-7:]
    block_refs = [block_refs[others.index(other)] for other in range(len(others))]
    keep_d_ref, send_d_ref, keep_t_ref, send_t_ref, x_ref, y_ref, t_ref = refs
    packed_width = block_refs[0].shape[0] // 2
    local_rows = straight_ref.shape[1]
    strips = local_rows // slot
    w_real = weights_ref[0, 0]
    w_imag = weights_ref[0, 1]
    col_index = place_ref[1]

    panel = jnp.concatenate([ref[...] for ref in block_refs], axis=1)
    with_real = rows_by_rows(panel, straight_ref[0])
    with_imag = rows_by_rows(panel, straight_ref[1])
    u_real = with_imag[packed_width:] - with_real[:packed_width]
    u_imag = -(with_real[packed_width:] + with_imag[:packed_width])
    weighted = w_real * u_real - w_imag * u_imag
    turned = w_real * u_imag + w_imag * u_real

    half = packed_width // 2
    upper = (col_index & (col_count // 2)) != 0
    keep_d_ref[...] = jnp.where(upper, weighted[half:], weighted[:half])
    send_d_ref[...] = jnp.where(upper, weighted[:half], weighted[half:])

    for ref, value in ((x_ref, weighted), (y_ref, turned)):
        for s in range(strips):
            ref[s, :packed_width] = value[:, s * slot:(s + 1) * slot]
            ref[s, packed_width:] = jnp.zeros((slot, slot), F32)

    offsets = offsets_of(widths_ref, supernodes)
    for k in range(supernodes):
        right = jnp.concatenate(
            [ref[s, pl.ds(offsets[k], slot), :] for ref in (x_ref, y_ref) for s in range(strips)],
            axis=1,
        )
        high = right.astype(BF16)
        low = (right - high.astype(F32)).astype(BF16)
        product = rows_by_rows(
            own_wide_ref[k * slot:(k + 1) * slot, :], jnp.concatenate([high, low], axis=0)
        )
        t_ref[pl.ds(offsets[k], slot), :] = product[:, :slot] + product[:, slot:]
    keep_t_ref[...] = jnp.where(upper, t_ref[half:2 * half], t_ref[:half])
    send_t_ref[...] = jnp.where(upper, t_ref[:half], t_ref[half:2 * half])


def picked(pick_ref, value):
    high = value.astype(BF16)
    low = (value - high.astype(F32)).astype(BF16)
    return jnp.dot(pick_ref[...], high, preferred_element_type=F32) + jnp.dot(
        pick_ref[...], low, preferred_element_type=F32
    )


def expand_kernel(
    pick_d_ref, pick_ref, keep_ref, upper_ref, mine_d_ref, other_d_ref, mine_t_ref,
    mine_term_ref, other_term_ref, density_ref, diagonal_ref,
):
    density_ref[...] = picked(pick_d_ref, jnp.concatenate([mine_d_ref[...], other_d_ref[...]], axis=0))
    product = picked(pick_ref, mine_t_ref[...])
    rows = mine_term_ref.shape[0]
    upper = upper_ref[:1, :] > 0.5
    terms = (
        jnp.where(upper, other_term_ref[...], mine_term_ref[...]),
        jnp.where(upper, mine_term_ref[...], other_term_ref[...]),
    )
    for side in range(2):
        part = slice(side * rows, (side + 1) * rows)
        diagonal_ref[part] = terms[side] - jnp.where(keep_ref[part] > 0.5, product[part], 0.0)


def finish_kernel(pick_ref, keep_ref, other_t_ref, partial_ref, diagonal_ref):
    product = picked(pick_ref, other_t_ref[...])
    diagonal_ref[...] = partial_ref[...] - jnp.where(keep_ref[...] > 0.5, product, 0.0)


def bits_of(count):
    return [1 << k for k in range(count.bit_length() - 1)]


def swap(value, axis, bit):
    return lax.ppermute(value, axis, [(i, i ^ bit) for i in range(lax.axis_size(axis))])


def tree_sum(terms):
    while len(terms) > 1:
        terms = [terms[j] + terms[j + 1] for j in range(0, len(terms), 2)]
    return terms[0]


def sum_direct(value, axis):
    return tree_sum([value] + [swap(value, axis, j) for j in range(1, lax.axis_size(axis))])


def scatter_rest(value, axis):
    index = lax.axis_index(axis)
    for bit in bits_of(lax.axis_size(axis))[:-1][::-1]:
        half = value.shape[0] // 2
        upper = (index & bit) != 0
        keep = jnp.where(upper, value[half:], value[:half])
        value = keep + swap(jnp.where(upper, value[:half], value[half:]), axis, bit)
    return value


def gather_but_last(value, axis):
    index = lax.axis_index(axis)
    for bit in bits_of(lax.axis_size(axis))[:-1]:
        other = swap(value, axis, bit)
        upper = (index & bit) != 0
        value = jnp.concatenate(
            [jnp.where(upper, other, value), jnp.where(upper, value, other)], axis=0
        )
    return value


def per_device(found_inverse, l_panel, block_pattern, sup_widths, diag_inverse, pole_weights):
    slot = diag_inverse.shape[-1]
    total_cols = l_panel.shape[-1]
    supernodes = total_cols // slot
    packed_width = slot + (supernodes - 1) * (slot // 2)
    half = packed_width // 2
    local_rows = found_inverse.shape[2]
    block = l_panel.shape[2]
    row_count = lax.axis_size("row")
    col_count = lax.axis_size("col")
    top = col_count // 2
    place = jnp.stack([lax.axis_index("row"), lax.axis_index("col")]).astype(jnp.int32)

    packed = pl.pallas_call(
        functools.partial(pack_kernel, supernodes, slot),
        in_specs=[SMEM_SPEC, SMEM_SPEC, VMEM_SPEC],
        out_specs=VMEM_SPEC,
        out_shape=jax.ShapeDtypeStruct((2 * packed_width, block), BF16),
        name="pack",
    )(block_pattern, sup_widths, l_panel[0])

    blocks = {0: packed}
    others = list(range(row_count))
    for other in range(1, row_count):
        blocks[other] = swap(packed, "row", other)
    own = [packed] + [swap(packed, "col", other) for other in range(1, col_count)]

    straight, own_wide, term, pick_d, pick_mine, pick_other, keep, upper = pl.pallas_call(
        functools.partial(prepare_kernel, (row_count, col_count)),
        in_specs=[SMEM_SPEC] * 3 + [VMEM_SPEC] * (2 + col_count),
        out_specs=[VMEM_SPEC] * 8,
        out_shape=[
            jax.ShapeDtypeStruct((2, local_rows, row_count * block), BF16),
            jax.ShapeDtypeStruct((total_cols, 2 * local_rows), BF16),
            jax.ShapeDtypeStruct((total_cols // col_count, slot), F32),
            jax.ShapeDtypeStruct((total_cols // col_count, packed_width), BF16),
            jax.ShapeDtypeStruct((total_cols, packed_width // 2), BF16),
            jax.ShapeDtypeStruct((total_cols, packed_width // 2), BF16),
            jax.ShapeDtypeStruct((total_cols, slot), F32),
            jax.ShapeDtypeStruct((8, slot), F32),
        ],
        compiler_params=PARAMS,
        cost_estimate=pl.CostEstimate(
            flops=4 * 256 * local_rows * row_count * block,
            bytes_accessed=8 * local_rows * row_count * block,
            transcendentals=0,
        ),
        name="prepare",
    )(
        sup_widths, pole_weights, place,
        found_inverse.reshape(2 * local_rows * row_count, block), diag_inverse[0], *own,
    )
    later, blocks[1] = lax.optimization_barrier((term, blocks[1]))
    term = tree_sum(
        [term]
        + [swap(later if j == 1 else term, "pole", j) for j in range(1, lax.axis_size("pole"))]
    )

    keep_d, send_d, keep_t, send_t = pl.pallas_call(
        functools.partial(compute_kernel, others, col_count, supernodes, slot),
        in_specs=[SMEM_SPEC] * 3 + [VMEM_SPEC] * (2 + row_count),
        out_specs=[VMEM_SPEC] * 4,
        out_shape=[jax.ShapeDtypeStruct((half, local_rows), F32)] * 2
        + [jax.ShapeDtypeStruct((half, slot), F32)] * 2,
        scratch_shapes=[
            pltpu.VMEM((local_rows // slot, packed_width + slot, slot), F32),
            pltpu.VMEM((local_rows // slot, packed_width + slot, slot), F32),
            pltpu.VMEM((packed_width + slot, slot), F32),
        ],
        compiler_params=PARAMS,
        name="compute",
    )(
        sup_widths, pole_weights, place, straight, own_wide,
        *[blocks[other] for other in others],
    )

    tie = lax.optimization_barrier
    products, send_d, term = tie((keep_t + swap(send_t, "col", top), send_d, term))
    term = gather_but_last(term, "col")
    products = scatter_rest(products, "col")
    for bit in bits_of(row_count)[::-1]:
        products = products + swap(products, "row", 2 * bit - 1)
    density = scatter_rest(keep_d + swap(send_d, "col", top), "col")
    density = sum_direct(density, "pole")
    products = sum_direct(products, "pole")
    density = gather_but_last(density, "col")
    products = gather_but_last(products, "col")

    density, partial = pl.pallas_call(
        expand_kernel,
        in_specs=[VMEM_SPEC] * 9,
        out_specs=[VMEM_SPEC] * 2,
        out_shape=[
            jax.ShapeDtypeStruct((total_cols // col_count, local_rows), F32),
            jax.ShapeDtypeStruct((total_cols, slot), F32),
        ],
        compiler_params=PARAMS,
        cost_estimate=pl.CostEstimate(
            flops=8 * total_cols * packed_width * (local_rows + slot),
            bytes_accessed=16 * total_cols * local_rows,
            transcendentals=0,
        ),
        name="expand",
    )(
        pick_d, pick_mine, keep, upper, density, swap(density, "col", top), products,
        term, swap(term, "col", top),
    )
    diagonal = pl.pallas_call(
        finish_kernel,
        in_specs=[VMEM_SPEC] * 4,
        out_specs=VMEM_SPEC,
        out_shape=jax.ShapeDtypeStruct((total_cols, slot), F32),
        compiler_params=PARAMS,
        name="finish",
    )(pick_other, keep, swap(products, "col", top), partial)
    return (density, diagonal)


def solution(mesh):
    in_specs = (
        P("pole", None, "row", None, "col", None),
        P("pole", None, ("row", "col"), None),
        P(("row", "col"), None),
        P(),
        P("pole", None, None, None),
        P("pole", None),
    )
    out_specs = (P("col", "row"), P())
    return jax.shard_map(
        per_device, mesh=mesh, in_specs=in_specs, out_specs=out_specs, check_vma=False
    )
```

```python
import functools

import jax
import jax.numpy as jnp
from jax import lax
from jax.experimental import pallas as pl
from jax.experimental.pallas import tpu as pltpu
from jax.sharding import PartitionSpec as P

F32 = jnp.float32
BF16 = jnp.bfloat16
VMEM_SPEC = pl.BlockSpec(memory_space=pltpu.VMEM)
SMEM_SPEC = pl.BlockSpec(memory_space=pltpu.SMEM)
PARAMS = pltpu.CompilerParams(vmem_limit_bytes=48 * 1024 * 1024)


def rows_by_rows(left, right):
    return lax.dot_general(left, right, (((1,), (1,)), ((), ())), preferred_element_type=F32)


def offsets_of(widths_ref, supernodes):
    offsets = [0]
    for k in range(supernodes):
        offsets.append(offsets[-1] + widths_ref[k])
    return offsets


def pack_kernel(supernodes, slot, pattern_ref, widths_ref, panel_ref, packed_ref):
    packed_width = packed_ref.shape[0] // 2
    offsets = offsets_of(widths_ref, supernodes)
    lane = lax.broadcasted_iota(jnp.int32, (1, slot), 1)
    place = []
    for k in range(supernodes):
        valid = (lane < widths_ref[k]) & (pattern_ref[0, k] == 1)
        place.append(jnp.where(valid, offsets[k] + lane, -1))
    place = jnp.concatenate(place, axis=1)
    target = lax.broadcasted_iota(jnp.int32, (packed_width, supernodes * slot), 0)
    select = jnp.where(target == place, 1.0, 0.0).astype(BF16)
    for part in range(2):
        packed_ref[part * packed_width:(part + 1) * packed_width, :] = rows_by_rows(
            select, panel_ref[part]
        ).astype(BF16)


def prepare_kernel(
    counts, widths_ref, weights_ref, place_ref, inverse_ref, diag_ref, *refs
):
    row_count, col_count = counts
    own_refs, refs = refs[:col_count], refs[col_count:]
    straight_ref, own_wide_ref, term_ref, pick_d_ref, mine_ref, other_ref, keep_ref, upper_ref = refs
    packed_width = own_refs[0].shape[0] // 2
    col_index = place_ref[1]
    block = inverse_ref.shape[1]
    local_rows = straight_ref.shape[1]
    row_index = place_ref[0]
    group = max(8, 256 // row_count)
    span = group * row_count
    row_id = lax.broadcasted_iota(jnp.int32, (span, span), 0)
    col_id = lax.broadcasted_iota(jnp.int32, (span, span), 1)
    source = (row_id % group) * row_count + ((row_id // group) ^ row_index)
    order = jnp.where(col_id == source, 1.0, 0.0).astype(BF16)
    for part in range(2):
        for chunk in range(local_rows // group):
            base = (part * local_rows + chunk * group) * row_count
            mixed = inverse_ref[base:base + span, :]
            sorted_rows = jnp.dot(order, mixed, preferred_element_type=F32).astype(BF16)
            for owner in range(row_count):
                straight_ref[
                    part, chunk * group:(chunk + 1) * group, owner * block:(owner + 1) * block
                ] = sorted_rows[owner * group:(owner + 1) * group]
    own = []
    for c in range(col_count):
        block_of = own_refs[0][...]
        for other in range(1, col_count):
            block_of = jnp.where((col_index ^ c) == other, own_refs[other][...], block_of)
        own.append(block_of)
    own = jnp.concatenate(own, axis=1)
    total_cols = own_wide_ref.shape[0]
    slot = diag_ref.shape[2]
    offsets = offsets_of(widths_ref, total_cols // slot)
    row_in_slot = lax.broadcasted_iota(jnp.int32, (slot, packed_width), 0)
    column = lax.broadcasted_iota(jnp.int32, (slot, packed_width), 1)
    for k in range(total_cols // slot):
        chosen = (column == row_in_slot + offsets[k]) & (row_in_slot < widths_ref[k])
        chosen = jnp.where(chosen, 1.0, 0.0).astype(BF16)
        for part, sign in enumerate((1.0, -1.0)):
            rows = own[part * packed_width:(part + 1) * packed_width]
            own_wide_ref[k * slot:(k + 1) * slot, part * local_rows:(part + 1) * local_rows] = (
                sign * jnp.dot(chosen, rows, preferred_element_type=F32)
            ).astype(BF16)
    per_col = term_ref.shape[0]
    first = pl.multiple_of(col_index * per_col, per_col)
    term_ref[...] = weights_ref[0, 0] * diag_ref[0, pl.ds(first, per_col), :].astype(
        F32
    ) - weights_ref[0, 1] * diag_ref[1, pl.ds(first, per_col), :].astype(F32)
    side = jnp.where((col_index & (col_count // 2)) != 0, 1, 0)
    half = packed_width // 2
    position = jnp.where(column < half, column + side * half, column - side * half)
    lane = lax.broadcasted_iota(jnp.int32, (slot, slot), 1)
    for k in range(total_cols // slot):
        rows = slice(k * slot, (k + 1) * slot)
        for ref, at in ((mine_ref, side), (other_ref, 1 - side)):
            inside = row_in_slot[:, :half]
            chosen = (column[:, :half] + at * half == inside + offsets[k]) & (inside < widths_ref[k])
            ref[rows, :] = jnp.where(chosen, 1.0, 0.0).astype(BF16)
        keep_ref[rows, :] = jnp.where(
            (lane < widths_ref[k]) & (row_in_slot[:, :slot] < widths_ref[k]), 1.0, 0.0
        )
    size = min(per_col, slot)
    for part in range(per_col // size):
        begin = col_index * per_col + part * size
        start, count = 0, 0
        for k in range(total_cols // slot):
            start = start + jnp.where(k < begin // slot, widths_ref[k], 0)
            count = count + jnp.where(k == begin // slot, widths_ref[k], 0)
        within = row_in_slot[:size] + begin % slot
        chosen = (position[:size] == within + start) & (within < count)
        pick_d_ref[part * size:(part + 1) * size, :] = jnp.where(chosen, 1.0, 0.0).astype(BF16)
    upper_ref[...] = jnp.full(upper_ref.shape, side, jnp.int32).astype(F32)


def compute_kernel(
    others, col_count, supernodes, slot, widths_ref, weights_ref, place_ref, straight_ref,
    own_wide_ref, *refs
):
    block_refs, refs = refs[:-7], refs[-7:]
    block_refs = [block_refs[others.index(other)] for other in range(len(others))]
    keep_d_ref, send_d_ref, keep_t_ref, send_t_ref, x_ref, y_ref, t_ref = refs
    packed_width = block_refs[0].shape[0] // 2
    local_rows = straight_ref.shape[1]
    strips = local_rows // slot
    w_real = weights_ref[0, 0]
    w_imag = weights_ref[0, 1]
    col_index = place_ref[1]

    panel = jnp.concatenate([ref[...] for ref in block_refs], axis=1)
    with_real = rows_by_rows(panel, straight_ref[0])
    with_imag = rows_by_rows(panel, straight_ref[1])
    u_real = with_imag[packed_width:] - with_real[:packed_width]
    u_imag = -(with_real[packed_width:] + with_imag[:packed_width])
    weighted = w_real * u_real - w_imag * u_imag
    turned = w_real * u_imag + w_imag * u_real

    half = packed_width // 2
    upper = (col_index & (col_count // 2)) != 0
    keep_d_ref[...] = jnp.where(upper, weighted[half:], weighted[:half])
    send_d_ref[...] = jnp.where(upper, weighted[:half], weighted[half:])

    for ref, value in ((x_ref, weighted), (y_ref, turned)):
        for s in range(strips):
            ref[s, :packed_width] = value[:, s * slot:(s + 1) * slot]
            ref[s, packed_width:] = jnp.zeros((slot, slot), F32)

    offsets = offsets_of(widths_ref, supernodes)
    for k in range(supernodes):
        right = jnp.concatenate(
            [ref[s, pl.ds(offsets[k], slot), :] for ref in (x_ref, y_ref) for s in range(strips)],
            axis=1,
        )
        high = right.astype(BF16)
        low = (right - high.astype(F32)).astype(BF16)
        product = rows_by_rows(
            own_wide_ref[k * slot:(k + 1) * slot, :], jnp.concatenate([high, low], axis=0)
        )
        t_ref[pl.ds(offsets[k], slot), :] = product[:, :slot] + product[:, slot:]
    keep_t_ref[...] = jnp.where(upper, t_ref[half:2 * half], t_ref[:half])
    send_t_ref[...] = jnp.where(upper, t_ref[:half], t_ref[half:2 * half])


def picked(pick_ref, value):
    high = value.astype(BF16)
    low = (value - high.astype(F32)).astype(BF16)
    return jnp.dot(pick_ref[...], high, preferred_element_type=F32) + jnp.dot(
        pick_ref[...], low, preferred_element_type=F32
    )


def expand_kernel(
    pick_d_ref, pick_ref, keep_ref, upper_ref, mine_d_ref, other_d_ref, mine_t_ref,
    mine_term_ref, other_term_ref, density_ref, diagonal_ref,
):
    density_ref[...] = picked(pick_d_ref, jnp.concatenate([mine_d_ref[...], other_d_ref[...]], axis=0))
    product = picked(pick_ref, mine_t_ref[...])
    rows = mine_term_ref.shape[0]
    upper = upper_ref[:1, :] > 0.5
    terms = (
        jnp.where(upper, other_term_ref[...], mine_term_ref[...]),
        jnp.where(upper, mine_term_ref[...], other_term_ref[...]),
    )
    for side in range(2):
        part = slice(side * rows, (side + 1) * rows)
        diagonal_ref[part] = terms[side] - jnp.where(keep_ref[part] > 0.5, product[part], 0.0)


def finish_kernel(pick_ref, keep_ref, other_t_ref, partial_ref, diagonal_ref):
    product = picked(pick_ref, other_t_ref[...])
    diagonal_ref[...] = partial_ref[...] - jnp.where(keep_ref[...] > 0.5, product, 0.0)


def bits_of(count):
    return [1 << k for k in range(count.bit_length() - 1)]


def swap(value, axis, bit):
    return lax.ppermute(value, axis, [(i, i ^ bit) for i in range(lax.axis_size(axis))])


def tree_sum(terms):
    while len(terms) > 1:
        terms = [terms[j] + terms[j + 1] for j in range(0, len(terms), 2)]
    return terms[0]


def sum_direct(value, axis):
    return tree_sum([value] + [swap(value, axis, j) for j in range(1, lax.axis_size(axis))])


def scatter_rest(value, axis):
    index = lax.axis_index(axis)
    for bit in bits_of(lax.axis_size(axis))[:-1][::-1]:
        half = value.shape[0] // 2
        upper = (index & bit) != 0
        keep = jnp.where(upper, value[half:], value[:half])
        value = keep + swap(jnp.where(upper, value[:half], value[half:]), axis, bit)
    return value


def gather_but_last(value, axis):
    index = lax.axis_index(axis)
    for bit in bits_of(lax.axis_size(axis))[:-1]:
        other = swap(value, axis, bit)
        upper = (index & bit) != 0
        value = jnp.concatenate(
            [jnp.where(upper, other, value), jnp.where(upper, value, other)], axis=0
        )
    return value


def per_device(found_inverse, l_panel, block_pattern, sup_widths, diag_inverse, pole_weights):
    slot = diag_inverse.shape[-1]
    total_cols = l_panel.shape[-1]
    supernodes = total_cols // slot
    packed_width = slot + (supernodes - 1) * (slot // 2)
    half = packed_width // 2
    local_rows = found_inverse.shape[2]
    block = l_panel.shape[2]
    row_count = lax.axis_size("row")
    col_count = lax.axis_size("col")
    top = col_count // 2
    place = jnp.stack([lax.axis_index("row"), lax.axis_index("col")]).astype(jnp.int32)

    packed = pl.pallas_call(
        functools.partial(pack_kernel, supernodes, slot),
        in_specs=[SMEM_SPEC, SMEM_SPEC, VMEM_SPEC],
        out_specs=VMEM_SPEC,
        out_shape=jax.ShapeDtypeStruct((2 * packed_width, block), BF16),
        name="pack",
    )(block_pattern, sup_widths, l_panel[0])

    blocks = {0: packed}
    others = sorted(range(row_count), key=lambda other: other > 0 and other % 2 == 0)
    for other in range(1, row_count):
        blocks[other] = swap(packed, "row", other)
    own = [packed] + [swap(packed, "col", other) for other in range(1, col_count)]

    straight, own_wide, term, pick_d, pick_mine, pick_other, keep, upper = pl.pallas_call(
        functools.partial(prepare_kernel, (row_count, col_count)),
        in_specs=[SMEM_SPEC] * 3 + [VMEM_SPEC] * (2 + col_count),
        out_specs=[VMEM_SPEC] * 8,
        out_shape=[
            jax.ShapeDtypeStruct((2, local_rows, row_count * block), BF16),
            jax.ShapeDtypeStruct((total_cols, 2 * local_rows), BF16),
            jax.ShapeDtypeStruct((total_cols // col_count, slot), F32),
            jax.ShapeDtypeStruct((total_cols // col_count, packed_width), BF16),
            jax.ShapeDtypeStruct((total_cols, packed_width // 2), BF16),
            jax.ShapeDtypeStruct((total_cols, packed_width // 2), BF16),
            jax.ShapeDtypeStruct((total_cols, slot), F32),
            jax.ShapeDtypeStruct((8, slot), F32),
        ],
        compiler_params=PARAMS,
        cost_estimate=pl.CostEstimate(
            flops=4 * 256 * local_rows * row_count * block,
            bytes_accessed=8 * local_rows * row_count * block,
            transcendentals=0,
        ),
        name="prepare",
    )(
        sup_widths, pole_weights, place,
        found_inverse.reshape(2 * local_rows * row_count, block), diag_inverse[0], *own,
    )
    later, blocks[1] = lax.optimization_barrier((term, blocks[1]))
    term = tree_sum(
        [term]
        + [swap(later if j == 1 else term, "pole", j) for j in range(1, lax.axis_size("pole"))]
    )

    keep_d, send_d, keep_t, send_t = pl.pallas_call(
        functools.partial(compute_kernel, others, col_count, supernodes, slot),
        in_specs=[SMEM_SPEC] * 3 + [VMEM_SPEC] * (2 + row_count),
        out_specs=[VMEM_SPEC] * 4,
        out_shape=[jax.ShapeDtypeStruct((half, local_rows), F32)] * 2
        + [jax.ShapeDtypeStruct((half, slot), F32)] * 2,
        scratch_shapes=[
            pltpu.VMEM((local_rows // slot, packed_width + slot, slot), F32),
            pltpu.VMEM((local_rows // slot, packed_width + slot, slot), F32),
            pltpu.VMEM((packed_width + slot, slot), F32),
        ],
        compiler_params=PARAMS,
        name="compute",
    )(
        sup_widths, pole_weights, place, straight, own_wide,
        *[blocks[other] for other in others],
    )

    tie = lax.optimization_barrier
    products, term = tie((keep_t + swap(send_t, "col", top), term))
    term = gather_but_last(term, "col")
    products = scatter_rest(products, "col")
    for bit in bits_of(row_count)[::-1]:
        products = products + swap(products, "row", 2 * bit - 1)
    density = scatter_rest(keep_d + swap(send_d, "col", top), "col")
    density = sum_direct(density, "pole")
    products = sum_direct(products, "pole")
    density = gather_but_last(density, "col")
    products = gather_but_last(products, "col")

    density, partial = pl.pallas_call(
        expand_kernel,
        in_specs=[VMEM_SPEC] * 9,
        out_specs=[VMEM_SPEC] * 2,
        out_shape=[
            jax.ShapeDtypeStruct((total_cols // col_count, local_rows), F32),
            jax.ShapeDtypeStruct((total_cols, slot), F32),
        ],
        compiler_params=PARAMS,
        cost_estimate=pl.CostEstimate(
            flops=8 * total_cols * packed_width * (local_rows + slot),
            bytes_accessed=16 * total_cols * local_rows,
            transcendentals=0,
        ),
        name="expand",
    )(
        pick_d, pick_mine, keep, upper, density, swap(density, "col", top), products,
        term, swap(term, "col", top),
    )
    diagonal = pl.pallas_call(
        finish_kernel,
        in_specs=[VMEM_SPEC] * 4,
        out_specs=VMEM_SPEC,
        out_shape=jax.ShapeDtypeStruct((total_cols, slot), F32),
        compiler_params=PARAMS,
        name="finish",
    )(pick_other, keep, swap(products, "col", top), partial)
    return (density, diagonal)


def solution(mesh):
    in_specs = (
        P("pole", None, "row", None, "col", None),
        P("pole", None, ("row", "col"), None),
        P(("row", "col"), None),
        P(),
        P("pole", None, None, None),
        P("pole", None),
    )
    out_specs = (P("col", "row"), P())
    return jax.shard_map(
        per_device, mesh=mesh, in_specs=in_specs, out_specs=out_specs, check_vma=False
    )
```

```python
import functools

import jax
import jax.numpy as jnp
from jax import lax
from jax.experimental import pallas as pl
from jax.experimental.pallas import tpu as pltpu
from jax.sharding import PartitionSpec as P

F32 = jnp.float32
BF16 = jnp.bfloat16
VMEM_SPEC = pl.BlockSpec(memory_space=pltpu.VMEM)
SMEM_SPEC = pl.BlockSpec(memory_space=pltpu.SMEM)
PARAMS = pltpu.CompilerParams(vmem_limit_bytes=48 * 1024 * 1024)


def rows_by_rows(left, right):
    return lax.dot_general(left, right, (((1,), (1,)), ((), ())), preferred_element_type=F32)


def offsets_of(widths_ref, supernodes):
    offsets = [0]
    for k in range(supernodes):
        offsets.append(offsets[-1] + widths_ref[k])
    return offsets


def pack_kernel(supernodes, slot, pattern_ref, widths_ref, panel_ref, packed_ref):
    packed_width = packed_ref.shape[0] // 2
    offsets = offsets_of(widths_ref, supernodes)
    lane = lax.broadcasted_iota(jnp.int32, (1, slot), 1)
    place = []
    for k in range(supernodes):
        valid = (lane < widths_ref[k]) & (pattern_ref[0, k] == 1)
        place.append(jnp.where(valid, offsets[k] + lane, -1))
    place = jnp.concatenate(place, axis=1)
    target = lax.broadcasted_iota(jnp.int32, (packed_width, supernodes * slot), 0)
    select = jnp.where(target == place, 1.0, 0.0).astype(BF16)
    for part in range(2):
        packed_ref[part * packed_width:(part + 1) * packed_width, :] = rows_by_rows(
            select, panel_ref[part]
        ).astype(BF16)


def prepare_kernel(
    counts, widths_ref, weights_ref, place_ref, inverse_ref, diag_ref, *refs
):
    row_count, col_count = counts
    own_refs, refs = refs[:col_count], refs[col_count:]
    straight_ref, own_wide_ref, term_ref, pick_d_ref, mine_ref, other_ref, keep_ref, upper_ref = refs
    packed_width = own_refs[0].shape[0] // 2
    col_index = place_ref[1]
    block = inverse_ref.shape[1]
    local_rows = straight_ref.shape[1]
    row_index = place_ref[0]
    group = max(8, 256 // row_count)
    span = group * row_count
    row_id = lax.broadcasted_iota(jnp.int32, (span, span), 0)
    col_id = lax.broadcasted_iota(jnp.int32, (span, span), 1)
    source = (row_id % group) * row_count + ((row_id // group) ^ row_index)
    order = jnp.where(col_id == source, 1.0, 0.0).astype(BF16)
    for part in range(2):
        for chunk in range(local_rows // group):
            base = (part * local_rows + chunk * group) * row_count
            mixed = inverse_ref[base:base + span, :]
            sorted_rows = jnp.dot(order, mixed, preferred_element_type=F32).astype(BF16)
            for owner in range(row_count):
                straight_ref[
                    part, chunk * group:(chunk + 1) * group, owner * block:(owner + 1) * block
                ] = sorted_rows[owner * group:(owner + 1) * group]
    own = []
    for c in range(col_count):
        block_of = own_refs[0][...]
        for other in range(1, col_count):
            block_of = jnp.where((col_index ^ c) == other, own_refs[other][...], block_of)
        own.append(block_of)
    own = jnp.concatenate(own, axis=1)
    total_cols = own_wide_ref.shape[0]
    slot = diag_ref.shape[2]
    offsets = offsets_of(widths_ref, total_cols // slot)
    row_in_slot = lax.broadcasted_iota(jnp.int32, (slot, packed_width), 0)
    column = lax.broadcasted_iota(jnp.int32, (slot, packed_width), 1)
    for k in range(total_cols // slot):
        chosen = (column == row_in_slot + offsets[k]) & (row_in_slot < widths_ref[k])
        chosen = jnp.where(chosen, 1.0, 0.0).astype(BF16)
        for part, sign in enumerate((1.0, -1.0)):
            rows = own[part * packed_width:(part + 1) * packed_width]
            own_wide_ref[k * slot:(k + 1) * slot, part * local_rows:(part + 1) * local_rows] = (
                sign * jnp.dot(chosen, rows, preferred_element_type=F32)
            ).astype(BF16)
    per_col = term_ref.shape[0]
    first = pl.multiple_of(col_index * per_col, per_col)
    term_ref[...] = weights_ref[0, 0] * diag_ref[0, pl.ds(first, per_col), :].astype(
        F32
    ) - weights_ref[0, 1] * diag_ref[1, pl.ds(first, per_col), :].astype(F32)
    side = jnp.where((col_index & (col_count // 2)) != 0, 1, 0)
    half = packed_width // 2
    position = jnp.where(column < half, column + side * half, column - side * half)
    lane = lax.broadcasted_iota(jnp.int32, (slot, slot), 1)
    for k in range(total_cols // slot):
        rows = slice(k * slot, (k + 1) * slot)
        for ref, at in ((mine_ref, side), (other_ref, 1 - side)):
            inside = row_in_slot[:, :half]
            chosen = (column[:, :half] + at * half == inside + offsets[k]) & (inside < widths_ref[k])
            ref[rows, :] = jnp.where(chosen, 1.0, 0.0).astype(BF16)
        keep_ref[rows, :] = jnp.where(
            (lane < widths_ref[k]) & (row_in_slot[:, :slot] < widths_ref[k]), 1.0, 0.0
        )
    size = min(per_col, slot)
    for part in range(per_col // size):
        begin = col_index * per_col + part * size
        start, count = 0, 0
        for k in range(total_cols // slot):
            start = start + jnp.where(k < begin // slot, widths_ref[k], 0)
            count = count + jnp.where(k == begin // slot, widths_ref[k], 0)
        within = row_in_slot[:size] + begin % slot
        chosen = (position[:size] == within + start) & (within < count)
        pick_d_ref[part * size:(part + 1) * size, :] = jnp.where(chosen, 1.0, 0.0).astype(BF16)
    upper_ref[...] = jnp.full(upper_ref.shape, side, jnp.int32).astype(F32)


def compute_kernel(
    others, col_count, supernodes, slot, widths_ref, weights_ref, place_ref, straight_ref,
    own_wide_ref, *refs
):
    block_refs, refs = refs[:-7], refs[-7:]
    block_refs = [block_refs[others.index(other)] for other in range(len(others))]
    keep_d_ref, send_d_ref, keep_t_ref, send_t_ref, x_ref, y_ref, t_ref = refs
    packed_width = block_refs[0].shape[0] // 2
    local_rows = straight_ref.shape[1]
    strips = local_rows // slot
    w_real = weights_ref[0, 0]
    w_imag = weights_ref[0, 1]
    col_index = place_ref[1]

    panel = jnp.concatenate([ref[...] for ref in block_refs], axis=1)
    with_real = rows_by_rows(panel, straight_ref[0])
    with_imag = rows_by_rows(panel, straight_ref[1])
    u_real = with_imag[packed_width:] - with_real[:packed_width]
    u_imag = -(with_real[packed_width:] + with_imag[:packed_width])
    weighted = w_real * u_real - w_imag * u_imag
    turned = w_real * u_imag + w_imag * u_real

    half = packed_width // 2
    upper = (col_index & (col_count // 2)) != 0
    keep_d_ref[...] = jnp.where(upper, weighted[half:], weighted[:half])
    send_d_ref[...] = jnp.where(upper, weighted[:half], weighted[half:])

    for ref, value in ((x_ref, weighted), (y_ref, turned)):
        for s in range(strips):
            ref[s, :packed_width] = value[:, s * slot:(s + 1) * slot]
            ref[s, packed_width:] = jnp.zeros((slot, slot), F32)

    offsets = offsets_of(widths_ref, supernodes)
    for k in range(supernodes):
        right = jnp.concatenate(
            [ref[s, pl.ds(offsets[k], slot), :] for ref in (x_ref, y_ref) for s in range(strips)],
            axis=1,
        )
        high = right.astype(BF16)
        low = (right - high.astype(F32)).astype(BF16)
        product = rows_by_rows(
            own_wide_ref[k * slot:(k + 1) * slot, :], jnp.concatenate([high, low], axis=0)
        )
        t_ref[pl.ds(offsets[k], slot), :] = product[:, :slot] + product[:, slot:]
    keep_t_ref[...] = jnp.where(upper, t_ref[half:2 * half], t_ref[:half])
    send_t_ref[...] = jnp.where(upper, t_ref[:half], t_ref[half:2 * half])


def picked(pick_ref, value):
    high = value.astype(BF16)
    low = (value - high.astype(F32)).astype(BF16)
    return jnp.dot(pick_ref[...], high, preferred_element_type=F32) + jnp.dot(
        pick_ref[...], low, preferred_element_type=F32
    )


def expand_kernel(
    pick_d_ref, pick_ref, keep_ref, upper_ref, mine_d_ref, other_d_ref, mine_t_ref,
    mine_term_ref, other_term_ref, density_ref, diagonal_ref,
):
    density_ref[...] = picked(pick_d_ref, jnp.concatenate([mine_d_ref[...], other_d_ref[...]], axis=0))
    product = picked(pick_ref, mine_t_ref[...])
    rows = mine_term_ref.shape[0]
    upper = upper_ref[:1, :] > 0.5
    terms = (
        jnp.where(upper, other_term_ref[...], mine_term_ref[...]),
        jnp.where(upper, mine_term_ref[...], other_term_ref[...]),
    )
    for side in range(2):
        part = slice(side * rows, (side + 1) * rows)
        diagonal_ref[part] = terms[side] - jnp.where(keep_ref[part] > 0.5, product[part], 0.0)


def finish_kernel(pick_ref, keep_ref, other_t_ref, partial_ref, diagonal_ref):
    product = picked(pick_ref, other_t_ref[...])
    diagonal_ref[...] = partial_ref[...] - jnp.where(keep_ref[...] > 0.5, product, 0.0)


def bits_of(count):
    return [1 << k for k in range(count.bit_length() - 1)]


def swap(value, axis, bit):
    return lax.ppermute(value, axis, [(i, i ^ bit) for i in range(lax.axis_size(axis))])


def tree_sum(terms):
    while len(terms) > 1:
        terms = [terms[j] + terms[j + 1] for j in range(0, len(terms), 2)]
    return terms[0]


def sum_direct(value, axis):
    return tree_sum([value] + [swap(value, axis, j) for j in range(1, lax.axis_size(axis))])


def scatter_rest(value, axis):
    index = lax.axis_index(axis)
    for bit in bits_of(lax.axis_size(axis))[:-1][::-1]:
        half = value.shape[0] // 2
        upper = (index & bit) != 0
        keep = jnp.where(upper, value[half:], value[:half])
        value = keep + swap(jnp.where(upper, value[:half], value[half:]), axis, bit)
    return value


def gather_but_last(value, axis):
    index = lax.axis_index(axis)
    for bit in bits_of(lax.axis_size(axis))[:-1]:
        other = swap(value, axis, bit)
        upper = (index & bit) != 0
        value = jnp.concatenate(
            [jnp.where(upper, other, value), jnp.where(upper, value, other)], axis=0
        )
    return value


def per_device(found_inverse, l_panel, block_pattern, sup_widths, diag_inverse, pole_weights):
    slot = diag_inverse.shape[-1]
    total_cols = l_panel.shape[-1]
    supernodes = total_cols // slot
    packed_width = slot + (supernodes - 1) * (slot // 2)
    half = packed_width // 2
    local_rows = found_inverse.shape[2]
    block = l_panel.shape[2]
    row_count = lax.axis_size("row")
    col_count = lax.axis_size("col")
    top = col_count // 2
    place = jnp.stack([lax.axis_index("row"), lax.axis_index("col")]).astype(jnp.int32)

    packed = pl.pallas_call(
        functools.partial(pack_kernel, supernodes, slot),
        in_specs=[SMEM_SPEC, SMEM_SPEC, VMEM_SPEC],
        out_specs=VMEM_SPEC,
        out_shape=jax.ShapeDtypeStruct((2 * packed_width, block), BF16),
        name="pack",
    )(block_pattern, sup_widths, l_panel[0])

    blocks = {0: packed}
    others = sorted(range(row_count), key=lambda other: other > 0 and other % 2 == 0)
    for other in range(1, row_count):
        blocks[other] = swap(packed, "row", other)
    own = [packed] + [swap(packed, "col", other) for other in range(1, col_count)]

    straight, own_wide, term, pick_d, pick_mine, pick_other, keep, upper = pl.pallas_call(
        functools.partial(prepare_kernel, (row_count, col_count)),
        in_specs=[SMEM_SPEC] * 3 + [VMEM_SPEC] * (2 + col_count),
        out_specs=[VMEM_SPEC] * 8,
        out_shape=[
            jax.ShapeDtypeStruct((2, local_rows, row_count * block), BF16),
            jax.ShapeDtypeStruct((total_cols, 2 * local_rows), BF16),
            jax.ShapeDtypeStruct((total_cols // col_count, slot), F32),
            jax.ShapeDtypeStruct((total_cols // col_count, packed_width), BF16),
            jax.ShapeDtypeStruct((total_cols, packed_width // 2), BF16),
            jax.ShapeDtypeStruct((total_cols, packed_width // 2), BF16),
            jax.ShapeDtypeStruct((total_cols, slot), F32),
            jax.ShapeDtypeStruct((8, slot), F32),
        ],
        compiler_params=PARAMS,
        cost_estimate=pl.CostEstimate(
            flops=4 * 256 * local_rows * row_count * block,
            bytes_accessed=8 * local_rows * row_count * block,
            transcendentals=0,
        ),
        name="prepare",
    )(
        sup_widths, pole_weights, place,
        found_inverse.reshape(2 * local_rows * row_count, block), diag_inverse[0], *own,
    )
    term = sum_direct(term, "pole")

    keep_d, send_d, keep_t, send_t = pl.pallas_call(
        functools.partial(compute_kernel, others, col_count, supernodes, slot),
        in_specs=[SMEM_SPEC] * 3 + [VMEM_SPEC] * (2 + row_count),
        out_specs=[VMEM_SPEC] * 4,
        out_shape=[jax.ShapeDtypeStruct((half, local_rows), F32)] * 2
        + [jax.ShapeDtypeStruct((half, slot), F32)] * 2,
        scratch_shapes=[
            pltpu.VMEM((local_rows // slot, packed_width + slot, slot), F32),
            pltpu.VMEM((local_rows // slot, packed_width + slot, slot), F32),
            pltpu.VMEM((packed_width + slot, slot), F32),
        ],
        compiler_params=PARAMS,
        name="compute",
    )(
        sup_widths, pole_weights, place, straight, own_wide,
        *[blocks[other] for other in others],
    )

    tie = lax.optimization_barrier
    products, term = tie((keep_t + swap(send_t, "col", top), term))
    term = gather_but_last(term, "col")
    products = scatter_rest(products, "col")
    for bit in bits_of(row_count)[::-1]:
        products = products + swap(products, "row", 2 * bit - 1)
    density = scatter_rest(keep_d + swap(send_d, "col", top), "col")
    density = sum_direct(density, "pole")
    products = sum_direct(products, "pole")
    density = gather_but_last(density, "col")
    products = gather_but_last(products, "col")

    density, partial = pl.pallas_call(
        expand_kernel,
        in_specs=[VMEM_SPEC] * 9,
        out_specs=[VMEM_SPEC] * 2,
        out_shape=[
            jax.ShapeDtypeStruct((total_cols // col_count, local_rows), F32),
            jax.ShapeDtypeStruct((total_cols, slot), F32),
        ],
        compiler_params=PARAMS,
        cost_estimate=pl.CostEstimate(
            flops=8 * total_cols * packed_width * (local_rows + slot),
            bytes_accessed=16 * total_cols * local_rows,
            transcendentals=0,
        ),
        name="expand",
    )(
        pick_d, pick_mine, keep, upper, density, swap(density, "col", top), products,
        term, swap(term, "col", top),
    )
    diagonal = pl.pallas_call(
        finish_kernel,
        in_specs=[VMEM_SPEC] * 4,
        out_specs=VMEM_SPEC,
        out_shape=jax.ShapeDtypeStruct((total_cols, slot), F32),
        compiler_params=PARAMS,
        name="finish",
    )(pick_other, keep, swap(products, "col", top), partial)
    return (density, diagonal)


def solution(mesh):
    in_specs = (
        P("pole", None, "row", None, "col", None),
        P("pole", None, ("row", "col"), None),
        P(("row", "col"), None),
        P(),
        P("pole", None, None, None),
        P("pole", None),
    )
    out_specs = (P("col", "row"), P())
    return jax.shard_map(
        per_device, mesh=mesh, in_specs=in_specs, out_specs=out_specs, check_vma=False
    )
```
